32 devices in a mesh: group: 4 (over y, x), dev: 8 (over z, core).
Axes of the slice: x: 2, y: 2, z: 4, core: 2. Of those that a mesh axis runs over, the one named last changes fastest.
Arguments:
- species: float32 [6, 64, 32768], P(None, ('group', 'dev')), may hold values from 0.5 to 2
- potential: float32 [64, 32768], P(('group', 'dev')), may hold values from -4 to 4
- pore: int32 [64, 32768], P(('group', 'dev')), may hold values 0 or 1
- openness: float32 [64, 32768], P(('group', 'dev')), may hold values from 0.3 to 1
- neighbours: int32 [64, 6], P(('group', 'dev')), may hold values from 0 to 1, as said below
- diffusivity: float32 [6], replicated, may hold values from 0.02 to 0.12
- rate_const: float32 [64], P(('group', 'dev')), may hold values from 0.1 to 1
- opened: int32 [64], P(('group', 'dev')), may hold values 0 or 1
- partner: int32 [32], P(('group', 'dev')), may hold values from 0 to 31, as said below
- give_slot: int32 [32], P(('group', 'dev')), may hold values from 0 to 1
Outputs:
- new_species: float32 [6, 64, 32768], P(None, ('group', 'dev'))
- new_potential: float32 [64, 32768], P(('group', 'dev'))
The draws below stay inside these ranges and needn't reach their ends.
Inputs may be any that keep to these rules, and one draw needn't show every extreme that they name: `neighbours`: entry k of brick b names a slot of the device given in the reference program for direction k; the lists are consistent: if brick c is the neighbour of b in direction +x, +y or +z, then b is the neighbour of c in the opposite direction. partner[partner[q]] = q for every device q; a partner other than q differs from q in exactly one bit of the device index; over all devices at most two distinct bits occur, at most one of them below 8.
All inputs are finite; a program needn't handle non-finite values. No bound on the sum of `pore` or of `opened` on one device may be relied on, other than what follows from the above.
Results may differ from the reference program's by a relative error of at most 0.00002.
Values sent between devices are 32-bit elements; how exact they have to be, the bound alone decides.
No kernel may reach another device: no remote copies, remote signals or barrier semaphores. Data moves between devices by JAX's collectives and lax.ppermute only.
A program may use at most 128 MiB of HBM per device.

```python
import math
import jax
import jax.numpy as jnp

SIDE = 32
BRICKS = 2
IONS = 6
SWEEPS = 8
CELLS = 32768
STRIDE = 2
TOTAL_BRICKS = 64
N_GROUP = 4
N_DEV = 8


def draw_neighbours(key, part):
    total = N_GROUP * N_DEV
    device = jnp.arange(total, dtype=jnp.int32)
    group_index = device // N_DEV
    dev_index = device % N_DEV
    stride = N_DEV // 4
    behind = [group_index * N_DEV + (dev_index - 1) % N_DEV, group_index * N_DEV + (dev_index - stride) % N_DEV, (group_index - 1) % N_GROUP * N_DEV + dev_index]
    columns = []
    for axis_number in range(3):
        keys = jax.random.split(jax.random.fold_in(key, axis_number + 11), total)
        orders = jax.vmap(lambda single: jax.random.permutation(single, BRICKS))(keys).astype(jnp.int32)
        inverse = jnp.argsort(orders, axis=1, stable=True).astype(jnp.int32)
        columns.append(orders.reshape(-1))
        columns.append(inverse[behind[axis_number]].reshape(-1))
    return jnp.stack(columns, axis=1).astype(jnp.int32)


def draw_partner(key, part):
    total = N_GROUP * N_DEV
    dev_bits = N_DEV.bit_length() - 1
    group_bits = N_GROUP.bit_length() - 1
    first_key, second_key, third_key = jax.random.split(jax.random.fold_in(key, 7), 3)
    inner_bit = jax.random.randint(first_key, (), 0, dev_bits)
    outer_bit = dev_bits + jax.random.randint(second_key, (), 0, group_bits)
    device = jnp.arange(total, dtype=jnp.int32)
    inner_mask = jnp.left_shift(jnp.int32(1), inner_bit.astype(jnp.int32))
    outer_mask = jnp.left_shift(jnp.int32(1), outer_bit.astype(jnp.int32))
    corner = jnp.bitwise_and(device, jnp.bitwise_not(jnp.bitwise_or(inner_mask, outer_mask)))
    modes = jax.random.randint(third_key, (total,), 0, 3)
    mode = modes[corner]
    paired = jnp.where(mode == 1, jnp.bitwise_xor(device, inner_mask), jnp.where(mode == 2, jnp.bitwise_xor(device, outer_mask), device))
    return paired.astype(jnp.int32)


def set_ends(result, own_key, least, high):
    place = [jax.random.randint(jax.random.fold_in(own_key, axis), (), 0, length) for axis, length in enumerate(result.shape)]
    longest = result.shape.index(max(result.shape))
    neighbour = place[:longest] + [(place[longest] + 1) % result.shape[longest]] + place[longest + 1:]
    return result.at[tuple(place)].set(least).at[tuple(neighbour)].set(high)


def block_scale(own_key, extent, cuts, least, largest):
    level = 1.0
    for dim, parts in cuts:
        draws = jax.random.uniform(jax.random.fold_in(jax.random.fold_in(own_key, 6), dim), (parts,), jnp.float32, least / len(cuts), largest / len(cuts))
        level = level * jnp.repeat(jnp.exp(draws), extent[dim] // parts).reshape((-1,) + (1,) * (len(extent) - 1 - dim))
    return level


def normal_values(rng, extent, spread, most, cuts=(), held_as=jnp.bfloat16):
    values = jax.random.normal(rng, extent, jnp.float32) * spread
    if len(cuts) > 0:
        values = block_scale(rng, extent, cuts, -0.22, 0.18) * values
    return jnp.clip(values, min=-most, max=most).astype(held_as)


def setup_inputs(seed: int = 0) -> dict:
    streams_of = jax.random.split(jax.random.key(seed), 11)
    return {
        "species": jnp.clip(0.5 + 1.5 * jax.random.uniform(streams_of[0], (IONS, TOTAL_BRICKS, CELLS), jnp.float32) ** block_scale(streams_of[0], (IONS, TOTAL_BRICKS, CELLS), ((1, 32),), -0.2, 0.2), 0.5, 2.0),
        "potential": normal_values(streams_of[1], (TOTAL_BRICKS, CELLS), 1.0, 4.0, ((0, 32),), jnp.float32),
        "pore": set_ends((jax.random.randint(streams_of[2], (TOTAL_BRICKS, CELLS), 0, 5) < 3).astype(jnp.int32), jax.random.fold_in(streams_of[2], 1), 0, 1),
        "openness": jnp.clip(0.3 + 0.7 * jax.random.uniform(streams_of[3], (TOTAL_BRICKS, CELLS), jnp.float32) ** block_scale(streams_of[3], (TOTAL_BRICKS, CELLS), ((0, 32),), -0.2, 0.2), 0.3, 1.0),
        "neighbours": draw_neighbours(jax.random.fold_in(streams_of[10], 71), 0),
        "diffusivity": jnp.clip(jnp.exp(jax.random.uniform(streams_of[5], (IONS,), jnp.float32, math.log(0.02), math.log(0.12))), 0.02, 0.12),
        "rate_const": jnp.clip(jnp.exp(math.log(1.0) - 2.3025851 * jax.random.uniform(streams_of[6], (TOTAL_BRICKS,), jnp.float32) ** block_scale(streams_of[6], (TOTAL_BRICKS,), ((0, 32),), -0.2, 0.2)), 0.1, 1.0),
        "opened": set_ends((jax.random.randint(streams_of[7], (TOTAL_BRICKS,), 0, 2) < 1).astype(jnp.int32), jax.random.fold_in(streams_of[7], 1), 0, 1),
        "partner": draw_partner(jax.random.fold_in(streams_of[10], 71), 0),
        "give_slot": set_ends(jax.random.randint(streams_of[9], (N_GROUP * N_DEV,), 0, BRICKS), jax.random.fold_in(streams_of[9], 1), 0, BRICKS - 1).astype(jnp.int32),
    }


charge_scale = 0.5
screening = 0.5
solubility = 2.0
valences = (2.0, -1.0, 1.0, -1.0, 1.0, 2.0)
reaction_signs = (1.0, 1.0, -1.0, 0.0, 0.0, 0.0)


def face_list(field):
    brick_side = field.shape[-2]
    cube_view = field.reshape(field.shape[:-1] + (brick_side, brick_side))
    flat_shape = field.shape[:-2] + (brick_side * brick_side,)
    return (field[..., 0, :], field[..., brick_side - 1, :],
            cube_view[..., :, 0, :].reshape(flat_shape), cube_view[..., :, brick_side - 1, :].reshape(flat_shape),
            cube_view[..., 0].reshape(flat_shape), cube_view[..., brick_side - 1].reshape(flat_shape))


def beside_values(field, halo_list):
    brick_side = field.shape[-2]
    plane_shape = field.shape[:-2] + (brick_side, brick_side)
    cube_shape = field.shape[:-2] + (brick_side, brick_side, brick_side)
    east_side = jnp.concatenate([field[..., 1:, :], halo_list[0][..., None, :]], axis=-2)
    west_side = jnp.concatenate([halo_list[1][..., None, :], field[..., :-1, :]], axis=-2)
    north_side = jnp.concatenate([field[..., brick_side:], halo_list[2].reshape(plane_shape)], axis=-1)
    south_side = jnp.concatenate([halo_list[3].reshape(plane_shape), field[..., :-brick_side]], axis=-1)
    depth_index = jnp.arange(brick_side * brick_side, dtype=jnp.int32) % brick_side
    upper_rim = jnp.broadcast_to(halo_list[4].reshape(plane_shape)[..., None], cube_shape).reshape(field.shape)
    lower_rim = jnp.broadcast_to(halo_list[5].reshape(plane_shape)[..., None], cube_shape).reshape(field.shape)
    upper_side = jnp.where(depth_index == brick_side - 1, upper_rim,
                           jnp.concatenate([field[..., 1:], field[..., :1]], axis=-1))
    lower_side = jnp.where(depth_index == 0, lower_rim,
                           jnp.concatenate([field[..., -1:], field[..., :-1]], axis=-1))
    return (east_side, west_side, north_side, south_side, upper_side, lower_side)


def relax(nearby, density):
    total = nearby[0] + nearby[1] + nearby[2] + nearby[3] + nearby[4] + nearby[5] + density
    return total / (6.0 + screening)


def local_update(species, swept, wetted, pore_float, halo_species, halo_swept, halo_wetted, diffusivity, reactivity):
    near_species = beside_values(species, halo_species)
    near_swept = beside_values(swept, halo_swept)
    near_wetted = beside_values(wetted, halo_wetted)
    half_charge = 0.5 * jnp.asarray(valences, jnp.float32)[:, None, None, None]
    outflow = jnp.zeros_like(species)
    for direction in range(6):
        conductance = wetted * near_wetted[direction]
        outflow = outflow + conductance * ((species - near_species[direction])
                                           + half_charge * (species + near_species[direction]) * (swept - near_swept[direction]))
    reaction = reactivity[:, None, None] * pore_float * (species[2] - species[0] * species[1] / solubility)
    signs = jnp.asarray(reaction_signs, jnp.float32)[:, None, None, None]
    return species - diffusivity[:, None, None, None] * outflow + signs * reaction


def global_slots(neighbours):
    slot_index = jnp.arange(TOTAL_BRICKS, dtype=jnp.int32)
    device = slot_index // BRICKS
    group_index = device // N_DEV
    dev_index = device % N_DEV
    owners = [group_index * N_DEV + (dev_index + 1) % N_DEV,
              group_index * N_DEV + (dev_index - 1) % N_DEV,
              group_index * N_DEV + (dev_index + STRIDE) % N_DEV,
              group_index * N_DEV + (dev_index - STRIDE) % N_DEV,
              ((group_index + 1) % N_GROUP) * N_DEV + dev_index,
              ((group_index - 1) % N_GROUP) * N_DEV + dev_index]
    owner_table = jnp.stack(owners, axis=1).astype(jnp.int32)
    return owner_table * BRICKS + neighbours


def gather_halos(field, table):
    faces = face_list(field)
    return tuple(jnp.take(faces[direction], table[:, direction], axis=-2) for direction in range(6))


def reference(species, potential, pore, openness, neighbours, diffusivity, rate_const, opened, partner, give_slot):
    cell_shape = (TOTAL_BRICKS, SIDE, SIDE * SIDE)
    table = global_slots(neighbours)
    species_cube = species.reshape((IONS,) + cell_shape)
    pore_float = pore.astype(jnp.float32).reshape(cell_shape)
    wetted = pore_float * openness.reshape(cell_shape)
    charges = jnp.asarray(valences, jnp.float32)[:, None, None, None]
    density = charge_scale * wetted * jnp.sum(charges * species_cube, axis=0)
    swept = potential.reshape(cell_shape)
    for sweep_index in range(SWEEPS):
        swept = relax(beside_values(swept, gather_halos(swept, table)), density)
    reactivity = rate_const * opened.astype(jnp.float32)
    updated = local_update(species_cube, swept, wetted, pore_float,
                           gather_halos(species_cube, table), gather_halos(swept, table),
                           gather_halos(wetted, table), diffusivity, reactivity)
    device = jnp.arange(N_GROUP * N_DEV, dtype=jnp.int32)
    target = device * BRICKS + give_slot
    source = partner * BRICKS + give_slot[partner]
    anchor = jnp.arange(TOTAL_BRICKS, dtype=jnp.int32).at[target].set(source)
    new_species = updated[:, anchor].reshape(IONS, TOTAL_BRICKS, SIDE * SIDE * SIDE)
    new_potential = swept[anchor].reshape(TOTAL_BRICKS, SIDE * SIDE * SIDE)
    return new_species, new_potential
```

```python
import functools

import jax
import jax.numpy as jnp
from jax import lax
from jax.experimental import pallas as pl
from jax.experimental.pallas import tpu as pltpu
from jax.sharding import PartitionSpec as P


SWEEPS = 8
DEPTH = SWEEPS + 1
LANES = 128

charge_scale = 0.5
screening = 0.5
solubility = 2.0
valences = (2.0, -1.0, 1.0, -1.0, 1.0, 2.0)
reaction_signs = (1.0, 1.0, -1.0, 0.0, 0.0, 0.0)

SIDE = 32
QUADS = 4
YQ = SIDE // QUADS
PAIRS = 3
PLANE = SIDE * YQ
HALF = SIDE // 2

FACE_SP = DEPTH * SIDE
FACE_WET = FACE_SP + PAIRS * SIDE
FACE_TBL = FACE_WET + SIDE
FACE_ROWS = FACE_TBL + 8
EDGE_TBL = 64
EDGE_ROWS = EDGE_TBL + 8
ZC_TBL = QUADS * PLANE // 2
ZC_ROWS = ZC_TBL + 8
ZH_EDGE = 4 * 2 * SIDE
ZH_TBL = ZH_EDGE + 64
ZH_ROWS = ZH_TBL + 32

ZH_PLACE = {0: (0, 0), 3: (0, 8), 4: (0, 13), 7: (0, 17), 1: (1, 0), 2: (1, 7), 5: (1, 13), 6: (1, 16)}

SIDES = ((-1, 0), (1, 0), (0, -1), (0, 1))
CORNERS = ((-1, -1), (-1, 1), (1, -1), (1, 1))
SPAN = 16
EXT = SIDE + 2 * DEPTH
NEAR = SIDE + 2
PAD = 8


def x_way(s):
    return 0 if s > 0 else 1


def y_way(s):
    return 2 if s > 0 else 3


def z_way(s):
    return 4 if s > 0 else 5


def roll(v, shift):
    shift = shift % LANES
    return v if shift == 0 else pltpu.roll(v, shift, 1)


def lane_of(rows):
    return lax.broadcasted_iota(jnp.int32, (rows, LANES), 1)


def swap_groups(v, lane):
    low = lane < 64
    a0 = jnp.where(low, v[0], roll(v[2], 64))
    a2 = jnp.where(low, roll(v[0], 64), v[2])
    a1 = jnp.where(low, v[1], roll(v[3], 64))
    a3 = jnp.where(low, roll(v[1], 64), v[3])
    even = (lane & 32) == 0
    return (
        jnp.where(even, a0, roll(a1, 32)),
        jnp.where(even, roll(a0, 96), a1),
        jnp.where(even, a2, roll(a3, 32)),
        jnp.where(even, roll(a2, 96), a3),
    )


def pack_kernel(pieces, species, potential, pore, openness, neighbours, sp, wd, pd, own, *rest):
    n_out = len(pieces)
    outs, (zlo, zhi) = rest[:n_out], rest[n_out:]
    where = {name: (outs[k], base) for k, held in enumerate(pieces) for name, base in held}
    lane = lane_of(8)
    lane32 = lane & 31
    low = lane < 64

    row_of = lax.broadcasted_iota(jnp.int32, (8, LANES), 0)
    table = jnp.zeros((8, LANES), jnp.float32)
    for way in range(6):
        sign = jnp.where(neighbours[0, way] == 0, 1.0, -1.0)
        table = jnp.where(row_of == way, sign, table)
    own[...] = table

    def planes_of(x):
        rows = [pl.ds(x * 16 + b, 8, stride=2) for b in range(2)]
        s = [[species[i, rows[b], :] for b in range(2)] for i in range(6)]
        w, d, p = [], [], []
        for b in range(2):
            wet = pore[rows[b], :].astype(jnp.float32) * openness[rows[b], :]
            total = valences[0] * s[0][b]
            for i in range(1, 6):
                total = total + valences[i] * s[i][b]
            w.append(wet)
            d.append(charge_scale * wet * total)
            p.append(potential[rows[b], :])
        ions = [swap_groups((s[2 * k][0], s[2 * k + 1][0], s[2 * k][1], s[2 * k + 1][1]), lane) for k in range(PAIRS)]
        wets = swap_groups((w[0], w[0], w[1], w[1]), lane)
        mixed = []
        for v in swap_groups((p[0], d[0], p[1], d[1]), lane):
            r = roll(v, 64)
            mixed.append(jnp.where(low, v + r, r - v))
        at = pl.ds(pl.multiple_of(x * 8, 8), 8)
        for j in range(QUADS):
            pd[j, at, :] = mixed[j]
            wd[j, at, :] = wets[j]
            for k in range(PAIRS):
                sp[k, j, at, :] = ions[k][j]
        return mixed, wets, ions

    def step(x, carry):
        first, second = planes_of(x), planes_of(x + HALF)
        for j in range(QUADS):
            at = pl.ds(pl.multiple_of(j * (PLANE // 2) + x * 8, 8), 8)
            lo = first[0][j]
            lo = jnp.where(lane32 >= 16, roll(second[0][j], 16), lo)
            hi = second[0][j]
            hi = jnp.where(lane32 < 16, roll(first[0][j], -16), hi)
            for k in range(PAIRS):
                lo = jnp.where(lane32 == 9 + k, roll(first[2][k][j], 9 + k), lo)
                lo = jnp.where(lane32 == 25 + k, roll(second[2][k][j], 25 + k), lo)
                hi = jnp.where(lane32 == 22 - k, roll(second[2][k][j], -9 - k), hi)
                hi = jnp.where(lane32 == 6 - k, roll(first[2][k][j], -25 - k), hi)
            lo = jnp.where(lane32 == 12, roll(first[1][j], 12), lo)
            lo = jnp.where(lane32 == 28, roll(second[1][j], 28), lo)
            hi = jnp.where(lane32 == 19, roll(second[1][j], -12), hi)
            hi = jnp.where(lane32 == 3, roll(first[1][j], -28), hi)
            zlo[at, :] = lo
            zhi[at, :] = hi
        return carry

    lax.fori_loop(0, HALF, step, 0)

    zlo[ZC_TBL:, :] = table
    zhi[ZC_TBL:, :] = table
    for sx, sy in SIDES:
        ref, base = where[(sx, sy)]
        for l in range(DEPTH):
            if sx:
                x = l if sx < 0 else SIDE - 1 - l
                for j in range(QUADS):
                    ref[base + l * SIDE + j * 8 : base + l * SIDE + j * 8 + 8, :] = pd[j, x * 8 : x * 8 + 8, :]
            else:
                y = l if sy < 0 else SIDE - 1 - l
                ref[base + l * SIDE : base + (l + 1) * SIDE, :] = pd[y % 4, pl.ds(y // 4, SIDE, stride=8), :]
        for k in range(PAIRS + 1):
            start = base + FACE_SP + k * SIDE
            for j in range(QUADS) if sx else range(1):
                if sx:
                    x = 0 if sx < 0 else SIDE - 1
                    pick, at = (j, slice(x * 8, x * 8 + 8)), slice(start + j * 8, start + j * 8 + 8)
                else:
                    y = 0 if sy < 0 else SIDE - 1
                    pick, at = (y % 4, pl.ds(y // 4, SIDE, stride=8)), slice(start, start + SIDE)
                ref[at, :] = sp[k, pick[0], pick[1], :] if k < PAIRS else wd[pick[0], pick[1], :]
        ref[base + FACE_TBL : base + FACE_ROWS, :] = table
    for sx, sy in CORNERS:
        ref, base = where[(sx, sy)]
        x0 = 0 if sx < 0 else SIDE - 8
        for m in range(8):
            y = m if sy < 0 else SIDE - 8 + m
            ref[base + m * 8 : base + m * 8 + 8, :] = pd[y % 4, pl.ds(x0 * 8 + y // 4, 8, stride=8), :]
        ref[base + EDGE_TBL : base + EDGE_ROWS, :] = table


def relay_kernel(pieces, *refs):
    arrived, (zl, zh) = refs[:-2], refs[-2:]
    where = {name: (arrived[k], base) for k, held in enumerate(pieces) for name, base in held}
    lane32 = lane_of(SIDE) & 31
    for number, (sx, sy) in enumerate(SIDES):
        ref, base = where[(-sx, -sy)]
        lo = [jnp.zeros((SIDE, LANES), jnp.float32)] * 2
        hi = [jnp.zeros((SIDE, LANES), jnp.float32)] * 2
        for l in range(8):
            block, off = ZH_PLACE[l]
            width = 8 - l
            v = ref[base + l * SIDE : base + (l + 1) * SIDE, :]
            lo[block] = jnp.where((lane32 >= off) & (lane32 < off + width), roll(v, off), lo[block])
            hi[block] = jnp.where((lane32 <= 31 - off) & (lane32 > 31 - off - width), roll(v, -off), hi[block])
        for block in range(2):
            at = slice((number * 2 + block) * SIDE, (number * 2 + block + 1) * SIDE)
            zl[at, :] = lo[block]
            zh[at, :] = hi[block]
        at = slice(ZH_TBL + number * 8, ZH_TBL + number * 8 + 8)
        zl[at, :] = ref[base + FACE_TBL : base + FACE_ROWS, :]
        zh[at, :] = ref[base + FACE_TBL : base + FACE_ROWS, :]
    group = lane_of(64) & 31
    lo = jnp.zeros((64, LANES), jnp.float32)
    hi = lo
    for number, (sx, sy) in enumerate(CORNERS):
        ref, base = where[(-sx, -sy)]
        v = ref[base : base + EDGE_TBL, :]
        lo = jnp.where((group >= 8 * number) & (group < 8 * number + 8), roll(v, 8 * number), lo)
        hi = jnp.where((group <= 31 - 8 * number) & (group > 23 - 8 * number), roll(v, -8 * number), hi)
    zl[ZH_EDGE : ZH_EDGE + 64, :] = lo
    zh[ZH_EDGE : ZH_EDGE + 64, :] = hi


def step_kernel(
    pieces,
    sp,
    wd,
    pd,
    own,
    zup,
    zdn,
    zhup,
    zhdn,
    *rest,
):
    n_in = len(pieces)
    arrived = rest[:n_in]
    diffusivity, rate_const, opened, give_slot = rest[n_in : n_in + 4]
    out_sp, out_pot, send = rest[n_in + 4 : n_in + 7]
    ua, ub, dn, fd, se, we, mx, myp, mym = rest[n_in + 7 :]
    where = {name: (arrived[k], base) for k, held in enumerate(pieces) for name, base in held}

    lane = lane_of(8)
    lane32, lane64 = lane & 31, lane & 63
    low = lane < 64
    core = (lane64 >= 16) & (lane64 < 48)
    upper = lane64 >= 48

    table = {(0, 0): own[...]}
    ztable = {1: {(0, 0): zup[ZC_TBL:, :]}, -1: {(0, 0): zdn[ZC_TBL:, :]}}
    for number, (sx, sy) in enumerate(SIDES):
        ref, base = where[(-sx, -sy)]
        table[(sx, sy)] = ref[base + FACE_TBL : base + FACE_ROWS, :]
        for sz, held in ((1, zhup), (-1, zhdn)):
            ztable[sz][(sx, sy)] = held[ZH_TBL + number * 8 : ZH_TBL + number * 8 + 8, :]
    for sx, sy in CORNERS:
        ref, base = where[(-sx, -sy)]
        table[(sx, sy)] = ref[base + EDGE_TBL : base + EDGE_ROWS, :]

    def sign(held, way):
        return jnp.broadcast_to(held[way : way + 1, :], (8, LANES))

    def crossing(way, here, there):
        level = sign(table[here], way)
        beyond = {}
        for sz in (1, -1):
            z = z_way(sz)
            beyond[sz] = sign(ztable[sz][here], way) * sign(table[here], z) * sign(table[there], z)
        m = jnp.where(core, level, jnp.where(upper, beyond[1], beyond[-1]))
        return jnp.where(low, 1.0, m)

    row8 = lax.broadcasted_iota(jnp.int32, (8, LANES), 0)
    one = jnp.ones((8, LANES), jnp.float32)
    for number, sx in enumerate((-1, 1)):
        m = {sy: crossing(x_way(sx), (0, sy), (sx, sy)) for sy in (-1, 0, 1)}
        mx[number, 0:8, :] = jnp.where(row8 < 4, m[-1], m[0])
        mx[number, 8:16, :] = jnp.where(row8 < 4, m[0], m[1])
    y_sign = {}
    for number, sx in enumerate((-1, 0, 1)):
        m = {sy: crossing(y_way(sy), (sx, 0), (sx, sy)) for sy in (-1, 1)}
        y_sign[sx] = m
        myp[number, 0:8, :] = jnp.where(row8 == 3, m[-1], one)
        myp[number, 8:16, :] = jnp.where(row8 == 3, m[1], one)
        mym[number, 0:8, :] = jnp.where(row8 == 4, m[-1], one)
        mym[number, 8:16, :] = jnp.where(row8 == 4, m[1], one)

    outer = {}
    for key, held in table.items():
        m = jnp.where(upper, sign(held, 4), sign(held, 5))
        outer[key] = jnp.where(low, 1.0, m)

    def spread(v, zu, zd, shift_u, shift_d, key):
        rows = v.shape[0]
        tall = lambda a: a if rows == 8 else jnp.concatenate([a] * (rows // 8), axis=0)
        if zu is None:
            return roll(v, 16), roll(v, -16)
        m, c, u = tall(outer[key]), tall(core), tall(upper)
        pot = jnp.where(u, roll(zu, 48 + shift_u), roll(zd, -16 + shift_d)) * m
        rho = jnp.where(u, roll(zu, 16 + shift_u), roll(zd, -48 + shift_d)) * m
        return jnp.where(c, roll(v, 16), pot), jnp.where(c, roll(v, -16), rho)

    for half in range(2):

        def fill(i, carry, half=half):
            x = i + half * HALF
            at = pl.ds(pl.multiple_of(x * 8, 8), 8)
            to = pl.ds(pl.multiple_of(PAD + (x + DEPTH) * SPAN + 4, 4), 8)
            near = pl.ds(pl.multiple_of(PAD + (x + 1) * SPAN + 4, 4), 8)
            for j in range(QUADS):
                zat = pl.ds(pl.multiple_of(j * (PLANE // 2) + i * 8, 8), 8)
                shift_u, shift_d = (0, 16) if half == 0 else (-16, 0)
                pot, rho = spread(pd[j, at, :], zup[zat, :], zdn[zat, :], shift_u, shift_d, (0, 0))
                ua[j, to, :] = pot
                dn[j, to, :] = rho
                we[j, near, :] = wd[j, at, :]
                for k in range(PAIRS):
                    se[k, j, near, :] = sp[k, j, at, :]
            return carry

        lax.fori_loop(0, HALF, fill, 0)

    def turned(v, way):
        s = own[way : way + 1, :]
        return jnp.where(jnp.broadcast_to(s, v.shape) > 0, v, roll(v, 64))

    for number, (sx, sy) in enumerate(SIDES):
        ref, base = where[(-sx, -sy)]
        for l in range(DEPTH):
            v = ref[base + l * SIDE : base + (l + 1) * SIDE, :]
            zu = zd = None
            off = 0
            if l < 8:
                block, off = ZH_PLACE[l]
                at = slice((number * 2 + block) * SIDE, (number * 2 + block + 1) * SIDE)
                zu, zd = zhup[at, :], zhdn[at, :]
            pot, rho = spread(v, zu, zd, -off, off, (sx, sy))
            if sx:
                x = SIDE + l if sx > 0 else -1 - l
                start = PAD + (x + DEPTH) * SPAN + 4
                for j in range(QUADS):
                    ua[j, start : start + 8, :] = pot[j * 8 : j * 8 + 8]
                    dn[j, start : start + 8, :] = rho[j * 8 : j * 8 + 8]
            else:
                j = l % 4 if sy > 0 else 3 - l % 4
                row = 12 + l // 4 if sy > 0 else 3 - l // 4
                at = pl.ds(PAD + DEPTH * SPAN + row, SIDE, stride=SPAN)
                ua[j, at, :] = pot
                dn[j, at, :] = rho
        way = x_way(sx) if sx else y_way(sy)
        for k in range(PAIRS + 1):
            start = base + FACE_SP + k * SIDE
            v = turned(ref[start : start + SIDE, :], way)
            if sx:
                begin = PAD + (SIDE + 1 if sx > 0 else 0) * SPAN + 4
                for j in range(QUADS):
                    if k < PAIRS:
                        se[k, j, begin : begin + 8, :] = v[j * 8 : j * 8 + 8]
                    else:
                        we[j, begin : begin + 8, :] = v[j * 8 : j * 8 + 8]
            else:
                j, row = (0, 12) if sy > 0 else (3, 3)
                at = pl.ds(PAD + SPAN + row, SIDE, stride=SPAN)
                if k < PAIRS:
                    se[k, j, at, :] = v
                else:
                    we[j, at, :] = v
    for number, (sx, sy) in enumerate(CORNERS):
        ref, base = where[(-sx, -sy)]
        for m in range(8):
            v = ref[base + m * 8 : base + m * 8 + 8, :]
            at = slice(ZH_EDGE + m * 8, ZH_EDGE + m * 8 + 8)
            pot, rho = spread(v, zhup[at, :], zhdn[at, :], -8 * number, 8 * number, (sx, sy))
            row = (12 if sy > 0 else 2) + m // 4
            x = SIDE if sx > 0 else -8
            to = pl.ds(PAD + (x + DEPTH) * SPAN + row, 8, stride=SPAN)
            ua[m % 4, to, :] = pot
            dn[m % 4, to, :] = rho

    scale = 1.0 / (6.0 + screening)

    def slab(src, dst, x, sx, before=None, after=None):
        r = pl.multiple_of(PAD + (x + DEPTH) * SPAN, 8)
        at = pl.ds(r, SPAN)
        c = [src[j, at, :] for j in range(QUADS)]
        for j in range(QUADS):
            left = src[j, pl.ds(r - SPAN, SPAN), :]
            right = src[j, pl.ds(r + SPAN, SPAN), :]
            if before is not None:
                left = left * mx[before]
            if after is not None:
                right = right * mx[after]
            north = c[j + 1] if j < 3 else src[0, pl.ds(r + 1, SPAN), :] * myp[sx + 1]
            south = c[j - 1] if j > 0 else src[3, pl.ds(r - 1, SPAN), :] * mym[sx + 1]
            total = (left + right) + (north + south) + (roll(c[j], 1) + roll(c[j], -1)) + dn[j, at, :]
            dst[j, at, :] = total * scale

    def sweep(src, dst, t):
        def run(begin, end, sx):
            lax.fori_loop(begin, end, lambda x, carry: (slab(src, dst, x, sx), carry)[1], 0)

        run(t - DEPTH, -1, -1)
        slab(src, dst, -1, -1, after=0)
        slab(src, dst, 0, 0, before=0)
        run(1, SIDE - 1, 0)
        slab(src, dst, SIDE - 1, 0, after=1)
        slab(src, dst, SIDE, 1, before=1)
        run(SIDE + 1, SIDE + DEPTH - t, 1)

    def two_sweeps(i, carry):
        sweep(ua, ub, 2 * i + 1)
        sweep(ub, ua, 2 * i + 2)
        return carry

    lax.fori_loop(0, SWEEPS // 2, two_sweeps, 0)

    lane16 = lane_of(SPAN)
    first = (lane16 & 32) == 0
    row16 = lax.broadcasted_iota(jnp.int32, (SPAN, LANES), 0)

    def slots(x, m):
        r = pl.multiple_of(PAD + (x + DEPTH) * SPAN, 8)
        near = pl.ds(pl.multiple_of(PAD + (x + 1) * SPAN, 8), SPAN)
        for j in range(QUADS):
            c = ua[j, pl.ds(r, SPAN), :] * m
            t = roll(c, 64)
            u = 0.5 * jnp.where(lane16 < 64, c + t, t - c)
            ub[j, pl.ds(r, SPAN), :] = u
            fd[j, near, :] = jnp.where(first, roll(u, -16), roll(u, 16))

    tall = lambda a: jnp.concatenate([a, a], axis=0)
    beside = jnp.where(row16 >= 12, tall(y_sign[0][1]), jnp.where(row16 < 4, tall(y_sign[0][-1]), 1.0))
    slots(-1, mx[0])
    slots(SIDE, mx[1])
    lax.fori_loop(0, SIDE, lambda x, carry: (slots(x, beside), carry)[1], 0)

    even = (lane & 32) == 0

    def by_ion(values, k):
        return jnp.where(even, values[2 * k], values[2 * k + 1])

    half_charge = [by_ion([0.5 * v for v in valences], k) for k in range(PAIRS)]
    rates = [by_ion([diffusivity[i] for i in range(6)], k) for k in range(PAIRS)]
    signs = [by_ion(reaction_signs, k) for k in range(PAIRS)]
    reactivity = [rate_const[b] * opened[b].astype(jnp.float32) for b in range(2)]
    reactivity = jnp.where(low, reactivity[0], reactivity[1])
    given = give_slot[0]
    up_turned = jnp.broadcast_to(own[4:5, :], (8, LANES)) > 0
    down_turned = jnp.broadcast_to(own[5:6, :], (8, LANES)) > 0
    top, bottom = lane32 == 31, lane32 == 0

    for half in range(2):

        def update(i, carry, half=half):
            x = i + half * HALF
            r = pl.multiple_of(PAD + (x + DEPTH) * SPAN, 8)
            q = pl.multiple_of(PAD + (x + 1) * SPAN, 8)
            here, left, right = pl.ds(q + 4, 8), pl.ds(q + 4 - SPAN, 8), pl.ds(q + 4 + SPAN, 8)
            north_at, south_at = pl.ds(q + 5, 8), pl.ds(q + 3, 8)
            done = [[None] * QUADS for _ in range(PAIRS + 1)]
            for j in range(QUADS):
                zat = pl.ds(pl.multiple_of(j * (PLANE // 2) + i * 8, 8), 8)
                zu, zd = zup[zat, :], zdn[zat, :]
                zu = jnp.where(up_turned, zu, roll(zu, 64))
                zd = jnp.where(down_turned, zd, roll(zd, 64))

                def around(ref, lead, off):
                    c = ref[lead + (j, here)]
                    return c, (
                        ref[lead + (j, right)],
                        ref[lead + (j, left)],
                        ref[lead + (j + 1, here)] if j < 3 else ref[lead + (0, north_at)],
                        ref[lead + (j - 1, here)] if j > 0 else ref[lead + (3, south_at)],
                        jnp.where(top, roll(zu, 31 - off - 16 * half), roll(c, -1)),
                        jnp.where(bottom, roll(zd, off - 31 + 16 * (1 - half)), roll(c, 1)),
                    )

                w, near_w = around(we, (), 12)
                u = ub[j, pl.ds(r + 4, 8), :]
                phi = fd[j, here, :]
                near_phi = (
                    fd[j, right, :],
                    fd[j, left, :],
                    fd[j + 1, here, :] if j < 3 else fd[0, north_at, :],
                    fd[j - 1, here, :] if j > 0 else fd[3, south_at, :],
                    jnp.where(even, roll(u, -17), roll(u, 15)),
                    jnp.where(even, roll(u, -15), roll(u, 17)),
                )
                drift = [near_w[d] * (phi - near_phi[d]) for d in range(6)]
                w_total = functools.reduce(lambda a, b: a + b, near_w)
                d_total = functools.reduce(lambda a, b: a + b, drift)
                conc = []
                for k in range(PAIRS):
                    c, near_c = around(se, (k,), 9 + k)
                    spread_w = functools.reduce(lambda a, b: a + b, [near_w[d] * near_c[d] for d in range(6)])
                    spread_d = functools.reduce(lambda a, b: a + b, [drift[d] * near_c[d] for d in range(6)])
                    outflow = w * ((c * w_total - spread_w) + half_charge[k] * (c * d_total + spread_d))
                    conc.append(c)
                    done[k][j] = c - rates[k] * outflow
                other = jnp.where(even, roll(conc[0], 96), roll(conc[0], 32))
                third = jnp.where(even, conc[1], roll(conc[1], 32))
                reaction = third - conc[0] * other / solubility
                reaction = jnp.where(w > 0, reactivity * reaction, 0.0)
                for k in range(PAIRS):
                    done[k][j] = done[k][j] + signs[k] * reaction
                done[PAIRS][j] = phi
            at = pl.ds(pl.multiple_of(x * 8, 8), 8)
            to = [pl.ds(x * 16 + b, 8, stride=2) for b in range(2)]
            for k in range(PAIRS + 1):
                native = swap_groups(done[k], lane)
                for f in range(2 if k < PAIRS else 1):
                    ion = 2 * k + f
                    for b in range(2):
                        if k < PAIRS:
                            out_sp[ion, to[b], :] = native[2 * b + f]
                        else:
                            out_pot[to[b], :] = native[2 * b]
                    send[ion, at, :] = jnp.where(given == 0, native[f], native[2 + f])
            return carry

        lax.fori_loop(0, HALF, update, 0)


def place_kernel(flags, received, sp_in, pot_in, sp_out, pot_out, sem):
    give = flags[1]

    @pl.when(flags[0] > 0)
    def _():
        ions = received.shape[0] - 1
        copies = [
            pltpu.make_async_copy(received.at[i], sp_out.at[i, :, give] if i < ions else pot_out.at[:, give], sem.at[i])
            for i in range(ions + 1)
        ]
        for c in copies:
            c.start()
        for c in copies:
            c.wait()


VMEM = pl.BlockSpec(memory_space=pltpu.VMEM)
SMEM = pl.BlockSpec(memory_space=pltpu.SMEM)
ANY = pl.BlockSpec(memory_space=pl.ANY)
PARAMS = pltpu.CompilerParams(vmem_limit_bytes=48 * 1024 * 1024)


def f32(*shape):
    return jax.ShapeDtypeStruct(shape, jnp.float32)


def rows_of(field):
    lead = field.shape[:-2]
    bricks, cells = field.shape[-2:]
    split = field.reshape(lead + (bricks, cells // LANES, LANES))
    return jnp.swapaxes(split, -3, -2).reshape(lead + (bricks * cells // LANES, LANES))


def cells_of(split):
    lead = split.shape[:-3]
    rows, bricks, _ = split.shape[-3:]
    return jnp.swapaxes(split, -3, -2).reshape(lead + (bricks, rows * LANES))


def moved(block, axis, offset):
    n = lax.axis_size(axis)
    return lax.ppermute(block, axis, [(i, (i + offset) % n) for i in range(n)])


def local(
    species,
    potential,
    pore,
    openness,
    neighbours,
    diffusivity,
    rate_const,
    opened,
    partner,
    give_slot,
):
    ion_count, brick_count, cells = species.shape
    dev_count = lax.axis_size("dev")
    stride = dev_count // 4

    held = {}
    for sx, sy in SIDES + CORNERS:
        offset = (sx + sy * stride) % dev_count
        offset = offset if offset <= dev_count // 2 else offset - dev_count
        rows, pieces = held.get(offset, (0, ()))
        held[offset] = (rows + (FACE_ROWS if 0 in (sx, sy) else EDGE_ROWS), pieces + (((sx, sy), rows),))
    offsets = sorted(held, key=lambda o: (-held[o][0], -abs(o), o))
    pieces = tuple(held[o][1] for o in offsets)

    packed = pl.pallas_call(
        functools.partial(pack_kernel, pieces),
        out_shape=(
            f32(PAIRS, QUADS, PLANE, LANES),
            f32(QUADS, PLANE, LANES),
            f32(QUADS, PLANE, LANES),
            f32(8, LANES),
            *(f32(held[o][0], LANES) for o in offsets),
            f32(ZC_ROWS, LANES),
            f32(ZC_ROWS, LANES),
        ),
        in_specs=[VMEM] * 4 + [SMEM],
        out_specs=tuple([VMEM] * (6 + len(offsets))),
        compiler_params=PARAMS,
        name="pack",
    )(rows_of(species), rows_of(potential), rows_of(pore), rows_of(openness), neighbours)
    sp, wd, pd, own = packed[:4]
    arrived = [moved(block, "dev", o) for block, o in zip(packed[4 : 4 + len(offsets)], offsets)]
    zup = moved(packed[-2], "group", -1)
    zdn = moved(packed[-1], "group", 1)

    zl, zh = pl.pallas_call(
        functools.partial(relay_kernel, pieces),
        out_shape=(f32(ZH_ROWS, LANES),) * 2,
        in_specs=[VMEM] * len(offsets),
        out_specs=(VMEM, VMEM),
        compiler_params=PARAMS,
        name="relay",
    )(*arrived)
    zhup = moved(zl, "group", -1)
    zhdn = moved(zh, "group", 1)

    wide = pltpu.VMEM((QUADS, EXT * SPAN + 2 * PAD, LANES), jnp.float32)
    near = pltpu.VMEM((QUADS, NEAR * SPAN + 2 * PAD, LANES), jnp.float32)
    out_sp, out_pot, outgoing = pl.pallas_call(
        functools.partial(step_kernel, pieces),
        out_shape=(
            f32(ion_count, brick_count * PLANE, LANES),
            f32(brick_count * PLANE, LANES),
            f32(ion_count + 1, PLANE, LANES),
        ),
        in_specs=[VMEM] * (8 + len(offsets)) + [SMEM] * 4,
        out_specs=(VMEM, VMEM, VMEM),
        scratch_shapes=[
            wide,
            wide,
            wide,
            near,
            pltpu.VMEM((PAIRS, QUADS, NEAR * SPAN + 2 * PAD, LANES), jnp.float32),
            near,
            pltpu.VMEM((2, SPAN, LANES), jnp.float32),
            pltpu.VMEM((3, SPAN, LANES), jnp.float32),
            pltpu.VMEM((3, SPAN, LANES), jnp.float32),
        ],
        compiler_params=PARAMS,
        name="step",
    )(sp, wd, pd, own, zup, zdn, zhup, zhdn, *arrived, diffusivity, rate_const, opened, give_slot)

    axes = ("group", "dev")
    total = lax.axis_size("group") * dev_count
    own_index = lax.axis_index("group") * dev_count + lax.axis_index("dev")
    apart = jnp.bitwise_xor(own_index, partner[0])
    branch = jnp.int32(0)
    branches = [lambda block: block]
    for bit in range(total.bit_length() - 1):
        route = [(i, i ^ (1 << bit)) for i in range(total)]
        branch = jnp.where(apart == (1 << bit), bit + 1, branch)
        branches.append(lambda block, route=route: lax.ppermute(block, axes, route))
    received = lax.switch(branch, branches, outgoing)

    split_sp = out_sp.reshape(ion_count, PLANE, brick_count, LANES)
    split_pot = out_pot.reshape(PLANE, brick_count, LANES)
    flags = jnp.stack([(apart != 0).astype(jnp.int32), give_slot[0]])
    new_sp, new_pot = pl.pallas_call(
        place_kernel,
        out_shape=(f32(*split_sp.shape), f32(*split_pot.shape)),
        in_specs=[SMEM, ANY, ANY, ANY],
        out_specs=(ANY, ANY),
        scratch_shapes=[pltpu.SemaphoreType.DMA((ion_count + 1,))],
        input_output_aliases={2: 0, 3: 1},
        name="place",
    )(flags, received, split_sp, split_pot)
    return cells_of(new_sp), cells_of(new_pot)


def solution(mesh):
    in_specs = (
        P(None, ("group", "dev"), None),
        P(("group", "dev"), None),
        P(("group", "dev"), None),
        P(("group", "dev"), None),
        P(("group", "dev"), None),
        P(),
        P(("group", "dev")),
        P(("group", "dev")),
        P(("group", "dev")),
        P(("group", "dev")),
    )
    out_specs = (P(None, ("group", "dev"), None), P(("group", "dev"), None))
    return jax.shard_map(local, mesh=mesh, in_specs=in_specs, out_specs=out_specs, check_vma=False)
```

```python
import functools

import jax
import jax.numpy as jnp
from jax import lax
from jax.experimental import pallas as pl
from jax.experimental.pallas import tpu as pltpu
from jax.sharding import PartitionSpec as P


SWEEPS = 8
DEPTH = SWEEPS + 1
LANES = 128

charge_scale = 0.5
screening = 0.5
solubility = 2.0
valences = (2.0, -1.0, 1.0, -1.0, 1.0, 2.0)
reaction_signs = (1.0, 1.0, -1.0, 0.0, 0.0, 0.0)

SIDE = 32
QUADS = 4
YQ = SIDE // QUADS
PAIRS = 3
PLANE = SIDE * YQ
HALF = SIDE // 2

FACE_SP = DEPTH * SIDE
FACE_WET = FACE_SP + PAIRS * SIDE
FACE_TBL = FACE_WET + SIDE
FACE_ROWS = FACE_TBL + 8
EDGE_TBL = 64
EDGE_ROWS = EDGE_TBL + 8
ZC_TBL = QUADS * PLANE // 2
ZC_ROWS = ZC_TBL + 8
ZH_EDGE = 4 * 2 * SIDE
ZH_TBL = ZH_EDGE + 64
ZH_ROWS = ZH_TBL + 32

ZH_PLACE = {0: (0, 0), 3: (0, 8), 4: (0, 13), 7: (0, 17), 1: (1, 0), 2: (1, 7), 5: (1, 13), 6: (1, 16)}

SIDES = ((-1, 0), (1, 0), (0, -1), (0, 1))
CORNERS = ((-1, -1), (-1, 1), (1, -1), (1, 1))
SPAN = 16
EXT = SIDE + 2 * DEPTH
MIDDLE = 10
NEAR = SIDE + 2
PAD = 24


def x_way(s):
    return 0 if s > 0 else 1


def y_way(s):
    return 2 if s > 0 else 3


def z_way(s):
    return 4 if s > 0 else 5


def roll(v, shift):
    shift = shift % LANES
    return v if shift == 0 else pltpu.roll(v, shift, 1)


def lane_of(rows):
    return lax.broadcasted_iota(jnp.int32, (rows, LANES), 1)


def swap_groups(v, lane):
    low = lane < 64
    a0 = jnp.where(low, v[0], roll(v[2], 64))
    a2 = jnp.where(low, roll(v[0], 64), v[2])
    a1 = jnp.where(low, v[1], roll(v[3], 64))
    a3 = jnp.where(low, roll(v[1], 64), v[3])
    even = (lane & 32) == 0
    return (
        jnp.where(even, a0, roll(a1, 32)),
        jnp.where(even, roll(a0, 96), a1),
        jnp.where(even, a2, roll(a3, 32)),
        jnp.where(even, roll(a2, 96), a3),
    )


def pack_kernel(pieces, species, potential, pore, openness, neighbours, sp, wd, pd, own, *rest):
    n_out = len(pieces)
    outs, (zlo, zhi) = rest[:n_out], rest[n_out:]
    where = {name: (outs[k], base) for k, held in enumerate(pieces) for name, base in held}
    lane = lane_of(8)
    lane32 = lane & 31
    low = lane < 64

    row_of = lax.broadcasted_iota(jnp.int32, (8, LANES), 0)
    table = jnp.zeros((8, LANES), jnp.float32)
    for way in range(6):
        sign = jnp.where(neighbours[0, way] == 0, 1.0, -1.0)
        table = jnp.where(row_of == way, sign, table)
    own[...] = table

    def planes_of(x):
        rows = [pl.ds(x * 16 + b, 8, stride=2) for b in range(2)]
        s = [[species[i, rows[b], :] for b in range(2)] for i in range(6)]
        w, d, p = [], [], []
        for b in range(2):
            wet = pore[rows[b], :].astype(jnp.float32) * openness[rows[b], :]
            total = valences[0] * s[0][b]
            for i in range(1, 6):
                total = total + valences[i] * s[i][b]
            w.append(wet)
            d.append(charge_scale * wet * total)
            p.append(potential[rows[b], :])
        ions = [swap_groups((s[k][0], s[k + PAIRS][0], s[k][1], s[k + PAIRS][1]), lane) for k in range(PAIRS)]
        wets = swap_groups((w[0], w[0], w[1], w[1]), lane)
        mixed = []
        for v in swap_groups((p[0], d[0], p[1], d[1]), lane):
            r = roll(v, 64)
            mixed.append(jnp.where(low, v + r, r - v))
        at = pl.ds(pl.multiple_of(x * 8, 8), 8)
        for j in range(QUADS):
            pd[j, at, :] = mixed[j]
            wd[j, at, :] = wets[j]
            for k in range(PAIRS):
                sp[k, j, at, :] = ions[k][j]
        return mixed, wets, ions

    def step(x, carry):
        first, second = planes_of(x), planes_of(x + HALF)
        for j in range(QUADS):
            at = pl.ds(pl.multiple_of(j * (PLANE // 2) + x * 8, 8), 8)
            lo = first[0][j]
            lo = jnp.where(lane32 >= 16, roll(second[0][j], 16), lo)
            hi = second[0][j]
            hi = jnp.where(lane32 < 16, roll(first[0][j], -16), hi)
            for k in range(PAIRS):
                lo = jnp.where(lane32 == 9 + k, roll(first[2][k][j], 9 + k), lo)
                lo = jnp.where(lane32 == 25 + k, roll(second[2][k][j], 25 + k), lo)
                hi = jnp.where(lane32 == 22 - k, roll(second[2][k][j], -9 - k), hi)
                hi = jnp.where(lane32 == 6 - k, roll(first[2][k][j], -25 - k), hi)
            lo = jnp.where(lane32 == 12, roll(first[1][j], 12), lo)
            lo = jnp.where(lane32 == 28, roll(second[1][j], 28), lo)
            hi = jnp.where(lane32 == 19, roll(second[1][j], -12), hi)
            hi = jnp.where(lane32 == 3, roll(first[1][j], -28), hi)
            zlo[at, :] = lo
            zhi[at, :] = hi
        return carry

    lax.fori_loop(0, HALF, step, 0)

    zlo[ZC_TBL:, :] = table
    zhi[ZC_TBL:, :] = table
    for sx, sy in SIDES:
        ref, base = where[(sx, sy)]
        for l in range(DEPTH):
            if sx:
                x = l if sx < 0 else SIDE - 1 - l
                for j in range(QUADS):
                    ref[base + l * SIDE + j * 8 : base + l * SIDE + j * 8 + 8, :] = pd[j, x * 8 : x * 8 + 8, :]
            else:
                y = l if sy < 0 else SIDE - 1 - l
                ref[base + l * SIDE : base + (l + 1) * SIDE, :] = pd[y % 4, pl.ds(y // 4, SIDE, stride=8), :]
        for k in range(PAIRS + 1):
            start = base + FACE_SP + k * SIDE
            for j in range(QUADS) if sx else range(1):
                if sx:
                    x = 0 if sx < 0 else SIDE - 1
                    pick, at = (j, slice(x * 8, x * 8 + 8)), slice(start + j * 8, start + j * 8 + 8)
                else:
                    y = 0 if sy < 0 else SIDE - 1
                    pick, at = (y % 4, pl.ds(y // 4, SIDE, stride=8)), slice(start, start + SIDE)
                ref[at, :] = sp[k, pick[0], pick[1], :] if k < PAIRS else wd[pick[0], pick[1], :]
        ref[base + FACE_TBL : base + FACE_ROWS, :] = table
    for sx, sy in CORNERS:
        ref, base = where[(sx, sy)]
        x0 = 0 if sx < 0 else SIDE - 8
        for m in range(8):
            y = m if sy < 0 else SIDE - 8 + m
            ref[base + m * 8 : base + m * 8 + 8, :] = pd[y % 4, pl.ds(x0 * 8 + y // 4, 8, stride=8), :]
        ref[base + EDGE_TBL : base + EDGE_ROWS, :] = table


def relay_kernel(pieces, *refs):
    arrived, (zl, zh) = refs[:-4], refs[-2:]
    where = {name: (arrived[k], base) for k, held in enumerate(pieces) for name, base in held}
    lane32 = lane_of(SIDE) & 31
    for number, (sx, sy) in enumerate(SIDES):
        ref, base = where[(-sx, -sy)]
        lo = [jnp.zeros((SIDE, LANES), jnp.float32)] * 2
        hi = [jnp.zeros((SIDE, LANES), jnp.float32)] * 2
        for l in range(8):
            block, off = ZH_PLACE[l]
            width = 8 - l
            v = ref[base + l * SIDE : base + (l + 1) * SIDE, :]
            lo[block] = jnp.where((lane32 >= off) & (lane32 < off + width), roll(v, off), lo[block])
            hi[block] = jnp.where((lane32 <= 31 - off) & (lane32 > 31 - off - width), roll(v, -off), hi[block])
        for block in range(2):
            at = slice((number * 2 + block) * SIDE, (number * 2 + block + 1) * SIDE)
            zl[at, :] = lo[block]
            zh[at, :] = hi[block]
        at = slice(ZH_TBL + number * 8, ZH_TBL + number * 8 + 8)
        zl[at, :] = ref[base + FACE_TBL : base + FACE_ROWS, :]
        zh[at, :] = ref[base + FACE_TBL : base + FACE_ROWS, :]
    group = lane_of(64) & 31
    lo = jnp.zeros((64, LANES), jnp.float32)
    hi = lo
    for number, (sx, sy) in enumerate(CORNERS):
        ref, base = where[(-sx, -sy)]
        v = ref[base : base + EDGE_TBL, :]
        lo = jnp.where((group >= 8 * number) & (group < 8 * number + 8), roll(v, 8 * number), lo)
        hi = jnp.where((group <= 31 - 8 * number) & (group > 23 - 8 * number), roll(v, -8 * number), hi)
    zl[ZH_EDGE : ZH_EDGE + 64, :] = lo
    zh[ZH_EDGE : ZH_EDGE + 64, :] = hi


def step_kernel(
    pieces,
    sp,
    wd,
    pd,
    own,
    zup,
    zdn,
    zhup,
    zhdn,
    *rest,
):
    n_in = len(pieces)
    arrived = rest[:n_in]
    diffusivity, rate_const, opened, give_slot = rest[n_in : n_in + 4]
    keep, send = rest[n_in + 4 : n_in + 6]
    ua, ub, dn, fd, se, we, mx, myp, mym = rest[n_in + 6 :]
    where = {name: (arrived[k], base) for k, held in enumerate(pieces) for name, base in held}

    lane = lane_of(8)
    lane32, lane64 = lane & 31, lane & 63
    low = lane < 64
    core = (lane64 >= 16) & (lane64 < 48)
    upper = lane64 >= 48

    table = {(0, 0): own[...]}
    ztable = {1: {(0, 0): zup[ZC_TBL:, :]}, -1: {(0, 0): zdn[ZC_TBL:, :]}}
    for number, (sx, sy) in enumerate(SIDES):
        ref, base = where[(-sx, -sy)]
        table[(sx, sy)] = ref[base + FACE_TBL : base + FACE_ROWS, :]
        for sz, held in ((1, zhup), (-1, zhdn)):
            ztable[sz][(sx, sy)] = held[ZH_TBL + number * 8 : ZH_TBL + number * 8 + 8, :]
    for sx, sy in CORNERS:
        ref, base = where[(-sx, -sy)]
        table[(sx, sy)] = ref[base + EDGE_TBL : base + EDGE_ROWS, :]

    def sign(held, way):
        return jnp.broadcast_to(held[way : way + 1, :], (8, LANES))

    def crossing(way, here, there):
        level = sign(table[here], way)
        beyond = {}
        for sz in (1, -1):
            z = z_way(sz)
            beyond[sz] = sign(ztable[sz][here], way) * sign(table[here], z) * sign(table[there], z)
        m = jnp.where(core, level, jnp.where(upper, beyond[1], beyond[-1]))
        return jnp.where(low, 1.0, m)

    row8 = lax.broadcasted_iota(jnp.int32, (8, LANES), 0)
    one = jnp.ones((8, LANES), jnp.float32)
    for number, sx in enumerate((-1, 1)):
        m = {sy: crossing(x_way(sx), (0, sy), (sx, sy)) for sy in (-1, 0, 1)}
        mx[number, 0:8, :] = jnp.where(row8 < 4, m[-1], m[0])
        mx[number, 8:16, :] = jnp.where(row8 < 4, m[0], m[1])
    y_sign = {}
    for number, sx in enumerate((-1, 0, 1)):
        m = {sy: crossing(y_way(sy), (sx, 0), (sx, sy)) for sy in (-1, 1)}
        y_sign[sx] = m
        myp[number, 0:8, :] = jnp.where(row8 == 3, m[-1], one)
        myp[number, 8:16, :] = jnp.where(row8 == 3, m[1], one)
        mym[number, 0:8, :] = jnp.where(row8 == 4, m[-1], one)
        mym[number, 8:16, :] = jnp.where(row8 == 4, m[1], one)

    outer = {}
    for key, held in table.items():
        m = jnp.where(upper, sign(held, 4), sign(held, 5))
        outer[key] = jnp.where(low, 1.0, m)

    def spread(v, zu, zd, shift_u, shift_d, key):
        rows = v.shape[0]
        tall = lambda a: a if rows == 8 else jnp.concatenate([a] * (rows // 8), axis=0)
        if zu is None:
            return roll(v, 16), roll(v, -16)
        m, c, u = tall(outer[key]), tall(core), tall(upper)
        pot = jnp.where(u, roll(zu, 48 + shift_u), roll(zd, -16 + shift_d)) * m
        rho = jnp.where(u, roll(zu, 16 + shift_u), roll(zd, -48 + shift_d)) * m
        return jnp.where(c, roll(v, 16), pot), jnp.where(c, roll(v, -16), rho)

    for half in range(2):

        def fill(i, carry, half=half):
            x = i + half * HALF
            at = pl.ds(pl.multiple_of(x * 8, 8), 8)
            to = pl.ds(pl.multiple_of(PAD + (x + DEPTH) * SPAN + 4, 4), 8)
            near = pl.ds(pl.multiple_of(PAD + (x + 1) * SPAN + 4, 4), 8)
            for j in range(QUADS):
                zat = pl.ds(pl.multiple_of(j * (PLANE // 2) + i * 8, 8), 8)
                shift_u, shift_d = (0, 16) if half == 0 else (-16, 0)
                pot, rho = spread(pd[j, at, :], zup[zat, :], zdn[zat, :], shift_u, shift_d, (0, 0))
                ua[j, to, :] = pot
                dn[j, to, :] = rho
                we[j, near, :] = wd[j, at, :]
                for k in range(PAIRS):
                    se[k, j, near, :] = sp[k, j, at, :]
            return carry

        lax.fori_loop(0, HALF, fill, 0)

    def turned(v, way):
        s = own[way : way + 1, :]
        return jnp.where(jnp.broadcast_to(s, v.shape) > 0, v, roll(v, 64))

    for number, (sx, sy) in enumerate(SIDES):
        ref, base = where[(-sx, -sy)]
        for l in range(DEPTH):
            v = ref[base + l * SIDE : base + (l + 1) * SIDE, :]
            zu = zd = None
            off = 0
            if l < 8:
                block, off = ZH_PLACE[l]
                at = slice((number * 2 + block) * SIDE, (number * 2 + block + 1) * SIDE)
                zu, zd = zhup[at, :], zhdn[at, :]
            pot, rho = spread(v, zu, zd, -off, off, (sx, sy))
            if sx:
                x = SIDE + l if sx > 0 else -1 - l
                start = PAD + (x + DEPTH) * SPAN + 4
                for j in range(QUADS):
                    ua[j, start : start + 8, :] = pot[j * 8 : j * 8 + 8]
                    dn[j, start : start + 8, :] = rho[j * 8 : j * 8 + 8]
            else:
                j = l % 4 if sy > 0 else 3 - l % 4
                row = 12 + l // 4 if sy > 0 else 3 - l // 4
                at = pl.ds(PAD + DEPTH * SPAN + row, SIDE, stride=SPAN)
                ua[j, at, :] = pot
                dn[j, at, :] = rho
        way = x_way(sx) if sx else y_way(sy)
        for k in range(PAIRS + 1):
            start = base + FACE_SP + k * SIDE
            v = turned(ref[start : start + SIDE, :], way)
            if sx:
                begin = PAD + (SIDE + 1 if sx > 0 else 0) * SPAN + 4
                for j in range(QUADS):
                    if k < PAIRS:
                        se[k, j, begin : begin + 8, :] = v[j * 8 : j * 8 + 8]
                    else:
                        we[j, begin : begin + 8, :] = v[j * 8 : j * 8 + 8]
            else:
                j, row = (0, 12) if sy > 0 else (3, 3)
                at = pl.ds(PAD + SPAN + row, SIDE, stride=SPAN)
                if k < PAIRS:
                    se[k, j, at, :] = v
                else:
                    we[j, at, :] = v
    for number, (sx, sy) in enumerate(CORNERS):
        ref, base = where[(-sx, -sy)]
        for m in range(8):
            v = ref[base + m * 8 : base + m * 8 + 8, :]
            at = slice(ZH_EDGE + m * 8, ZH_EDGE + m * 8 + 8)
            pot, rho = spread(v, zhup[at, :], zhdn[at, :], -8 * number, 8 * number, (sx, sy))
            row = (12 if sy > 0 else 2) + m // 4
            x = SIDE if sx > 0 else -8
            to = pl.ds(PAD + (x + DEPTH) * SPAN + row, 8, stride=SPAN)
            ua[m % 4, to, :] = pot
            dn[m % 4, to, :] = rho

    scale = 1.0 / (6.0 + screening)

    def slab(src, dst, x, sx, before=None, after=None):
        r = pl.multiple_of(PAD + (x + DEPTH) * SPAN, 8)
        at = pl.ds(r, SPAN)
        c = [src[j, at, :] for j in range(QUADS)]
        for j in range(QUADS):
            left = src[j, pl.ds(r - SPAN, SPAN), :]
            right = src[j, pl.ds(r + SPAN, SPAN), :]
            if before is not None:
                left = left * mx[before]
            if after is not None:
                right = right * mx[after]
            north = c[j + 1] if j < 3 else src[0, pl.ds(r + 1, SPAN), :] * myp[sx + 1]
            south = c[j - 1] if j > 0 else src[3, pl.ds(r - 1, SPAN), :] * mym[sx + 1]
            total = (left + right) + (north + south) + (roll(c[j], 1) + roll(c[j], -1)) + dn[j, at, :]
            dst[j, at, :] = total * scale

    def sweep(src, dst, t):
        def middle(i, carry):
            for n in range(MIDDLE):
                slab(src, dst, 1 + i * MIDDLE + n, 0)
            return carry

        def fringe(i, carry):
            for n in range(2):
                slab(src, dst, -2 - 2 * i - n, -1)
                slab(src, dst, SIDE + 1 + 2 * i + n, 1)
            return carry

        lax.fori_loop(0, (SIDE - 2) // MIDDLE, middle, 0)
        slab(src, dst, -1, -1, after=0)
        slab(src, dst, 0, 0, before=0)
        slab(src, dst, SIDE - 1, 0, after=1)
        slab(src, dst, SIDE, 1, before=1)
        lax.fori_loop(0, (SWEEPS + 1 - t) // 2, fringe, 0)

    def two_sweeps(i, carry):
        sweep(ua, ub, 2 * i + 1)
        sweep(ub, ua, 2 * i + 2)
        return carry

    lax.fori_loop(0, SWEEPS // 2, two_sweeps, 0)

    lane16 = lane_of(SPAN)
    first = (lane16 & 32) == 0
    row16 = lax.broadcasted_iota(jnp.int32, (SPAN, LANES), 0)

    def slots(x, m):
        r = pl.multiple_of(PAD + (x + DEPTH) * SPAN, 8)
        near = pl.ds(pl.multiple_of(PAD + (x + 1) * SPAN, 8), SPAN)
        for j in range(QUADS):
            c = ua[j, pl.ds(r, SPAN), :] * m
            t = roll(c, 64)
            u = 0.5 * jnp.where(lane16 < 64, c + t, t - c)
            ub[j, pl.ds(r, SPAN), :] = u
            fd[j, near, :] = jnp.where(first, roll(u, -16), roll(u, 16))

    tall = lambda a: jnp.concatenate([a, a], axis=0)
    beside = jnp.where(row16 >= 12, tall(y_sign[0][1]), jnp.where(row16 < 4, tall(y_sign[0][-1]), 1.0))
    slots(-1, mx[0])
    slots(SIDE, mx[1])
    def all_slots(i, carry):
        for n in range(4):
            slots(4 * i + n, beside)
        return carry

    lax.fori_loop(0, SIDE // 4, all_slots, 0)

    even = (lane & 32) == 0

    def by_ion(values, k):
        return jnp.where(even, values[k], values[k + PAIRS])

    half_charge = [by_ion([0.5 * v for v in valences], k) for k in range(PAIRS)]
    rates = [by_ion([diffusivity[i] for i in range(6)], k) for k in range(PAIRS)]
    signs = [by_ion(reaction_signs, k) for k in range(PAIRS)]
    reactivity = [rate_const[b] * opened[b].astype(jnp.float32) for b in range(2)]
    reactivity = jnp.where(low, reactivity[0], reactivity[1])
    given = give_slot[0]
    up_turned = jnp.broadcast_to(own[4:5, :], (8, LANES)) > 0
    down_turned = jnp.broadcast_to(own[5:6, :], (8, LANES)) > 0
    top, bottom = lane32 == 31, lane32 == 0

    for half in range(2):

        def update(i, carry, half=half):
            x = i + half * HALF
            r = pl.multiple_of(PAD + (x + DEPTH) * SPAN, 8)
            q = pl.multiple_of(PAD + (x + 1) * SPAN, 8)
            here, left, right = pl.ds(q + 4, 8), pl.ds(q + 4 - SPAN, 8), pl.ds(q + 4 + SPAN, 8)
            north_at, south_at = pl.ds(q + 5, 8), pl.ds(q + 3, 8)
            done = [[None] * QUADS for _ in range(PAIRS + 1)]
            for j in range(QUADS):
                zat = pl.ds(pl.multiple_of(j * (PLANE // 2) + i * 8, 8), 8)
                zu, zd = zup[zat, :], zdn[zat, :]
                zu = jnp.where(up_turned, zu, roll(zu, 64))
                zd = jnp.where(down_turned, zd, roll(zd, 64))

                def around(ref, lead, off):
                    c = ref[lead + (j, here)]
                    return c, (
                        ref[lead + (j, right)],
                        ref[lead + (j, left)],
                        ref[lead + (j + 1, here)] if j < 3 else ref[lead + (0, north_at)],
                        ref[lead + (j - 1, here)] if j > 0 else ref[lead + (3, south_at)],
                        jnp.where(top, roll(zu, 31 - off - 16 * half), roll(c, -1)),
                        jnp.where(bottom, roll(zd, off - 31 + 16 * (1 - half)), roll(c, 1)),
                    )

                w, near_w = around(we, (), 12)
                u = ub[j, pl.ds(r + 4, 8), :]
                phi = fd[j, here, :]
                near_phi = (
                    fd[j, right, :],
                    fd[j, left, :],
                    fd[j + 1, here, :] if j < 3 else fd[0, north_at, :],
                    fd[j - 1, here, :] if j > 0 else fd[3, south_at, :],
                    jnp.where(even, roll(u, -17), roll(u, 15)),
                    jnp.where(even, roll(u, -15), roll(u, 17)),
                )
                drift = [near_w[d] * (phi - near_phi[d]) for d in range(6)]
                w_total = functools.reduce(lambda a, b: a + b, near_w)
                d_total = functools.reduce(lambda a, b: a + b, drift)
                conc = []
                for k in range(PAIRS):
                    c, near_c = around(se, (k,), 9 + k)
                    spread_w = functools.reduce(lambda a, b: a + b, [near_w[d] * near_c[d] for d in range(6)])
                    spread_d = functools.reduce(lambda a, b: a + b, [drift[d] * near_c[d] for d in range(6)])
                    outflow = w * ((c * w_total - spread_w) + half_charge[k] * (c * d_total + spread_d))
                    conc.append(c)
                    done[k][j] = c - rates[k] * outflow
                reaction = conc[2] - conc[0] * conc[1] / solubility
                reaction = jnp.where(w > 0, reactivity * reaction, 0.0)
                for k in range(PAIRS):
                    done[k][j] = done[k][j] + signs[k] * reaction
                done[PAIRS][j] = phi
            at = pl.ds(pl.multiple_of(x * 8, 8), 8)
            for k in range(PAIRS + 1):
                native = swap_groups(done[k], lane)
                for f in range(2 if k < PAIRS else 1):
                    ion = k + f * PAIRS if k < PAIRS else 2 * PAIRS
                    send[ion, at, :] = jnp.where(given == 0, native[f], native[2 + f])
                    keep[ion, at, :] = jnp.where(given == 0, native[2 + f], native[f])
            return carry

        lax.fori_loop(0, HALF, update, 0)


def place_kernel(give_slot, keep, received, new_sp, new_pot):
    given = give_slot[0]
    theirs, ours = pl.ds(given, PLANE, stride=2), pl.ds(1 - given, PLANE, stride=2)
    ions = new_sp.shape[0]
    for i in range(ions):
        new_sp[i, theirs, :] = received[i]
        new_sp[i, ours, :] = keep[i]
    new_pot[theirs, :] = received[ions]
    new_pot[ours, :] = keep[ions]


VMEM = pl.BlockSpec(memory_space=pltpu.VMEM)
SMEM = pl.BlockSpec(memory_space=pltpu.SMEM)
ANY = pl.BlockSpec(memory_space=pl.ANY)
PARAMS = pltpu.CompilerParams(vmem_limit_bytes=28 * 1024 * 1024)


def f32(*shape):
    return jax.ShapeDtypeStruct(shape, jnp.float32)


def rows_of(field):
    lead = field.shape[:-2]
    bricks, cells = field.shape[-2:]
    split = field.reshape(lead + (bricks, cells // LANES, LANES))
    return jnp.swapaxes(split, -3, -2).reshape(lead + (bricks * cells // LANES, LANES))


def cells_of(rows):
    lead = rows.shape[:-2]
    count, lanes = rows.shape[-2:]
    split = rows.reshape(lead + (count // 2, 2, lanes))
    return jnp.swapaxes(split, -3, -2).reshape(lead + (2, count // 2 * lanes))


def moved(block, axis, offset):
    n = lax.axis_size(axis)
    return lax.ppermute(block, axis, [(i, (i + offset) % n) for i in range(n)])


def local(
    species,
    potential,
    pore,
    openness,
    neighbours,
    diffusivity,
    rate_const,
    opened,
    partner,
    give_slot,
):
    ion_count, brick_count, cells = species.shape
    dev_count = lax.axis_size("dev")
    stride = dev_count // 4

    held = {}
    for sx, sy in SIDES + CORNERS:
        offset = (sx + sy * stride) % dev_count
        offset = offset if offset <= dev_count // 2 else offset - dev_count
        rows, pieces = held.get(offset, (0, ()))
        held[offset] = (rows + (FACE_ROWS if 0 in (sx, sy) else EDGE_ROWS), pieces + (((sx, sy), rows),))
    offsets = sorted(held, key=lambda o: (-held[o][0], -abs(o), o))
    pieces = tuple(held[o][1] for o in offsets)

    packed = pl.pallas_call(
        functools.partial(pack_kernel, pieces),
        out_shape=(
            f32(PAIRS, QUADS, PLANE, LANES),
            f32(QUADS, PLANE, LANES),
            f32(QUADS, PLANE, LANES),
            f32(8, LANES),
            *(f32(held[o][0], LANES) for o in offsets),
            f32(ZC_ROWS, LANES),
            f32(ZC_ROWS, LANES),
        ),
        in_specs=[VMEM] * 4 + [SMEM],
        out_specs=tuple([VMEM] * (6 + len(offsets))),
        compiler_params=PARAMS,
        name="pack",
    )(rows_of(species), rows_of(potential), rows_of(pore), rows_of(openness), neighbours)
    sp, wd, pd, own = packed[:4]
    arrived = [moved(block, "dev", o) for block, o in zip(packed[4 : 4 + len(offsets)], offsets)]
    zup = moved(packed[-2], "group", -1)
    zdn = moved(packed[-1], "group", 1)

    zl, zh = pl.pallas_call(
        functools.partial(relay_kernel, pieces),
        out_shape=(f32(ZH_ROWS, LANES),) * 2,
        in_specs=[VMEM] * len(offsets) + [ANY] * 2,
        out_specs=(VMEM, VMEM),
        compiler_params=PARAMS,
        name="relay",
    )(*arrived, zup, zdn)
    zhup = moved(zl, "group", -1)
    zhdn = moved(zh, "group", 1)

    wide = pltpu.VMEM((QUADS, EXT * SPAN + 2 * PAD, LANES), jnp.float32)
    near = pltpu.VMEM((QUADS, NEAR * SPAN + 2 * PAD, LANES), jnp.float32)
    kept, outgoing = pl.pallas_call(
        functools.partial(step_kernel, pieces),
        out_shape=(f32(ion_count + 1, PLANE, LANES),) * 2,
        in_specs=[VMEM] * (8 + len(offsets)) + [SMEM] * 4,
        out_specs=(VMEM, VMEM),
        scratch_shapes=[
            wide,
            wide,
            wide,
            near,
            pltpu.VMEM((PAIRS, QUADS, NEAR * SPAN + 2 * PAD, LANES), jnp.float32),
            near,
            pltpu.VMEM((2, SPAN, LANES), jnp.float32),
            pltpu.VMEM((3, SPAN, LANES), jnp.float32),
            pltpu.VMEM((3, SPAN, LANES), jnp.float32),
        ],
        compiler_params=PARAMS,
        name="step",
    )(sp, wd, pd, own, zup, zdn, zhup, zhdn, *arrived, diffusivity, rate_const, opened, give_slot)

    axes = ("group", "dev")
    total = lax.axis_size("group") * dev_count
    own_index = lax.axis_index("group") * dev_count + lax.axis_index("dev")
    apart = jnp.bitwise_xor(own_index, partner[0])
    branch = jnp.int32(0)
    branches = [lambda block: block]
    for bit in range(total.bit_length() - 1):
        route = [(i, i ^ (1 << bit)) for i in range(total)]
        branch = jnp.where(apart == (1 << bit), bit + 1, branch)
        branches.append(lambda block, route=route: lax.ppermute(block, axes, route))
    received = lax.switch(branch, branches, outgoing)

    new_sp, new_pot = pl.pallas_call(
        place_kernel,
        out_shape=(f32(ion_count, brick_count * PLANE, LANES), f32(brick_count * PLANE, LANES)),
        in_specs=[SMEM, VMEM, VMEM],
        out_specs=(VMEM, VMEM),
        compiler_params=PARAMS,
        name="place",
    )(give_slot, kept, received)
    return cells_of(new_sp), cells_of(new_pot)


def solution(mesh):
    in_specs = (
        P(None, ("group", "dev"), None),
        P(("group", "dev"), None),
        P(("group", "dev"), None),
        P(("group", "dev"), None),
        P(("group", "dev"), None),
        P(),
        P(("group", "dev")),
        P(("group", "dev")),
        P(("group", "dev")),
        P(("group", "dev")),
    )
    out_specs = (P(None, ("group", "dev"), None), P(("group", "dev"), None))
    return jax.shard_map(local, mesh=mesh, in_specs=in_specs, out_specs=out_specs, check_vma=False)
```

```python
import functools

import jax
import jax.numpy as jnp
from jax import lax
from jax.experimental import pallas as pl
from jax.experimental.pallas import tpu as pltpu
from jax.sharding import PartitionSpec as P


SWEEPS = 8
DEPTH = SWEEPS + 1
LANES = 128

charge_scale = 0.5
screening = 0.5
solubility = 2.0
valences = (2.0, -1.0, 1.0, -1.0, 1.0, 2.0)
reaction_signs = (1.0, 1.0, -1.0, 0.0, 0.0, 0.0)

SIDE = 32
QUADS = 4
YQ = SIDE // QUADS
PAIRS = 3
PLANE = SIDE * YQ
HALF = SIDE // 2

FACE_SP = DEPTH * SIDE
FACE_WET = FACE_SP + PAIRS * SIDE
FACE_TBL = FACE_WET + SIDE
FACE_ROWS = FACE_TBL + 8
EDGE_TBL = 64
EDGE_ROWS = EDGE_TBL + 8
ZC_TBL = QUADS * PLANE // 2
ZC_ROWS = ZC_TBL + 8
ZH_EDGE = 4 * 2 * SIDE
ZH_TBL = ZH_EDGE + 64
ZH_ROWS = ZH_TBL + 32

ZH_PLACE = {0: (0, 0), 3: (0, 8), 4: (0, 13), 7: (0, 17), 1: (1, 0), 2: (1, 7), 5: (1, 13), 6: (1, 16)}

SIDES = ((-1, 0), (1, 0), (0, -1), (0, 1))
CORNERS = ((-1, -1), (-1, 1), (1, -1), (1, 1))
SPAN = 16
EXT = SIDE + 2 * DEPTH
MIDDLE = 10
PARTS = 4
NEAR = SIDE + 2
PAD = 24


def x_way(s):
    return 0 if s > 0 else 1


def y_way(s):
    return 2 if s > 0 else 3


def z_way(s):
    return 4 if s > 0 else 5


def roll(v, shift):
    shift = shift % LANES
    return v if shift == 0 else pltpu.roll(v, shift, 1)


def lane_of(rows):
    return lax.broadcasted_iota(jnp.int32, (rows, LANES), 1)


def swap_groups(v, lane):
    low = lane < 64
    a0 = jnp.where(low, v[0], roll(v[2], 64))
    a2 = jnp.where(low, roll(v[0], 64), v[2])
    a1 = jnp.where(low, v[1], roll(v[3], 64))
    a3 = jnp.where(low, roll(v[1], 64), v[3])
    even = (lane & 32) == 0
    return (
        jnp.where(even, a0, roll(a1, 32)),
        jnp.where(even, roll(a0, 96), a1),
        jnp.where(even, a2, roll(a3, 32)),
        jnp.where(even, roll(a2, 96), a3),
    )


def pack_kernel(pieces, species_in, potential_in, pore_in, openness_in, neighbours, sp, wd, pd, own, *rest):
    n_out = len(pieces)
    outs, (zlo, zhi) = rest[:n_out], rest[n_out : n_out + 2]
    species, potential, pore, openness, sems = rest[n_out + 2 :]
    copies = []
    for part in range(PARTS):
        for half in range(2):
            rows = pl.ds((half * PARTS + part) * (PLANE // PARTS), PLANE // PARTS)
            for number, (src, dst) in enumerate(
                ((species_in, species), (potential_in, potential), (pore_in, pore), (openness_in, openness))
            ):
                at = (slice(None), rows) if number == 0 else (rows,)
                copies.append(pltpu.make_async_copy(src.at[at], dst.at[at], sems.at[part, half, number]))
                copies[-1].start()
    where = {name: (outs[k], base) for k, held in enumerate(pieces) for name, base in held}
    lane = lane_of(8)
    lane32 = lane & 31
    low = lane < 64

    row_of = lax.broadcasted_iota(jnp.int32, (8, LANES), 0)
    table = jnp.zeros((8, LANES), jnp.float32)
    for way in range(6):
        sign = jnp.where(neighbours[0, way] == 0, 1.0, -1.0)
        table = jnp.where(row_of == way, sign, table)
    own[...] = table

    def planes_of(x):
        rows = [pl.ds(x * 16 + b, 8, stride=2) for b in range(2)]
        s = [[species[i, rows[b], :] for b in range(2)] for i in range(6)]
        w, d, p = [], [], []
        for b in range(2):
            wet = pore[rows[b], :].astype(jnp.float32) * openness[rows[b], :]
            total = valences[0] * s[0][b]
            for i in range(1, 6):
                total = total + valences[i] * s[i][b]
            w.append(wet)
            d.append(charge_scale * wet * total)
            p.append(potential[rows[b], :])
        ions = [swap_groups((s[k][0], s[k + PAIRS][0], s[k][1], s[k + PAIRS][1]), lane) for k in range(PAIRS)]
        wets = swap_groups((w[0], w[0], w[1], w[1]), lane)
        mixed = []
        for v in swap_groups((p[0], d[0], p[1], d[1]), lane):
            r = roll(v, 64)
            mixed.append(jnp.where(low, v + r, r - v))
        at = pl.ds(pl.multiple_of(x * 8, 8), 8)
        for j in range(QUADS):
            pd[j, at, :] = mixed[j]
            wd[j, at, :] = wets[j]
            for k in range(PAIRS):
                sp[k, j, at, :] = ions[k][j]
        return mixed, wets, ions

    def step(x, carry):
        first, second = planes_of(x), planes_of(x + HALF)
        for j in range(QUADS):
            at = pl.ds(pl.multiple_of(j * (PLANE // 2) + x * 8, 8), 8)
            lo = first[0][j]
            lo = jnp.where(lane32 >= 16, roll(second[0][j], 16), lo)
            hi = second[0][j]
            hi = jnp.where(lane32 < 16, roll(first[0][j], -16), hi)
            for k in range(PAIRS):
                lo = jnp.where(lane32 == 9 + k, roll(first[2][k][j], 9 + k), lo)
                lo = jnp.where(lane32 == 25 + k, roll(second[2][k][j], 25 + k), lo)
                hi = jnp.where(lane32 == 22 - k, roll(second[2][k][j], -9 - k), hi)
                hi = jnp.where(lane32 == 6 - k, roll(first[2][k][j], -25 - k), hi)
            lo = jnp.where(lane32 == 12, roll(first[1][j], 12), lo)
            lo = jnp.where(lane32 == 28, roll(second[1][j], 28), lo)
            hi = jnp.where(lane32 == 19, roll(second[1][j], -12), hi)
            hi = jnp.where(lane32 == 3, roll(first[1][j], -28), hi)
            zlo[at, :] = lo
            zhi[at, :] = hi
        return carry

    for part in range(PARTS):
        for c in copies[part * 8 : part * 8 + 8]:
            c.wait()
        lax.fori_loop(part * (HALF // PARTS), (part + 1) * (HALF // PARTS), step, 0)

    zlo[ZC_TBL:, :] = table
    zhi[ZC_TBL:, :] = table
    for sx, sy in SIDES:
        ref, base = where[(sx, sy)]
        for l in range(DEPTH):
            if sx:
                x = l if sx < 0 else SIDE - 1 - l
                for j in range(QUADS):
                    ref[base + l * SIDE + j * 8 : base + l * SIDE + j * 8 + 8, :] = pd[j, x * 8 : x * 8 + 8, :]
            else:
                y = l if sy < 0 else SIDE - 1 - l
                ref[base + l * SIDE : base + (l + 1) * SIDE, :] = pd[y % 4, pl.ds(y // 4, SIDE, stride=8), :]
        for k in range(PAIRS + 1):
            start = base + FACE_SP + k * SIDE
            for j in range(QUADS) if sx else range(1):
                if sx:
                    x = 0 if sx < 0 else SIDE - 1
                    pick, at = (j, slice(x * 8, x * 8 + 8)), slice(start + j * 8, start + j * 8 + 8)
                else:
                    y = 0 if sy < 0 else SIDE - 1
                    pick, at = (y % 4, pl.ds(y // 4, SIDE, stride=8)), slice(start, start + SIDE)
                ref[at, :] = sp[k, pick[0], pick[1], :] if k < PAIRS else wd[pick[0], pick[1], :]
        ref[base + FACE_TBL : base + FACE_ROWS, :] = table
    cut_corners(where, pd, table)


def corner_kernel(pieces, pd, own, *outs):
    cut_corners({name: (outs[k], base) for k, held in enumerate(pieces) for name, base in held}, pd, own[...])


def cut_corners(where, pd, table):
    for sx, sy in CORNERS:
        if (sx, sy) not in where:
            continue
        ref, base = where[(sx, sy)]
        x0 = 0 if sx < 0 else SIDE - 8
        for m in range(8):
            y = m if sy < 0 else SIDE - 8 + m
            ref[base + m * 8 : base + m * 8 + 8, :] = pd[y % 4, pl.ds(x0 * 8 + y // 4, 8, stride=8), :]
        ref[base + EDGE_TBL : base + EDGE_ROWS, :] = table


def relay_kernel(pieces, *refs):
    arrived, (zl, zh) = refs[:-4], refs[-2:]
    where = {name: (arrived[k], base) for k, held in enumerate(pieces) for name, base in held}
    lane32 = lane_of(SIDE) & 31
    for number, (sx, sy) in enumerate(SIDES):
        ref, base = where[(-sx, -sy)]
        lo = [jnp.zeros((SIDE, LANES), jnp.float32)] * 2
        hi = [jnp.zeros((SIDE, LANES), jnp.float32)] * 2
        for l in range(8):
            block, off = ZH_PLACE[l]
            width = 8 - l
            v = ref[base + l * SIDE : base + (l + 1) * SIDE, :]
            lo[block] = jnp.where((lane32 >= off) & (lane32 < off + width), roll(v, off), lo[block])
            hi[block] = jnp.where((lane32 <= 31 - off) & (lane32 > 31 - off - width), roll(v, -off), hi[block])
        for block in range(2):
            at = slice((number * 2 + block) * SIDE, (number * 2 + block + 1) * SIDE)
            zl[at, :] = lo[block]
            zh[at, :] = hi[block]
        at = slice(ZH_TBL + number * 8, ZH_TBL + number * 8 + 8)
        zl[at, :] = ref[base + FACE_TBL : base + FACE_ROWS, :]
        zh[at, :] = ref[base + FACE_TBL : base + FACE_ROWS, :]
    group = lane_of(64) & 31
    lo = jnp.zeros((64, LANES), jnp.float32)
    hi = lo
    for number, (sx, sy) in enumerate(CORNERS):
        ref, base = where[(-sx, -sy)]
        v = ref[base : base + EDGE_TBL, :]
        lo = jnp.where((group >= 8 * number) & (group < 8 * number + 8), roll(v, 8 * number), lo)
        hi = jnp.where((group <= 31 - 8 * number) & (group > 23 - 8 * number), roll(v, -8 * number), hi)
    zl[ZH_EDGE : ZH_EDGE + 64, :] = lo
    zh[ZH_EDGE : ZH_EDGE + 64, :] = hi


def step_kernel(
    pieces,
    sp,
    wd,
    pd,
    own,
    zup,
    zdn,
    zhup,
    zhdn,
    *rest,
):
    n_in = len(pieces)
    sources = (own, pd, zup, zdn, *rest[:n_in], zhup, zhdn)
    diffusivity, rate_const, opened, give_slot = rest[n_in : n_in + 4]
    keep, send = rest[n_in + 4 : n_in + 6]
    ua, ub, dn, fd, se_cube, we_cube, mx, myp, mym, sems = rest[n_in + 6 : n_in + 16]
    held = rest[n_in + 16 :]
    early = [pltpu.make_async_copy(src, dst, sems.at[i]) for i, (src, dst) in enumerate(zip(sources, held))]
    for c in early:
        c.start()
    core_at = (pl.ds(1, SIDE), pl.ds(4, YQ))
    late = [
        pltpu.make_async_copy(sp.at[k], se_cube.at[(k, slice(None), *core_at)], sems.at[len(early) + k])
        for k in range(PAIRS)
    ]
    late.append(pltpu.make_async_copy(wd, we_cube.at[(slice(None), *core_at)], sems.at[len(early) + PAIRS]))
    for c in late:
        c.start()
    for c in early:
        c.wait()
    own, pd, zup, zdn = held[:4]
    arrived, (zhup, zhdn) = held[4:-2], held[-2:]
    se = se_cube.reshape(PAIRS, QUADS, NEAR * SPAN, LANES)
    we = we_cube.reshape(QUADS, NEAR * SPAN, LANES)
    where = {name: (arrived[k], base) for k, held in enumerate(pieces) for name, base in held}

    lane = lane_of(8)
    lane32, lane64 = lane & 31, lane & 63
    low = lane < 64
    core = (lane64 >= 16) & (lane64 < 48)
    upper = lane64 >= 48

    table = {(0, 0): own[...]}
    ztable = {1: {(0, 0): zup[ZC_TBL:, :]}, -1: {(0, 0): zdn[ZC_TBL:, :]}}
    for number, (sx, sy) in enumerate(SIDES):
        ref, base = where[(-sx, -sy)]
        table[(sx, sy)] = ref[base + FACE_TBL : base + FACE_ROWS, :]
        for sz, held in ((1, zhup), (-1, zhdn)):
            ztable[sz][(sx, sy)] = held[ZH_TBL + number * 8 : ZH_TBL + number * 8 + 8, :]
    for sx, sy in CORNERS:
        ref, base = where[(-sx, -sy)]
        table[(sx, sy)] = ref[base + EDGE_TBL : base + EDGE_ROWS, :]

    def sign(held, way):
        return jnp.broadcast_to(held[way : way + 1, :], (8, LANES))

    def crossing(way, here, there):
        level = sign(table[here], way)
        beyond = {}
        for sz in (1, -1):
            z = z_way(sz)
            beyond[sz] = sign(ztable[sz][here], way) * sign(table[here], z) * sign(table[there], z)
        m = jnp.where(core, level, jnp.where(upper, beyond[1], beyond[-1]))
        return jnp.where(low, 1.0, m)

    row8 = lax.broadcasted_iota(jnp.int32, (8, LANES), 0)
    one = jnp.ones((8, LANES), jnp.float32)
    for number, sx in enumerate((-1, 1)):
        m = {sy: crossing(x_way(sx), (0, sy), (sx, sy)) for sy in (-1, 0, 1)}
        mx[number, 0:8, :] = jnp.where(row8 < 4, m[-1], m[0])
        mx[number, 8:16, :] = jnp.where(row8 < 4, m[0], m[1])
    y_sign = {}
    for number, sx in enumerate((-1, 0, 1)):
        m = {sy: crossing(y_way(sy), (sx, 0), (sx, sy)) for sy in (-1, 1)}
        y_sign[sx] = m
        myp[number, 0:8, :] = jnp.where(row8 == 3, m[-1], one)
        myp[number, 8:16, :] = jnp.where(row8 == 3, m[1], one)
        mym[number, 0:8, :] = jnp.where(row8 == 4, m[-1], one)
        mym[number, 8:16, :] = jnp.where(row8 == 4, m[1], one)

    outer = {}
    for key, held in table.items():
        m = jnp.where(upper, sign(held, 4), sign(held, 5))
        outer[key] = jnp.where(low, 1.0, m)

    def spread(v, zu, zd, shift_u, shift_d, key):
        rows = v.shape[0]
        tall = lambda a: a if rows == 8 else jnp.concatenate([a] * (rows // 8), axis=0)
        if zu is None:
            return roll(v, 16), roll(v, -16)
        m, c, u = tall(outer[key]), tall(core), tall(upper)
        pot = jnp.where(u, roll(zu, 48 + shift_u), roll(zd, -16 + shift_d)) * m
        rho = jnp.where(u, roll(zu, 16 + shift_u), roll(zd, -48 + shift_d)) * m
        return jnp.where(c, roll(v, 16), pot), jnp.where(c, roll(v, -16), rho)

    for half in range(2):

        def fill(i, carry, half=half):
            x = i + half * HALF
            at = pl.ds(pl.multiple_of(x * 8, 8), 8)
            to = pl.ds(pl.multiple_of(PAD + (x + DEPTH) * SPAN + 4, 4), 8)
            for j in range(QUADS):
                zat = pl.ds(pl.multiple_of(j * (PLANE // 2) + i * 8, 8), 8)
                shift_u, shift_d = (0, 16) if half == 0 else (-16, 0)
                pot, rho = spread(pd[j, at, :], zup[zat, :], zdn[zat, :], shift_u, shift_d, (0, 0))
                ua[j, to, :] = pot
                dn[j, to, :] = rho
            return carry

        lax.fori_loop(0, HALF, fill, 0)

    def turned(v, way):
        s = own[way : way + 1, :]
        return jnp.where(jnp.broadcast_to(s, v.shape) > 0, v, roll(v, 64))

    for number, (sx, sy) in enumerate(SIDES):
        ref, base = where[(-sx, -sy)]
        for l in range(DEPTH):
            v = ref[base + l * SIDE : base + (l + 1) * SIDE, :]
            zu = zd = None
            off = 0
            if l < 8:
                block, off = ZH_PLACE[l]
                at = slice((number * 2 + block) * SIDE, (number * 2 + block + 1) * SIDE)
                zu, zd = zhup[at, :], zhdn[at, :]
            pot, rho = spread(v, zu, zd, -off, off, (sx, sy))
            if sx:
                x = SIDE + l if sx > 0 else -1 - l
                start = PAD + (x + DEPTH) * SPAN + 4
                for j in range(QUADS):
                    ua[j, start : start + 8, :] = pot[j * 8 : j * 8 + 8]
                    dn[j, start : start + 8, :] = rho[j * 8 : j * 8 + 8]
            else:
                j = l % 4 if sy > 0 else 3 - l % 4
                row = 12 + l // 4 if sy > 0 else 3 - l // 4
                at = pl.ds(PAD + DEPTH * SPAN + row, SIDE, stride=SPAN)
                ua[j, at, :] = pot
                dn[j, at, :] = rho
        way = x_way(sx) if sx else y_way(sy)
        for k in range(PAIRS + 1):
            start = base + FACE_SP + k * SIDE
            v = turned(ref[start : start + SIDE, :], way)
            if sx:
                begin = (SIDE + 1 if sx > 0 else 0) * SPAN + 4
                for j in range(QUADS):
                    if k < PAIRS:
                        se[k, j, begin : begin + 8, :] = v[j * 8 : j * 8 + 8]
                    else:
                        we[j, begin : begin + 8, :] = v[j * 8 : j * 8 + 8]
            else:
                j, row = (0, 12) if sy > 0 else (3, 3)
                at = pl.ds(SPAN + row, SIDE, stride=SPAN)
                if k < PAIRS:
                    se[k, j, at, :] = v
                else:
                    we[j, at, :] = v
    for number, (sx, sy) in enumerate(CORNERS):
        ref, base = where[(-sx, -sy)]
        for m in range(8):
            v = ref[base + m * 8 : base + m * 8 + 8, :]
            at = slice(ZH_EDGE + m * 8, ZH_EDGE + m * 8 + 8)
            pot, rho = spread(v, zhup[at, :], zhdn[at, :], -8 * number, 8 * number, (sx, sy))
            row = (12 if sy > 0 else 2) + m // 4
            x = SIDE if sx > 0 else -8
            to = pl.ds(PAD + (x + DEPTH) * SPAN + row, 8, stride=SPAN)
            ua[m % 4, to, :] = pot
            dn[m % 4, to, :] = rho

    scale = 1.0 / (6.0 + screening)

    def slab(src, dst, x, sx, before=None, after=None):
        r = pl.multiple_of(PAD + (x + DEPTH) * SPAN, 8)
        at = pl.ds(r, SPAN)
        c = [src[j, at, :] for j in range(QUADS)]
        for j in range(QUADS):
            left = src[j, pl.ds(r - SPAN, SPAN), :]
            right = src[j, pl.ds(r + SPAN, SPAN), :]
            if before is not None:
                left = left * mx[before]
            if after is not None:
                right = right * mx[after]
            north = c[j + 1] if j < 3 else src[0, pl.ds(r + 1, SPAN), :] * myp[sx + 1]
            south = c[j - 1] if j > 0 else src[3, pl.ds(r - 1, SPAN), :] * mym[sx + 1]
            total = (left + right) + (north + south) + (roll(c[j], 1) + roll(c[j], -1)) + dn[j, at, :]
            dst[j, at, :] = total * scale

    def sweep(src, dst, t):
        def middle(i, carry):
            for n in range(MIDDLE):
                slab(src, dst, 1 + i * MIDDLE + n, 0)
            return carry

        def fringe(i, carry):
            for n in range(2):
                slab(src, dst, -2 - 2 * i - n, -1)
                slab(src, dst, SIDE + 1 + 2 * i + n, 1)
            return carry

        lax.fori_loop(0, (SIDE - 2) // MIDDLE, middle, 0)
        slab(src, dst, -1, -1, after=0)
        slab(src, dst, 0, 0, before=0)
        slab(src, dst, SIDE - 1, 0, after=1)
        slab(src, dst, SIDE, 1, before=1)
        lax.fori_loop(0, (SWEEPS + 1 - t) // 2, fringe, 0)

    def two_sweeps(i, carry):
        sweep(ua, ub, 2 * i + 1)
        sweep(ub, ua, 2 * i + 2)
        return carry

    lax.fori_loop(0, SWEEPS // 2, two_sweeps, 0)

    lane16 = lane_of(SPAN)
    first = (lane16 & 32) == 0
    row16 = lax.broadcasted_iota(jnp.int32, (SPAN, LANES), 0)

    def slots(x, m):
        r = pl.multiple_of(PAD + (x + DEPTH) * SPAN, 8)
        near = pl.ds(pl.multiple_of((x + 1) * SPAN, 8), SPAN)
        for j in range(QUADS):
            c = ua[j, pl.ds(r, SPAN), :] * m
            t = roll(c, 64)
            u = 0.5 * jnp.where(lane16 < 64, c + t, t - c)
            ub[j, pl.ds(r, SPAN), :] = u
            fd[j, near, :] = jnp.where(first, roll(u, -16), roll(u, 16))

    tall = lambda a: jnp.concatenate([a, a], axis=0)
    beside = jnp.where(row16 >= 12, tall(y_sign[0][1]), jnp.where(row16 < 4, tall(y_sign[0][-1]), 1.0))
    slots(-1, mx[0])
    slots(SIDE, mx[1])
    def all_slots(i, carry):
        for n in range(4):
            slots(4 * i + n, beside)
        return carry

    lax.fori_loop(0, SIDE // 4, all_slots, 0)

    for c in late:
        c.wait()
    even = (lane & 32) == 0

    def by_ion(values, k):
        return jnp.where(even, values[k], values[k + PAIRS])

    half_charge = [by_ion([0.5 * v for v in valences], k) for k in range(PAIRS)]
    rates = [by_ion([diffusivity[i] for i in range(6)], k) for k in range(PAIRS)]
    signs = [by_ion(reaction_signs, k) for k in range(PAIRS)]
    reactivity = [rate_const[b] * opened[b].astype(jnp.float32) for b in range(2)]
    reactivity = jnp.where(low, reactivity[0], reactivity[1])
    given = give_slot[0]
    up_turned = jnp.broadcast_to(own[4:5, :], (8, LANES)) > 0
    down_turned = jnp.broadcast_to(own[5:6, :], (8, LANES)) > 0
    top, bottom = lane32 == 31, lane32 == 0

    for half in range(2):

        def update(i, carry, half=half):
            x = i + half * HALF
            r = pl.multiple_of(PAD + (x + DEPTH) * SPAN, 8)
            q = pl.multiple_of((x + 1) * SPAN, 8)
            here, left, right = pl.ds(q + 4, 8), pl.ds(q + 4 - SPAN, 8), pl.ds(q + 4 + SPAN, 8)
            north_at, south_at = pl.ds(q + 5, 8), pl.ds(q + 3, 8)
            done = [[None] * QUADS for _ in range(PAIRS + 1)]
            for j in range(QUADS):
                zat = pl.ds(pl.multiple_of(j * (PLANE // 2) + i * 8, 8), 8)
                zu, zd = zup[zat, :], zdn[zat, :]
                zu = jnp.where(up_turned, zu, roll(zu, 64))
                zd = jnp.where(down_turned, zd, roll(zd, 64))

                def around(ref, lead, off):
                    c = ref[lead + (j, here)]
                    return c, (
                        ref[lead + (j, right)],
                        ref[lead + (j, left)],
                        ref[lead + (j + 1, here)] if j < 3 else ref[lead + (0, north_at)],
                        ref[lead + (j - 1, here)] if j > 0 else ref[lead + (3, south_at)],
                        jnp.where(top, roll(zu, 31 - off - 16 * half), roll(c, -1)),
                        jnp.where(bottom, roll(zd, off - 31 + 16 * (1 - half)), roll(c, 1)),
                    )

                w, near_w = around(we, (), 12)
                u = ub[j, pl.ds(r + 4, 8), :]
                phi = fd[j, here, :]
                near_phi = (
                    fd[j, right, :],
                    fd[j, left, :],
                    fd[j + 1, here, :] if j < 3 else fd[0, north_at, :],
                    fd[j - 1, here, :] if j > 0 else fd[3, south_at, :],
                    jnp.where(even, roll(u, -17), roll(u, 15)),
                    jnp.where(even, roll(u, -15), roll(u, 17)),
                )
                drift = [near_w[d] * (phi - near_phi[d]) for d in range(6)]
                w_total = functools.reduce(lambda a, b: a + b, near_w)
                d_total = functools.reduce(lambda a, b: a + b, drift)
                conc = []
                for k in range(PAIRS):
                    c, near_c = around(se, (k,), 9 + k)
                    spread_w = functools.reduce(lambda a, b: a + b, [near_w[d] * near_c[d] for d in range(6)])
                    spread_d = functools.reduce(lambda a, b: a + b, [drift[d] * near_c[d] for d in range(6)])
                    outflow = w * ((c * w_total - spread_w) + half_charge[k] * (c * d_total + spread_d))
                    conc.append(c)
                    done[k][j] = c - rates[k] * outflow
                reaction = conc[2] - conc[0] * conc[1] / solubility
                reaction = jnp.where(w > 0, reactivity * reaction, 0.0)
                for k in range(PAIRS):
                    done[k][j] = done[k][j] + signs[k] * reaction
                done[PAIRS][j] = phi
            at = pl.ds(pl.multiple_of(x * 8, 8), 8)
            for k in range(PAIRS + 1):
                native = swap_groups(done[k], lane)
                for f in range(2 if k < PAIRS else 1):
                    ion = k + f * PAIRS if k < PAIRS else 2 * PAIRS
                    send[ion, at, :] = jnp.where(given == 0, native[f], native[2 + f])
                    keep[ion, at, :] = jnp.where(given == 0, native[2 + f], native[f])
            return carry

        lax.fori_loop(0, HALF, update, 0)


def place_kernel(give_slot, keep, received, new_sp, new_pot):
    given = give_slot[0]
    theirs, ours = pl.ds(given, PLANE, stride=2), pl.ds(1 - given, PLANE, stride=2)
    ions = new_sp.shape[0]
    for i in range(ions):
        new_sp[i, theirs, :] = received[i]
        new_sp[i, ours, :] = keep[i]
    new_pot[theirs, :] = received[ions]
    new_pot[ours, :] = keep[ions]


VMEM = pl.BlockSpec(memory_space=pltpu.VMEM)
SMEM = pl.BlockSpec(memory_space=pltpu.SMEM)
ANY = pl.BlockSpec(memory_space=pl.ANY)
HBM = pl.BlockSpec(memory_space=pltpu.HBM)
MIB = 1024 * 1024


def grant(mib):
    return pltpu.CompilerParams(vmem_limit_bytes=mib * MIB)


def f32(*shape):
    return jax.ShapeDtypeStruct(shape, jnp.float32)


def rows_of(field):
    lead = field.shape[:-2]
    bricks, cells = field.shape[-2:]
    split = field.reshape(lead + (bricks, cells // LANES, LANES))
    return jnp.swapaxes(split, -3, -2).reshape(lead + (bricks * cells // LANES, LANES))


def cells_of(rows):
    lead = rows.shape[:-2]
    count, lanes = rows.shape[-2:]
    split = rows.reshape(lead + (count // 2, 2, lanes))
    return jnp.swapaxes(split, -3, -2).reshape(lead + (2, count // 2 * lanes))


def moved(block, axis, offset):
    n = lax.axis_size(axis)
    return lax.ppermute(block, axis, [(i, (i + offset) % n) for i in range(n)])


def local(
    species,
    potential,
    pore,
    openness,
    neighbours,
    diffusivity,
    rate_const,
    opened,
    partner,
    give_slot,
):
    ion_count, brick_count, cells = species.shape
    dev_count = lax.axis_size("dev")
    stride = dev_count // 4

    held = {}
    for sx, sy in SIDES + CORNERS:
        offset = (sx + sy * stride) % dev_count
        offset = offset if offset <= dev_count // 2 else offset - dev_count
        rows, pieces = held.get(offset, (0, ()))
        held[offset] = (rows + (FACE_ROWS if 0 in (sx, sy) else EDGE_ROWS), pieces + (((sx, sy), rows),))
    offsets = sorted(held, key=lambda o: (-held[o][0], -abs(o), o))
    pieces = tuple(held[o][1] for o in offsets)

    with_face = [k for k, o in enumerate(offsets) if held[o][0] >= FACE_ROWS]
    alone = [k for k in range(len(offsets)) if k not in with_face]
    rows = brick_count * PLANE
    packed = pl.pallas_call(
        functools.partial(pack_kernel, tuple(pieces[k] for k in with_face)),
        out_shape=(
            f32(PAIRS, QUADS, PLANE, LANES),
            f32(QUADS, PLANE, LANES),
            f32(QUADS, PLANE, LANES),
            f32(8, LANES),
            *(f32(held[offsets[k]][0], LANES) for k in with_face),
            f32(ZC_ROWS, LANES),
            f32(ZC_ROWS, LANES),
        ),
        in_specs=[HBM] * 4 + [SMEM],
        out_specs=tuple([VMEM] * (6 + len(with_face))),
        scratch_shapes=[
            pltpu.VMEM((ion_count, rows, LANES), jnp.float32),
            pltpu.VMEM((rows, LANES), jnp.float32),
            pltpu.VMEM((rows, LANES), jnp.int32),
            pltpu.VMEM((rows, LANES), jnp.float32),
            pltpu.SemaphoreType.DMA((PARTS, 2, 4)),
        ],
        compiler_params=grant(60),
        name="pack",
    )(rows_of(species), rows_of(potential), rows_of(pore), rows_of(openness), neighbours)
    sp, wd, pd, own = packed[:4]
    blocks = dict(zip(with_face, packed[4:-2]))
    if alone:
        corners = pl.pallas_call(
            functools.partial(corner_kernel, tuple(pieces[k] for k in alone)),
            out_shape=tuple(f32(held[offsets[k]][0], LANES) for k in alone),
            in_specs=[VMEM, VMEM],
            out_specs=tuple([VMEM] * len(alone)),
            compiler_params=grant(4),
            name="corners",
        )(pd, own)
        blocks.update(zip(alone, corners))
    arrived = [moved(blocks[k], "dev", o) for k, o in enumerate(offsets)]
    zup = moved(packed[-2], "group", -1)
    zdn = moved(packed[-1], "group", 1)

    zl, zh = pl.pallas_call(
        functools.partial(relay_kernel, pieces),
        out_shape=(f32(ZH_ROWS, LANES),) * 2,
        in_specs=[VMEM] * len(offsets) + [ANY] * 2,
        out_specs=(VMEM, VMEM),
        compiler_params=grant(6),
        name="relay",
    )(*arrived, zup, zdn)
    zhup = moved(zl, "group", -1)
    zhdn = moved(zh, "group", 1)

    wide = pltpu.VMEM((QUADS, EXT * SPAN + 2 * PAD, LANES), jnp.float32)
    near = pltpu.VMEM((QUADS, NEAR * SPAN, LANES), jnp.float32)
    by_layer = lambda a: a.reshape(a.shape[:-2] + (SIDE, YQ, LANES))
    sources = (own, pd, zup, zdn, *arrived, zhup, zhdn)
    kept, outgoing = pl.pallas_call(
        functools.partial(step_kernel, pieces),
        out_shape=(f32(ion_count + 1, PLANE, LANES),) * 2,
        in_specs=[HBM] * (8 + len(offsets)) + [SMEM] * 4,
        out_specs=(VMEM, VMEM),
        scratch_shapes=[
            wide,
            wide,
            wide,
            near,
            pltpu.VMEM((PAIRS, QUADS, NEAR, SPAN, LANES), jnp.float32),
            pltpu.VMEM((QUADS, NEAR, SPAN, LANES), jnp.float32),
            pltpu.VMEM((2, SPAN, LANES), jnp.float32),
            pltpu.VMEM((3, SPAN, LANES), jnp.float32),
            pltpu.VMEM((3, SPAN, LANES), jnp.float32),
            pltpu.SemaphoreType.DMA((len(sources) + PAIRS + 1,)),
            *(pltpu.VMEM(a.shape, jnp.float32) for a in sources),
        ],
        compiler_params=grant(60),
        name="step",
    )(by_layer(sp), by_layer(wd), pd, own, zup, zdn, zhup, zhdn, *arrived, diffusivity, rate_const, opened, give_slot)

    def placed(received):
        new_sp, new_pot = pl.pallas_call(
            place_kernel,
            out_shape=(f32(ion_count, rows, LANES), f32(rows, LANES)),
            in_specs=[SMEM, VMEM, VMEM],
            out_specs=(VMEM, VMEM),
            compiler_params=grant(8),
            name="place",
        )(give_slot, kept, received)
        return cells_of(new_sp), cells_of(new_pot)

    axes = ("group", "dev")
    total = lax.axis_size("group") * dev_count
    own_index = lax.axis_index("group") * dev_count + lax.axis_index("dev")
    apart = jnp.bitwise_xor(own_index, partner[0])
    branch = jnp.int32(0)
    branches = [lambda block: placed(block)]
    for bit in range(total.bit_length() - 1):
        route = [(i, i ^ (1 << bit)) for i in range(total)]
        branch = jnp.where(apart == (1 << bit), bit + 1, branch)
        branches.append(lambda block, route=route: placed(lax.ppermute(block, axes, route)))
    return lax.switch(branch, branches, outgoing)


def solution(mesh):
    in_specs = (
        P(None, ("group", "dev"), None),
        P(("group", "dev"), None),
        P(("group", "dev"), None),
        P(("group", "dev"), None),
        P(("group", "dev"), None),
        P(),
        P(("group", "dev")),
        P(("group", "dev")),
        P(("group", "dev")),
        P(("group", "dev")),
    )
    out_specs = (P(None, ("group", "dev"), None), P(("group", "dev"), None))
    return jax.shard_map(local, mesh=mesh, in_specs=in_specs, out_specs=out_specs, check_vma=False)
```

```python
import functools

import jax
import jax.numpy as jnp
from jax import lax
from jax.experimental import pallas as pl
from jax.experimental.pallas import tpu as pltpu
from jax.sharding import PartitionSpec as P


SWEEPS = 8
DEPTH = SWEEPS + 1
LANES = 128

charge_scale = 0.5
screening = 0.5
solubility = 2.0
valences = (2.0, -1.0, 1.0, -1.0, 1.0, 2.0)
reaction_signs = (1.0, 1.0, -1.0, 0.0, 0.0, 0.0)

SIDE = 32
QUADS = 4
YQ = SIDE // QUADS
PAIRS = 3
PLANE = SIDE * YQ
HALF = SIDE // 2

FACE_TBL = DEPTH * SIDE
Y_ROWS = FACE_TBL + 8
EDGE_TBL = 64
EDGE_ROWS = EDGE_TBL + 8
THIRD = 11
ZC_TBL = QUADS * THIRD * YQ
ZC_ROWS = ZC_TBL + 8
ZH_EDGE = 2 * 3 * SIDE
ZH_TBL = ZH_EDGE + 64
ZH_ROWS = ZH_TBL + 32
FIELDS = PAIRS + 1
ION_ROWS = FIELDS * SIDE
X_ROWS = Y_ROWS + ION_ROWS
BLOCKS = SIDE // FIELDS

ZH_PLACE = {
    (n, l): (n, off) if l < 5 else (2, 6 * n + off)
    for n in range(2)
    for l, off in enumerate((0, 8, 15, 21, 26, 0, 3, 5))
}

SIDES = ((-1, 0), (1, 0), (0, -1), (0, 1))
CORNERS = ((-1, -1), (-1, 1), (1, -1), (1, 1))
SPAN = 16
EXT = SIDE + 2 * DEPTH
MIDDLE = 10
PARTS = 3
PART = 4
NEAR = SIDE + 2
PAD = 24


def x_way(s):
    return 0 if s > 0 else 1


def y_way(s):
    return 2 if s > 0 else 3


def z_way(s):
    return 4 if s > 0 else 5


def roll(v, shift):
    shift = shift % LANES
    return v if shift == 0 else pltpu.roll(v, shift, 1)


def lane_of(rows):
    return lax.broadcasted_iota(jnp.int32, (rows, LANES), 1)


def swap_groups(v, lane):
    low = lane < 64
    a0 = jnp.where(low, v[0], roll(v[2], 64))
    a2 = jnp.where(low, roll(v[0], 64), v[2])
    a1 = jnp.where(low, v[1], roll(v[3], 64))
    a3 = jnp.where(low, roll(v[1], 64), v[3])
    even = (lane & 32) == 0
    return (
        jnp.where(even, a0, roll(a1, 32)),
        jnp.where(even, roll(a0, 96), a1),
        jnp.where(even, a2, roll(a3, 32)),
        jnp.where(even, roll(a2, 96), a3),
    )


def sign_rows(neighbours):
    row = lax.broadcasted_iota(jnp.int32, (8, LANES), 0)
    table = jnp.zeros((8, LANES), jnp.float32)
    for way in range(6):
        table = jnp.where(row == way, jnp.where(neighbours[0, way] == 0, 1.0, -1.0), table)
    return table


def pack_kernel(pieces, species_in, potential_in, pore_in, openness_in, neighbours, pd, own, *rest):
    n_out = len(pieces)
    outs, (zlo, zhi) = rest[:n_out], rest[n_out : n_out + 2]
    species, potential, pore, openness, sems = rest[n_out + 2 :]
    parts = []
    for part in range(PARTS):
        copies = []
        for c in range(3):
            x0 = c * THIRD + part * PART
            count = min(PART, (c + 1) * THIRD - x0, SIDE - x0)
            rows = pl.ds(x0 * 16, count * 16)
            for number, (src, dst) in enumerate(
                ((species_in, species), (potential_in, potential), (pore_in, pore), (openness_in, openness))
            ):
                at = (slice(None), rows) if number == 0 else (rows,)
                copies.append(pltpu.make_async_copy(src.at[at], dst.at[at], sems.at[part, c, number]))
                copies[-1].start()
        parts.append(copies)
    where = {name: (outs[k], base) for k, held in enumerate(pieces) for name, base in held}
    lane = lane_of(8)
    lane32 = lane & 31
    low = lane < 64
    table = sign_rows(neighbours)
    own[...] = table

    def planes_of(x):
        d, p = [], []
        for b in range(2):
            rows = pl.ds(x * 16 + b, 8, stride=2)
            total = valences[0] * species[0, rows, :]
            for i in range(1, 2 * PAIRS):
                total = total + valences[i] * species[i, rows, :]
            wet = pore[rows, :].astype(jnp.float32) * openness[rows, :]
            d.append(charge_scale * wet * total)
            p.append(potential[rows, :])
        mixed = []
        for v in swap_groups((p[0], d[0], p[1], d[1]), lane):
            r = roll(v, 64)
            mixed.append(jnp.where(low, v + r, r - v))
        at = pl.ds(pl.multiple_of(x * 8, 8), 8)
        for j in range(QUADS):
            pd[j, at, :] = mixed[j]
        return mixed

    def step(i, blocks=3):
        planes = [planes_of(i + c * THIRD) for c in range(blocks)]
        for j in range(QUADS):
            at = pl.ds(pl.multiple_of((j * THIRD + i) * 8, 8), 8)
            lo = hi = planes[0][j]
            for c in range(1, blocks):
                lo = jnp.where(lane32 >= DEPTH * c, roll(planes[c][j], DEPTH * c), lo)
                hi = jnp.where(lane32 < SIDE - DEPTH * c, roll(planes[c][j], -DEPTH * c), hi)
            zlo[at, :] = lo
            zhi[at, :] = hi

    for part in range(PARTS):
        for c in parts[part]:
            c.wait()
        end = min((part + 1) * PART, THIRD - 1)
        lax.fori_loop(part * PART, end, lambda i, carry: (step(i), carry)[1], 0)
    step(THIRD - 1, 2)

    zlo[ZC_TBL:, :] = table
    zhi[ZC_TBL:, :] = table

    def ion_planes(x, ref, start):
        for k, planes in enumerate(dense_ions(species, pore, openness, x, lane)):
            for j in range(QUADS):
                ref[start + k * SIDE + j * 8 : start + k * SIDE + j * 8 + 8, :] = planes[j]

    for sx, sy in SIDES:
        ref, base = where[(sx, sy)]
        for l in range(DEPTH):
            if sx:
                x = l if sx < 0 else SIDE - 1 - l
                for j in range(QUADS):
                    ref[base + l * SIDE + j * 8 : base + l * SIDE + j * 8 + 8, :] = pd[j, x * 8 : x * 8 + 8, :]
            else:
                y = l if sy < 0 else SIDE - 1 - l
                ref[base + l * SIDE : base + (l + 1) * SIDE, :] = pd[y % 4, pl.ds(y // 4, SIDE, stride=8), :]
        ref[base + FACE_TBL : base + Y_ROWS, :] = table
        if sx:
            ion_planes(0 if sx < 0 else SIDE - 1, ref, base + Y_ROWS)
    for sx, sy in CORNERS:
        ref, base = where[(sx, sy)]
        x0 = 0 if sx < 0 else SIDE - 8
        for m in range(8):
            y = m if sy < 0 else SIDE - 8 + m
            ref[base + m * 8 : base + m * 8 + 8, :] = pd[y % 4, pl.ds(x0 * 8 + y // 4, 8, stride=8), :]
        ref[base + EDGE_TBL : base + EDGE_ROWS, :] = table


def dense_ions(species, pore, openness, x, lane):
    rows = [pl.ds(x * 16 + b, 8, stride=2) for b in range(2)]
    w = [pore[rows[b], :].astype(jnp.float32) * openness[rows[b], :] for b in range(2)]
    s = [[species[n, rows[b], :] for b in range(2)] for n in range(2 * PAIRS)]
    fields = [swap_groups((s[k][0], s[k + PAIRS][0], s[k][1], s[k + PAIRS][1]), lane) for k in range(PAIRS)]
    return fields + [swap_groups((w[0], w[0], w[1], w[1]), lane)]


def ions_kernel(species_in, pore_in, openness_in, sp, wd, ylo, yhi, species, pore, openness, sems):
    parts = []
    for part in range(2):
        rows = pl.ds(part * PLANE, PLANE)
        copies = [
            pltpu.make_async_copy(species_in.at[:, rows], species.at[:, rows], sems.at[part, 0]),
            pltpu.make_async_copy(pore_in.at[rows], pore.at[rows], sems.at[part, 1]),
            pltpu.make_async_copy(openness_in.at[rows], openness.at[rows], sems.at[part, 2]),
        ]
        for c in copies:
            c.start()
        parts.append(copies)
    lane = lane_of(8)

    def step(x, carry):
        at = pl.ds(pl.multiple_of(x * 8, 8), 8)
        for k, planes in enumerate(dense_ions(species, pore, openness, x, lane)):
            for j in range(QUADS):
                if k < PAIRS:
                    sp[k, j, at, :] = planes[j]
                else:
                    wd[j, at, :] = planes[j]
        return carry

    for part in range(2):
        for c in parts[part]:
            c.wait()
        lax.fori_loop(part * HALF, (part + 1) * HALF, step, 0, unroll=2)
    for k in range(FIELDS):
        for y, ref in ((0, ylo), (SIDE - 1, yhi)):
            at = pl.ds(y // 4, SIDE, stride=8)
            ref[k * SIDE : (k + 1) * SIDE, :] = sp[k, y % 4, at, :] if k < PAIRS else wd[y % 4, at, :]


def ion_z_kernel(sp, wd, zlo, zhi):
    lane32 = lane_of(8) & 31

    def step(i, carry):
        for j in range(QUADS):
            lo = hi = jnp.zeros((8, LANES), jnp.float32)
            for spot in range(SIDE):
                block, k = spot // FIELDS, spot % FIELDS
                at = pl.ds(pl.multiple_of((i + block * FIELDS) * 8, 8), 8)
                v = sp[k, j, at, :] if k < PAIRS else wd[j, at, :]
                lo = jnp.where(lane32 == spot, roll(v, spot), lo)
                hi = jnp.where(lane32 == spot, roll(v, spot - 31), hi)
            zat = pl.ds(pl.multiple_of(j * SIDE + i * 8, 8), 8)
            zlo[zat, :] = lo
            zhi[zat, :] = hi
        return carry

    lax.fori_loop(0, FIELDS, step, 0)


def relay_kernel(pieces, *refs):
    arrived, (zl, zh) = refs[:-2], refs[-2:]
    where = {name: (arrived[k], base) for k, held in enumerate(pieces) for name, base in held}
    lane32 = lane_of(SIDE) & 31
    for axis in range(2):
        lo = [jnp.zeros((SIDE, LANES), jnp.float32)] * 3
        hi = [jnp.zeros((SIDE, LANES), jnp.float32)] * 3
        for n in range(2):
            sx, sy = SIDES[2 * axis + n]
            ref, base = where[(-sx, -sy)]
            for l in range(8):
                block, off = ZH_PLACE[n, l]
                width = 8 - l
                v = ref[base + l * SIDE : base + (l + 1) * SIDE, :]
                lo[block] = jnp.where((lane32 >= off) & (lane32 < off + width), roll(v, off), lo[block])
                hi[block] = jnp.where((lane32 <= 31 - off) & (lane32 > 31 - off - width), roll(v, -off), hi[block])
            at = slice(ZH_TBL + (2 * axis + n) * 8, ZH_TBL + (2 * axis + n) * 8 + 8)
            zl[at, :] = ref[base + FACE_TBL : base + Y_ROWS, :]
            zh[at, :] = ref[base + FACE_TBL : base + Y_ROWS, :]
        for block in range(3):
            at = slice((axis * 3 + block) * SIDE, (axis * 3 + block + 1) * SIDE)
            zl[at, :] = lo[block]
            zh[at, :] = hi[block]
    group = lane_of(64) & 31
    lo = jnp.zeros((64, LANES), jnp.float32)
    hi = lo
    for number, (sx, sy) in enumerate(CORNERS):
        ref, base = where[(-sx, -sy)]
        v = ref[base : base + EDGE_TBL, :]
        lo = jnp.where((group >= 8 * number) & (group < 8 * number + 8), roll(v, 8 * number), lo)
        hi = jnp.where((group <= 31 - 8 * number) & (group > 23 - 8 * number), roll(v, -8 * number), hi)
    zl[ZH_EDGE : ZH_EDGE + 64, :] = lo
    zh[ZH_EDGE : ZH_EDGE + 64, :] = hi


def sweep_kernel(pieces, *refs):
    n_in = 10 + len(pieces)
    sources, (sp, wd), scalars = refs[:n_in], refs[n_in : n_in + 2], refs[n_in + 2 : n_in + 6]
    ud, fd, keep, send = refs[n_in + 6 : n_in + 10]
    ua, ub, dn, mx, myp, mym, se_cube, we_cube, zw, udv, fdv, sems, ion_sems, out_sems = refs[n_in + 10 : n_in + 24]
    held = refs[n_in + 24 :]
    copies = [pltpu.make_async_copy(src, dst, sems.at[i]) for i, (src, dst) in enumerate(zip(sources, held))]
    for c in copies:
        c.start()
    late = ion_copies(0, sp, wd, se_cube, we_cube, ion_sems)
    for c in late:
        c.start()
    own, pd, zup, zdn, zhup, zhdn = held[:6]
    yz_halos, arrived = held[6:10], held[10:]
    where = {name: (arrived[k], base) for k, held in enumerate(pieces) for name, base in held}

    lane = lane_of(8)
    lane64 = lane & 63
    low = lane < 64
    core = (lane64 >= 16) & (lane64 < 48)
    upper = lane64 >= 48

    for c in copies:
        c.wait()
    table = {(0, 0): own[...]}
    ztable = {1: {(0, 0): zup[ZC_TBL:, :]}, -1: {(0, 0): zdn[ZC_TBL:, :]}}
    for number, (sx, sy) in enumerate(SIDES):
        ref, base = where[(-sx, -sy)]
        table[(sx, sy)] = ref[base + FACE_TBL : base + Y_ROWS, :]
        for sz, held in ((1, zhup), (-1, zhdn)):
            ztable[sz][(sx, sy)] = held[ZH_TBL + number * 8 : ZH_TBL + number * 8 + 8, :]
    for sx, sy in CORNERS:
        ref, base = where[(-sx, -sy)]
        table[(sx, sy)] = ref[base + EDGE_TBL : base + EDGE_ROWS, :]

    def sign(held, way):
        return jnp.broadcast_to(held[way : way + 1, :], (8, LANES))

    def crossing(way, here, there):
        level = sign(table[here], way)
        beyond = {}
        for sz in (1, -1):
            z = z_way(sz)
            beyond[sz] = sign(ztable[sz][here], way) * sign(table[here], z) * sign(table[there], z)
        m = jnp.where(core, level, jnp.where(upper, beyond[1], beyond[-1]))
        return jnp.where(low, 1.0, m)

    row8 = lax.broadcasted_iota(jnp.int32, (8, LANES), 0)
    one = jnp.ones((8, LANES), jnp.float32)
    for number, sx in enumerate((-1, 1)):
        m = {sy: crossing(x_way(sx), (0, sy), (sx, sy)) for sy in (-1, 0, 1)}
        mx[number, 0:8, :] = jnp.where(row8 < 4, m[-1], m[0])
        mx[number, 8:16, :] = jnp.where(row8 < 4, m[0], m[1])
    y_sign = {}
    for number, sx in enumerate((-1, 0, 1)):
        m = {sy: crossing(y_way(sy), (sx, 0), (sx, sy)) for sy in (-1, 1)}
        y_sign[sx] = m
        myp[number, 0:8, :] = jnp.where(row8 == 3, m[-1], one)
        myp[number, 8:16, :] = jnp.where(row8 == 3, m[1], one)
        mym[number, 0:8, :] = jnp.where(row8 == 4, m[-1], one)
        mym[number, 8:16, :] = jnp.where(row8 == 4, m[1], one)

    outer = {}
    for key, held in table.items():
        m = jnp.where(upper, sign(held, 4), sign(held, 5))
        outer[key] = jnp.where(low, 1.0, m)

    def spread(v, zu, zd, shift_u, shift_d, key):
        rows = v.shape[0]
        tall = lambda a: a if rows == 8 else jnp.concatenate([a] * (rows // 8), axis=0)
        if zu is None:
            return roll(v, 16), roll(v, -16)
        m, c, u = tall(outer[key]), tall(core), tall(upper)
        pot = jnp.where(u, roll(zu, 48 + shift_u), roll(zd, -16 + shift_d)) * m
        rho = jnp.where(u, roll(zu, 16 + shift_u), roll(zd, -48 + shift_d)) * m
        return jnp.where(c, roll(v, 16), pot), jnp.where(c, roll(v, -16), rho)

    def fill(i, c):
        x = i + c * THIRD
        at = pl.ds(pl.multiple_of(x * 8, 8), 8)
        to = pl.ds(pl.multiple_of(PAD + (x + DEPTH) * SPAN + 4, 4), 8)
        for j in range(QUADS):
            zat = pl.ds(pl.multiple_of((j * THIRD + i) * 8, 8), 8)
            pot, rho = spread(pd[j, at, :], zup[zat, :], zdn[zat, :], -DEPTH * c, DEPTH * c, (0, 0))
            ua[j, to, :] = pot
            dn[j, to, :] = rho

    def fill_three(i, carry):
        for c in range(3):
            fill(i, c)
        return carry

    lax.fori_loop(0, THIRD - 1, fill_three, 0)
    fill(THIRD - 1, 0)
    fill(THIRD - 1, 1)

    for number, (sx, sy) in enumerate(SIDES):
        ref, base = where[(-sx, -sy)]
        for l in range(DEPTH):
            v = ref[base + l * SIDE : base + (l + 1) * SIDE, :]
            zu = zd = None
            off = 0
            if l < 8:
                block, off = ZH_PLACE[number % 2, l]
                block += number // 2 * 3
                at = slice(block * SIDE, (block + 1) * SIDE)
                zu, zd = zhup[at, :], zhdn[at, :]
            pot, rho = spread(v, zu, zd, -off, off, (sx, sy))
            if sx:
                x = SIDE + l if sx > 0 else -1 - l
                start = PAD + (x + DEPTH) * SPAN + 4
                for j in range(QUADS):
                    ua[j, start : start + 8, :] = pot[j * 8 : j * 8 + 8]
                    dn[j, start : start + 8, :] = rho[j * 8 : j * 8 + 8]
            else:
                j = l % 4 if sy > 0 else 3 - l % 4
                row = 12 + l // 4 if sy > 0 else 3 - l // 4
                at = pl.ds(PAD + DEPTH * SPAN + row, SIDE, stride=SPAN)
                ua[j, at, :] = pot
                dn[j, at, :] = rho
    for number, (sx, sy) in enumerate(CORNERS):
        ref, base = where[(-sx, -sy)]
        for m in range(8):
            v = ref[base + m * 8 : base + m * 8 + 8, :]
            at = slice(ZH_EDGE + m * 8, ZH_EDGE + m * 8 + 8)
            pot, rho = spread(v, zhup[at, :], zhdn[at, :], -8 * number, 8 * number, (sx, sy))
            row = (12 if sy > 0 else 2) + m // 4
            x = SIDE if sx > 0 else -8
            to = pl.ds(PAD + (x + DEPTH) * SPAN + row, 8, stride=SPAN)
            ua[m % 4, to, :] = pot
            dn[m % 4, to, :] = rho

    scale = 1.0 / (6.0 + screening)

    def slab(src, dst, x, sx, before=None, after=None):
        r = pl.multiple_of(PAD + (x + DEPTH) * SPAN, 8)
        at = pl.ds(r, SPAN)
        c = [src[j, at, :] for j in range(QUADS)]
        for j in range(QUADS):
            left = src[j, pl.ds(r - SPAN, SPAN), :]
            right = src[j, pl.ds(r + SPAN, SPAN), :]
            if before is not None:
                left = left * mx[before]
            if after is not None:
                right = right * mx[after]
            north = c[j + 1] if j < 3 else src[0, pl.ds(r + 1, SPAN), :] * myp[sx + 1]
            south = c[j - 1] if j > 0 else src[3, pl.ds(r - 1, SPAN), :] * mym[sx + 1]
            total = (left + right) + (north + south) + (roll(c[j], 1) + roll(c[j], -1)) + dn[j, at, :]
            dst[j, at, :] = total * scale

    def sweep(src, dst, t):
        def middle(i, carry):
            for n in range(MIDDLE):
                slab(src, dst, 1 + i * MIDDLE + n, 0)
            return carry

        def fringe(i, carry):
            for n in range(2):
                slab(src, dst, -2 - 2 * i - n, -1)
                slab(src, dst, SIDE + 1 + 2 * i + n, 1)
            return carry

        lax.fori_loop(0, (SIDE - 2) // MIDDLE, middle, 0)
        slab(src, dst, -1, -1, after=0)
        slab(src, dst, 0, 0, before=0)
        slab(src, dst, SIDE - 1, 0, after=1)
        slab(src, dst, SIDE, 1, before=1)
        lax.fori_loop(0, (SWEEPS + 1 - t) // 2, fringe, 0)

    def two_sweeps(i, carry):
        sweep(ua, ub, 2 * i + 1)
        sweep(ub, ua, 2 * i + 2)
        return carry

    lax.fori_loop(0, SWEEPS // 2, two_sweeps, 0)

    lane16 = lane_of(SPAN)
    first = (lane16 & 32) == 0
    row16 = lax.broadcasted_iota(jnp.int32, (SPAN, LANES), 0)

    def slots(x, m, centre=False):
        r = pl.multiple_of(PAD + (x + DEPTH) * SPAN, 8)
        near = pl.ds(pl.multiple_of((x + 1) * SPAN, 8), SPAN)
        for j in range(QUADS):
            c = ua[j, pl.ds(r, SPAN), :] * m
            t = roll(c, 64)
            u = 0.5 * jnp.where(lane16 < 64, c + t, t - c)
            if centre:
                udv[j, pl.ds(pl.multiple_of(x * 8, 8), 8), :] = u[4:12]
            fdv[j, near, :] = jnp.where(first, roll(u, -16), roll(u, 16))

    tall = lambda a: jnp.concatenate([a, a], axis=0)
    beside = jnp.where(row16 >= 12, tall(y_sign[0][1]), jnp.where(row16 < 4, tall(y_sign[0][-1]), 1.0))
    slots(-1, mx[0])
    slots(SIDE, mx[1])
    def all_slots(i, carry):
        for n in range(4):
            slots(4 * i + n, beside, True)
        return carry

    lax.fori_loop(0, SIDE // 4, all_slots, 0)
    back = [pltpu.make_async_copy(udv, ud, out_sems.at[0]), pltpu.make_async_copy(fdv, fd, out_sems.at[1])]
    for c in back:
        c.start()
    for c in late:
        c.wait()
    x_halos = [(ref, start + Y_ROWS) for ref, start in (where[(1, 0)], where[(-1, 0)])]
    update_half(0, se_cube, we_cube, zw, own, *x_halos, *yz_halos, udv, fdv, *scalars, keep, send)
    for c in back:
        c.wait()


def ion_copies(half, sp, wd, se_cube, we_cube, sems):
    first, skip = (0, 1) if half == 0 else (half * HALF - 1, 0)
    at, to = pl.ds(first, HALF + 1), (pl.ds(skip, HALF + 1), pl.ds(4, YQ))
    copies = [pltpu.make_async_copy(sp.at[k, :, at], se_cube.at[(k, slice(None), *to)], sems.at[k]) for k in range(PAIRS)]
    copies.append(pltpu.make_async_copy(wd.at[:, at], we_cube.at[(slice(None), *to)], sems.at[PAIRS]))
    return copies


def update_kernel(half, x_starts, sp, wd, *refs):
    sources, scalars, outs = refs[:9], refs[9:13], refs[13:15]
    se_cube, we_cube, zw, sems = refs[15:19]
    held = refs[19:]
    copies = ion_copies(half, sp, wd, se_cube, we_cube, sems)
    copies += [pltpu.make_async_copy(src, dst, sems.at[FIELDS + n]) for n, (src, dst) in enumerate(zip(sources, held))]
    for c in copies:
        c.start()
    for c in copies:
        c.wait()
    own, xdn, xup, *others = held
    update_half(half, se_cube, we_cube, zw, own, (xdn, x_starts[0]), (xup, x_starts[1]), *others, *scalars, *outs)


def update_half(
    half,
    se_cube,
    we_cube,
    zw,
    own,
    xdn,
    xup,
    ydn,
    yup,
    zup,
    zdn,
    ud,
    fd,
    diffusivity,
    rate_const,
    opened,
    give_slot,
    keep,
    send,
):
    x0 = half * HALF
    layers = HALF + 2
    se = se_cube.reshape(PAIRS, QUADS, layers * SPAN, LANES)
    we = we_cube.reshape(QUADS, layers * SPAN, LANES)

    lane = lane_of(8)
    lane32 = lane & 31
    low = lane < 64
    even = (lane & 32) == 0

    def turned(v, way):
        s = jnp.broadcast_to(own[way : way + 1, :], v.shape)
        return jnp.where(s > 0, v, roll(v, 64))

    def put(k, j, rows, v):
        if k < PAIRS:
            se[k, j, rows, :] = v
        else:
            we[j, rows, :] = v

    for k in range(FIELDS):
        (ref, start), way, layer = (xdn, 1, 0) if half == 0 else (xup, 0, layers - 1)
        v = turned(ref[start + k * SIDE : start + (k + 1) * SIDE, :], way)
        for j in range(QUADS):
            put(k, j, slice(layer * SPAN + 4, layer * SPAN + 12), v[j * 8 : j * 8 + 8])
        rows = slice(k * SIDE + x0, k * SIDE + x0 + HALF)
        put(k, 0, pl.ds(SPAN + 12, HALF, stride=SPAN), turned(yup[rows, :], 2))
        put(k, 3, pl.ds(SPAN + 3, HALF, stride=SPAN), turned(ydn[rows, :], 3))

    odd = (lane & 1) == 1
    for j in range(QUADS):
        for i in range(FIELDS):
            rows = slice(j * SIDE + i * 8, j * SIDE + i * 8 + 8)
            zu = turned(zup[rows, :], 4)
            zd = roll(turned(zdn[rows, :], 5), -31)
            both = (jnp.where(odd, zd, zu), jnp.where(odd, zu, zd))
            for c in range(BLOCKS // 2):
                spots = (c + half * (BLOCKS // 2)) * FIELDS
                x = c * FIELDS + i
                for k in range(FIELDS):
                    zw[k, j, x * 8 : x * 8 + 8, :] = roll(both[(spots + k) % 2], 31 - spots - k)

    def by_ion(values, k):
        return jnp.where(even, values[k], values[k + PAIRS])

    half_charge = [by_ion([0.5 * v for v in valences], k) for k in range(PAIRS)]
    rates = [by_ion([diffusivity[i] for i in range(2 * PAIRS)], k) for k in range(PAIRS)]
    signs = [by_ion(reaction_signs, k) for k in range(PAIRS)]
    reactivity = [rate_const[b] * opened[b].astype(jnp.float32) for b in range(2)]
    reactivity = jnp.where(low, reactivity[0], reactivity[1])
    given = give_slot[0]
    top, bottom = lane32 == 31, lane32 == 0
    add = lambda values: functools.reduce(lambda a, b: a + b, values)

    def update(i, carry):
        x = i + x0
        at = pl.ds(pl.multiple_of(i * 8, 8), 8)
        done = [[None] * QUADS for _ in range(PAIRS + 1)]
        for j in range(QUADS):

            def around(ref, lead, layer):
                q = pl.multiple_of(layer * SPAN, 8)
                here = pl.ds(q + 4, 8)
                return (
                    ref[lead + (j, here)],
                    ref[lead + (j, pl.ds(q + 4 + SPAN, 8))],
                    ref[lead + (j, pl.ds(q + 4 - SPAN, 8))],
                    ref[lead + (j + 1, here)] if j < 3 else ref[lead + (0, pl.ds(q + 5, 8))],
                    ref[lead + (j - 1, here)] if j > 0 else ref[lead + (3, pl.ds(q + 3, 8))],
                )

            def all_around(ref, lead, k):
                c, *near = around(ref, lead, i + 1)
                z = zw[k, j, at, :]
                return c, near + [jnp.where(top, z, roll(c, -1)), jnp.where(bottom, z, roll(c, 1))]

            w, near_w = all_around(we, (), PAIRS)
            u = ud[j, pl.ds(pl.multiple_of(x * 8, 8), 8), :]
            phi, *near_phi = around(fd, (), x + 1)
            near_phi += [jnp.where(even, roll(u, -17), roll(u, 15)), jnp.where(even, roll(u, -15), roll(u, 17))]
            drift = [near_w[d] * (phi - near_phi[d]) for d in range(6)]
            w_total, d_total = add(near_w), add(drift)
            conc = []
            for k in range(PAIRS):
                c, near_c = all_around(se, (k,), k)
                spread_w = add([near_w[d] * near_c[d] for d in range(6)])
                spread_d = add([drift[d] * near_c[d] for d in range(6)])
                outflow = w * ((c * w_total - spread_w) + half_charge[k] * (c * d_total + spread_d))
                conc.append(c)
                done[k][j] = c - rates[k] * outflow
            reaction = conc[2] - conc[0] * conc[1] / solubility
            reaction = jnp.where(w > 0, reactivity * reaction, 0.0)
            for k in range(PAIRS):
                done[k][j] = done[k][j] + signs[k] * reaction
            done[PAIRS][j] = phi
        for k in range(PAIRS + 1):
            native = swap_groups(done[k], lane)
            for f in range(2 if k < PAIRS else 1):
                ion = k + f * PAIRS if k < PAIRS else 2 * PAIRS
                send[ion, at, :] = jnp.where(given == 0, native[f], native[2 + f])
                keep[ion, at, :] = jnp.where(given == 0, native[2 + f], native[f])
        return carry

    lax.fori_loop(0, HALF, update, 0, unroll=2)


def place_kernel(give_slot, *refs):
    keep, received, (new_sp, new_pot) = refs[:2], refs[2:4], refs[4:]
    given = give_slot[0]
    ions = new_sp.shape[0]
    for half in range(2):
        rows = [pl.ds(half * PLANE + slot, PLANE // 2, stride=2) for slot in (given, 1 - given)]
        for i in range(ions):
            new_sp[i, rows[0], :] = received[half][i]
            new_sp[i, rows[1], :] = keep[half][i]
        new_pot[rows[0], :] = received[half][ions]
        new_pot[rows[1], :] = keep[half][ions]


VMEM = pl.BlockSpec(memory_space=pltpu.VMEM)
SMEM = pl.BlockSpec(memory_space=pltpu.SMEM)
ANY = pl.BlockSpec(memory_space=pl.ANY)
HBM = pl.BlockSpec(memory_space=pltpu.HBM)
MIB = 1024 * 1024


def grant(mib):
    return pltpu.CompilerParams(vmem_limit_bytes=mib * MIB)


def f32(*shape):
    return jax.ShapeDtypeStruct(shape, jnp.float32)


def rows_of(field):
    lead = field.shape[:-2]
    bricks, cells = field.shape[-2:]
    split = field.reshape(lead + (bricks, cells // LANES, LANES))
    return jnp.swapaxes(split, -3, -2).reshape(lead + (bricks * cells // LANES, LANES))


def cells_of(rows):
    lead = rows.shape[:-2]
    count, lanes = rows.shape[-2:]
    split = rows.reshape(lead + (count // 2, 2, lanes))
    return jnp.swapaxes(split, -3, -2).reshape(lead + (2, count // 2 * lanes))


def moved(block, axis, offset):
    n = lax.axis_size(axis)
    return lax.ppermute(block, axis, [(i, (i + offset) % n) for i in range(n)])


def local(
    species,
    potential,
    pore,
    openness,
    neighbours,
    diffusivity,
    rate_const,
    opened,
    partner,
    give_slot,
):
    ion_count, brick_count, cells = species.shape
    dev_count = lax.axis_size("dev")
    stride = dev_count // 4

    held = {}
    for sx, sy in SIDES + CORNERS:
        offset = (sx + sy * stride) % dev_count
        offset = offset if offset <= dev_count // 2 else offset - dev_count
        rows, pieces = held.get(offset, (0, ()))
        held[offset] = (rows + (X_ROWS if sy == 0 else Y_ROWS if sx == 0 else EDGE_ROWS), pieces + (((sx, sy), rows),))
    offsets = sorted(held, key=lambda o: (-held[o][0], -abs(o), o))
    pieces = tuple(held[o][1] for o in offsets)

    with_face = [k for k, o in enumerate(offsets) if held[o][0] >= Y_ROWS]
    alone = [k for k in range(len(offsets)) if k not in with_face]
    rows = brick_count * PLANE
    species_rows, pore_rows, openness_rows = rows_of(species), rows_of(pore), rows_of(openness)
    field = pltpu.VMEM((rows, LANES), jnp.float32)
    field_int = pltpu.VMEM((rows, LANES), jnp.int32)
    fields = pltpu.VMEM((ion_count, rows, LANES), jnp.float32)
    pd, own, *blocks, down, up = pl.pallas_call(
        functools.partial(pack_kernel, pieces),
        out_shape=(
            f32(QUADS, PLANE, LANES),
            f32(8, LANES),
            *(f32(held[o][0], LANES) for o in offsets),
            f32(ZC_ROWS, LANES),
            f32(ZC_ROWS, LANES),
        ),
        in_specs=[HBM] * 4 + [SMEM],
        out_specs=tuple([VMEM] * (4 + len(offsets))),
        scratch_shapes=[fields, field, field_int, field, pltpu.SemaphoreType.DMA((PARTS, 3, 4))],
        compiler_params=grant(60),
        name="pack",
    )(species_rows, rows_of(potential), pore_rows, openness_rows, neighbours)
    faces = [k for k, o in enumerate(offsets) if held[o][0] >= Y_ROWS]
    rest = faces[-1:] + [k for k in range(len(offsets)) if k not in faces]
    zup = moved(down, "group", -1)
    zdn = moved(up, "group", 1)
    arrived = {k: moved(blocks[k], "dev", offsets[k]) for k in faces[:-1]}

    sp, wd, ydown, yup = pl.pallas_call(
        ions_kernel,
        out_shape=(f32(PAIRS, QUADS, PLANE, LANES), f32(QUADS, PLANE, LANES), *([f32(ION_ROWS, LANES)] * 2)),
        in_specs=[HBM] * 3,
        out_specs=(VMEM,) * 4,
        scratch_shapes=[fields, field_int, field, pltpu.SemaphoreType.DMA((2, 3))],
        compiler_params=grant(60),
        name="ions",
    )(species_rows, pore_rows, openness_rows)

    zup, zdn, sp, wd, *more = lax.optimization_barrier((zup, zdn, sp, wd, *(blocks[k] for k in rest)))
    arrived.update((k, moved(block, "dev", offsets[k])) for k, block in zip(rest, more))

    zdown, zupper = pl.pallas_call(
        ion_z_kernel,
        out_shape=(f32(ION_ROWS, LANES),) * 2,
        in_specs=[VMEM] * 2,
        out_specs=(VMEM,) * 2,
        compiler_params=grant(8),
        name="ion_z_faces",
    )(sp, wd)

    z_halos = [moved(zdown, "group", -1), moved(zupper, "group", 1)]
    arrived = [arrived[k] for k in range(len(offsets))]

    zl, zh = pl.pallas_call(
        functools.partial(relay_kernel, pieces),
        out_shape=(f32(ZH_ROWS, LANES),) * 2,
        in_specs=[VMEM] * len(offsets),
        out_specs=(VMEM, VMEM),
        compiler_params=grant(6),
        name="relay",
    )(*arrived)
    ydown, yup, zl, zh = lax.optimization_barrier((ydown, yup, zl, zh))
    zhup = moved(zl, "group", -1)
    zhdn = moved(zh, "group", 1)
    y_halos = [moved(yup, "dev", stride), moved(ydown, "dev", -stride)]

    wide = pltpu.VMEM((QUADS, EXT * SPAN + 2 * PAD, LANES), jnp.float32)
    by_layer = lambda a: a.reshape(a.shape[:-2] + (SIDE, YQ, LANES))
    sp, wd = by_layer(sp), by_layer(wd)
    scalars = (diffusivity, rate_const, opened, give_slot)
    half_out = (f32(ion_count + 1, PLANE // 2, LANES),) * 2
    half_scratch = [
        pltpu.VMEM((PAIRS, QUADS, HALF + 2, SPAN, LANES), jnp.float32),
        pltpu.VMEM((QUADS, HALF + 2, SPAN, LANES), jnp.float32),
        pltpu.VMEM((FIELDS, QUADS, PLANE // 2, LANES), jnp.float32),
    ]
    sources = (own, pd, zup, zdn, zhup, zhdn, *y_halos, *z_halos, *arrived)
    ud, fd, *first_half = pl.pallas_call(
        functools.partial(sweep_kernel, pieces),
        out_shape=(f32(QUADS, PLANE, LANES), f32(QUADS, NEAR * SPAN, LANES), *half_out),
        in_specs=[HBM] * (len(sources) + 2) + [SMEM] * 4,
        out_specs=(HBM, HBM, VMEM, VMEM),
        scratch_shapes=[
            wide,
            wide,
            wide,
            pltpu.VMEM((2, SPAN, LANES), jnp.float32),
            pltpu.VMEM((3, SPAN, LANES), jnp.float32),
            pltpu.VMEM((3, SPAN, LANES), jnp.float32),
            *half_scratch,
            pltpu.VMEM((QUADS, PLANE, LANES), jnp.float32),
            pltpu.VMEM((QUADS, NEAR * SPAN, LANES), jnp.float32),
            pltpu.SemaphoreType.DMA((len(sources),)),
            pltpu.SemaphoreType.DMA((FIELDS,)),
            pltpu.SemaphoreType.DMA((2,)),
            *(pltpu.VMEM(a.shape, jnp.float32) for a in sources),
        ],
        compiler_params=grant(60),
        name="sweeps",
    )(*sources, sp, wd, *scalars)

    def second_half():
        x_halos, x_starts = [], []
        for sx in (1, -1):
            for k, parts in enumerate(pieces):
                for name, start in parts:
                    if name == (sx, 0):
                        x_halos.append(arrived[k])
                        x_starts.append(start + Y_ROWS)
        sources = (own, *x_halos, *y_halos, *z_halos, ud, fd)
        return pl.pallas_call(
            functools.partial(update_kernel, 1, x_starts),
            out_shape=half_out,
            in_specs=[HBM] * (len(sources) + 2) + [SMEM] * 4,
            out_specs=(VMEM, VMEM),
            scratch_shapes=[
                *half_scratch,
                pltpu.SemaphoreType.DMA((FIELDS + len(sources),)),
                *(pltpu.VMEM(a.shape, jnp.float32) for a in sources),
            ],
            compiler_params=grant(32),
            name="update",
        )(sp, wd, *sources, *scalars)

    def placed(kept, received):
        new_sp, new_pot = pl.pallas_call(
            place_kernel,
            out_shape=(f32(ion_count, rows, LANES), f32(rows, LANES)),
            in_specs=[SMEM] + [VMEM] * 4,
            out_specs=(VMEM, VMEM),
            compiler_params=grant(8),
            name="place",
        )(give_slot, *kept, *received)
        return cells_of(new_sp), cells_of(new_pot)

    def finished(route):
        across = lambda block: block if route is None else lax.ppermute(block, ("group", "dev"), route)
        keep, send = first_half
        keep_more, send_more = second_half()
        return placed((keep, keep_more), (across(send), across(send_more)))

    total = lax.axis_size("group") * dev_count
    own_index = lax.axis_index("group") * dev_count + lax.axis_index("dev")
    apart = jnp.bitwise_xor(own_index, partner[0])
    branch = jnp.int32(0)
    branches = [lambda: finished(None)]
    for bit in range(total.bit_length() - 1):
        route = [(i, i ^ (1 << bit)) for i in range(total)]
        branch = jnp.where(apart == (1 << bit), bit + 1, branch)
        branches.append(lambda route=route: finished(route))
    return lax.switch(branch, branches)


def solution(mesh):
    in_specs = (
        P(None, ("group", "dev"), None),
        P(("group", "dev"), None),
        P(("group", "dev"), None),
        P(("group", "dev"), None),
        P(("group", "dev"), None),
        P(),
        P(("group", "dev")),
        P(("group", "dev")),
        P(("group", "dev")),
        P(("group", "dev")),
    )
    out_specs = (P(None, ("group", "dev"), None), P(("group", "dev"), None))
    return jax.shard_map(local, mesh=mesh, in_specs=in_specs, out_specs=out_specs, check_vma=False)
```

```python
import functools

import jax
import jax.numpy as jnp
from jax import lax
from jax.experimental import pallas as pl
from jax.experimental.pallas import tpu as pltpu
from jax.sharding import PartitionSpec as P


SWEEPS = 8
DEPTH = SWEEPS + 1
LANES = 128

charge_scale = 0.5
screening = 0.5
solubility = 2.0
valences = (2.0, -1.0, 1.0, -1.0, 1.0, 2.0)
reaction_signs = (1.0, 1.0, -1.0, 0.0, 0.0, 0.0)

SIDE = 32
QUADS = 4
YQ = SIDE // QUADS
PAIRS = 3
PLANE = SIDE * YQ
HALF = SIDE // 2

FACE_TBL = DEPTH * SIDE
Y_ION = FACE_TBL + 8
EDGE_TBL = 64
EDGE_ROWS = EDGE_TBL + 8
THIRD = 11
ZC_TBL = QUADS * THIRD * YQ
ZC_ROWS = ZC_TBL + 8
ZH_EDGE = 2 * 3 * SIDE
ZH_TBL = ZH_EDGE + 64
ZH_ION = ZH_TBL + 32
FIELDS = PAIRS + 1
ION_ROWS = FIELDS * SIDE
Y_ROWS = Y_ION + ION_ROWS
BLOCKS = SIDE // FIELDS
ZH_ROWS = ZH_ION + ION_ROWS

ZH_PLACE = {
    (n, l): (n, off) if l < 5 else (2, 6 * n + off)
    for n in range(2)
    for l, off in enumerate((0, 8, 15, 21, 26, 0, 3, 5))
}

SIDES = ((-1, 0), (1, 0), (0, -1), (0, 1))
CORNERS = ((-1, -1), (-1, 1), (1, -1), (1, 1))
SPAN = 16
EXT = SIDE + 2 * DEPTH
MIDDLE = 10
PARTS = 3
PART = 4
NEAR = SIDE + 2
PAD = 24


def x_way(s):
    return 0 if s > 0 else 1


def y_way(s):
    return 2 if s > 0 else 3


def z_way(s):
    return 4 if s > 0 else 5


def roll(v, shift):
    shift = shift % LANES
    return v if shift == 0 else pltpu.roll(v, shift, 1)


def lane_of(rows):
    return lax.broadcasted_iota(jnp.int32, (rows, LANES), 1)


def swap_groups(v, lane):
    low = lane < 64
    a0 = jnp.where(low, v[0], roll(v[2], 64))
    a2 = jnp.where(low, roll(v[0], 64), v[2])
    a1 = jnp.where(low, v[1], roll(v[3], 64))
    a3 = jnp.where(low, roll(v[1], 64), v[3])
    even = (lane & 32) == 0
    return (
        jnp.where(even, a0, roll(a1, 32)),
        jnp.where(even, roll(a0, 96), a1),
        jnp.where(even, a2, roll(a3, 32)),
        jnp.where(even, roll(a2, 96), a3),
    )


def sign_rows(neighbours):
    row = lax.broadcasted_iota(jnp.int32, (8, LANES), 0)
    table = jnp.zeros((8, LANES), jnp.float32)
    for way in range(6):
        table = jnp.where(row == way, jnp.where(neighbours[0, way] == 0, 1.0, -1.0), table)
    return table


def pack_kernel(pieces, species_in, potential_in, pore_in, openness_in, neighbours, pd, own, *rest):
    n_out = len(pieces)
    outs, (zlo, zhi) = rest[:n_out], rest[n_out : n_out + 2]
    species, potential, pore, openness, sems = rest[n_out + 2 :]
    parts = []
    for part in range(PARTS):
        copies = []
        for c in range(3):
            x0 = c * THIRD + part * PART
            count = min(PART, (c + 1) * THIRD - x0, SIDE - x0)
            rows = pl.ds(x0 * 16, count * 16)
            for number, (src, dst) in enumerate(
                ((species_in, species), (potential_in, potential), (pore_in, pore), (openness_in, openness))
            ):
                at = (slice(None), rows) if number == 0 else (rows,)
                copies.append(pltpu.make_async_copy(src.at[at], dst.at[at], sems.at[part, c, number]))
                copies[-1].start()
        parts.append(copies)
    where = {name: (outs[k], base) for k, held in enumerate(pieces) for name, base in held}
    lane = lane_of(8)
    lane32 = lane & 31
    low = lane < 64
    table = sign_rows(neighbours)
    own[...] = table

    def planes_of(x):
        d, p = [], []
        for b in range(2):
            rows = pl.ds(x * 16 + b, 8, stride=2)
            total = valences[0] * species[0, rows, :]
            for i in range(1, 2 * PAIRS):
                total = total + valences[i] * species[i, rows, :]
            wet = pore[rows, :].astype(jnp.float32) * openness[rows, :]
            d.append(charge_scale * wet * total)
            p.append(potential[rows, :])
        mixed = []
        for v in swap_groups((p[0], d[0], p[1], d[1]), lane):
            r = roll(v, 64)
            mixed.append(jnp.where(low, v + r, r - v))
        at = pl.ds(pl.multiple_of(x * 8, 8), 8)
        for j in range(QUADS):
            pd[j, at, :] = mixed[j]
        return mixed

    def step(i, blocks=3):
        planes = [planes_of(i + c * THIRD) for c in range(blocks)]
        for j in range(QUADS):
            at = pl.ds(pl.multiple_of((j * THIRD + i) * 8, 8), 8)
            lo = hi = planes[0][j]
            for c in range(1, blocks):
                lo = jnp.where(lane32 >= DEPTH * c, roll(planes[c][j], DEPTH * c), lo)
                hi = jnp.where(lane32 < SIDE - DEPTH * c, roll(planes[c][j], -DEPTH * c), hi)
            zlo[at, :] = lo
            zhi[at, :] = hi

    for part in range(PARTS):
        for c in parts[part]:
            c.wait()
        end = min((part + 1) * PART, THIRD - 1)
        lax.fori_loop(part * PART, end, lambda i, carry: (step(i), carry)[1], 0)
    step(THIRD - 1, 2)

    zlo[ZC_TBL:, :] = table
    zhi[ZC_TBL:, :] = table

    def ion_planes(x, ref, start):
        for k, planes in enumerate(dense_ions(species, pore, openness, x, lane)):
            for j in range(QUADS):
                ref[start + k * SIDE + j * 8 : start + k * SIDE + j * 8 + 8, :] = planes[j]

    group = lane_of(SIDE) >> 5

    def ion_rows(y, ref, start):
        for k in range(FIELDS):
            v = jnp.zeros((SIDE, LANES), jnp.float32)
            for b in range(2):
                rows = pl.ds(y // 4 * 2 + b, SIDE, stride=16)
                if k == PAIRS:
                    wet = pore[rows, :].astype(jnp.float32) * openness[rows, :]
                for f in range(2):
                    native = species[k + f * PAIRS, rows, :] if k < PAIRS else wet
                    v = jnp.where(group == 2 * b + f, roll(native, (2 * b + f - y % 4) * SIDE), v)
            ref[start + k * SIDE : start + (k + 1) * SIDE, :] = v

    for sx, sy in SIDES:
        ref, base = where[(sx, sy)]
        for l in range(DEPTH):
            if sx:
                x = l if sx < 0 else SIDE - 1 - l
                for j in range(QUADS):
                    ref[base + l * SIDE + j * 8 : base + l * SIDE + j * 8 + 8, :] = pd[j, x * 8 : x * 8 + 8, :]
            else:
                y = l if sy < 0 else SIDE - 1 - l
                ref[base + l * SIDE : base + (l + 1) * SIDE, :] = pd[y % 4, pl.ds(y // 4, SIDE, stride=8), :]
        ref[base + FACE_TBL : base + Y_ION, :] = table
        if sx:
            ion_planes(0 if sx < 0 else SIDE - 1, ref, base + Y_ION)
        else:
            ion_rows(0 if sy < 0 else SIDE - 1, ref, base + Y_ION)
    for sx, sy in CORNERS:
        ref, base = where[(sx, sy)]
        x0 = 0 if sx < 0 else SIDE - 8
        for m in range(8):
            y = m if sy < 0 else SIDE - 8 + m
            ref[base + m * 8 : base + m * 8 + 8, :] = pd[y % 4, pl.ds(x0 * 8 + y // 4, 8, stride=8), :]
        ref[base + EDGE_TBL : base + EDGE_ROWS, :] = table


def dense_ions(species, pore, openness, x, lane):
    rows = [pl.ds(x * 16 + b, 8, stride=2) for b in range(2)]
    w = [pore[rows[b], :].astype(jnp.float32) * openness[rows[b], :] for b in range(2)]
    s = [[species[n, rows[b], :] for b in range(2)] for n in range(2 * PAIRS)]
    fields = [swap_groups((s[k][0], s[k + PAIRS][0], s[k][1], s[k + PAIRS][1]), lane) for k in range(PAIRS)]
    return fields + [swap_groups((w[0], w[0], w[1], w[1]), lane)]


def ions_kernel(species_in, pore_in, openness_in, sp, wd, species, pore, openness, sems):
    parts = []
    for part in range(2):
        rows = pl.ds(part * PLANE, PLANE)
        copies = [
            pltpu.make_async_copy(species_in.at[:, rows], species.at[:, rows], sems.at[part, 0]),
            pltpu.make_async_copy(pore_in.at[rows], pore.at[rows], sems.at[part, 1]),
            pltpu.make_async_copy(openness_in.at[rows], openness.at[rows], sems.at[part, 2]),
        ]
        for c in copies:
            c.start()
        parts.append(copies)
    lane = lane_of(8)

    def step(x, carry):
        at = pl.ds(pl.multiple_of(x * 8, 8), 8)
        for k, planes in enumerate(dense_ions(species, pore, openness, x, lane)):
            for j in range(QUADS):
                if k < PAIRS:
                    sp[k, j, at, :] = planes[j]
                else:
                    wd[j, at, :] = planes[j]
        return carry

    for part in range(2):
        for c in parts[part]:
            c.wait()
        lax.fori_loop(part * HALF, (part + 1) * HALF, step, 0, unroll=2)


def ion_z_kernel(sp, wd, zlo, zhi):
    lane32 = lane_of(8) & 31

    def step(i, carry):
        for j in range(QUADS):
            lo = hi = jnp.zeros((8, LANES), jnp.float32)
            for spot in range(SIDE):
                block, k = spot // FIELDS, spot % FIELDS
                at = pl.ds(pl.multiple_of((i + block * FIELDS) * 8, 8), 8)
                v = sp[k, j, at, :] if k < PAIRS else wd[j, at, :]
                lo = jnp.where(lane32 == spot, roll(v, spot), lo)
                hi = jnp.where(lane32 == spot, roll(v, spot - 31), hi)
            zat = pl.ds(pl.multiple_of(j * SIDE + i * 8, 8), 8)
            zlo[zat, :] = lo
            zhi[zat, :] = hi
        return carry

    lax.fori_loop(0, FIELDS, step, 0)


def relay_kernel(pieces, *refs):
    arrived, (ions_lo, ions_hi, zl, zh) = refs[:-5], refs[-4:]
    zl[ZH_ION:, :] = ions_lo[...]
    zh[ZH_ION:, :] = ions_hi[...]
    where = {name: (arrived[k], base) for k, held in enumerate(pieces) for name, base in held}
    lane32 = lane_of(SIDE) & 31
    for axis in range(2):
        lo = [jnp.zeros((SIDE, LANES), jnp.float32)] * 3
        hi = [jnp.zeros((SIDE, LANES), jnp.float32)] * 3
        for n in range(2):
            sx, sy = SIDES[2 * axis + n]
            ref, base = where[(-sx, -sy)]
            for l in range(8):
                block, off = ZH_PLACE[n, l]
                width = 8 - l
                v = ref[base + l * SIDE : base + (l + 1) * SIDE, :]
                lo[block] = jnp.where((lane32 >= off) & (lane32 < off + width), roll(v, off), lo[block])
                hi[block] = jnp.where((lane32 <= 31 - off) & (lane32 > 31 - off - width), roll(v, -off), hi[block])
            at = slice(ZH_TBL + (2 * axis + n) * 8, ZH_TBL + (2 * axis + n) * 8 + 8)
            zl[at, :] = ref[base + FACE_TBL : base + Y_ION, :]
            zh[at, :] = ref[base + FACE_TBL : base + Y_ION, :]
        for block in range(3):
            at = slice((axis * 3 + block) * SIDE, (axis * 3 + block + 1) * SIDE)
            zl[at, :] = lo[block]
            zh[at, :] = hi[block]
    group = lane_of(64) & 31
    lo = jnp.zeros((64, LANES), jnp.float32)
    hi = lo
    for number, (sx, sy) in enumerate(CORNERS):
        ref, base = where[(-sx, -sy)]
        v = ref[base : base + EDGE_TBL, :]
        lo = jnp.where((group >= 8 * number) & (group < 8 * number + 8), roll(v, 8 * number), lo)
        hi = jnp.where((group <= 31 - 8 * number) & (group > 23 - 8 * number), roll(v, -8 * number), hi)
    zl[ZH_EDGE : ZH_EDGE + 64, :] = lo
    zh[ZH_EDGE : ZH_EDGE + 64, :] = hi


def sweep_kernel(pieces, *refs):
    n_in = 6 + len(pieces)
    sources, (sp, wd), scalars = refs[:n_in], refs[n_in : n_in + 2], refs[n_in + 2 : n_in + 6]
    ud, fd, keep, send = refs[n_in + 6 : n_in + 10]
    ua, ub, dn, mx, myp, mym, se_cube, we_cube, zw, udv, fdv, sems, ion_sems, out_sems = refs[n_in + 10 : n_in + 24]
    held = refs[n_in + 24 :]
    copies = [pltpu.make_async_copy(src, dst, sems.at[i]) for i, (src, dst) in enumerate(zip(sources, held))]
    for c in copies:
        c.start()
    late = ion_copies(0, sp, wd, se_cube, we_cube, ion_sems)
    for c in late:
        c.start()
    own, pd, zup, zdn, zhup, zhdn = held[:6]
    arrived = held[6:]
    where = {name: (arrived[k], base) for k, held in enumerate(pieces) for name, base in held}

    lane = lane_of(8)
    lane64 = lane & 63
    low = lane < 64
    core = (lane64 >= 16) & (lane64 < 48)
    upper = lane64 >= 48

    for c in copies:
        c.wait()
    table = {(0, 0): own[...]}
    ztable = {1: {(0, 0): zup[ZC_TBL:, :]}, -1: {(0, 0): zdn[ZC_TBL:, :]}}
    for number, (sx, sy) in enumerate(SIDES):
        ref, base = where[(-sx, -sy)]
        table[(sx, sy)] = ref[base + FACE_TBL : base + Y_ION, :]
        for sz, held in ((1, zhup), (-1, zhdn)):
            ztable[sz][(sx, sy)] = held[ZH_TBL + number * 8 : ZH_TBL + number * 8 + 8, :]
    for sx, sy in CORNERS:
        ref, base = where[(-sx, -sy)]
        table[(sx, sy)] = ref[base + EDGE_TBL : base + EDGE_ROWS, :]

    def sign(held, way):
        return jnp.broadcast_to(held[way : way + 1, :], (8, LANES))

    def crossing(way, here, there):
        level = sign(table[here], way)
        beyond = {}
        for sz in (1, -1):
            z = z_way(sz)
            beyond[sz] = sign(ztable[sz][here], way) * sign(table[here], z) * sign(table[there], z)
        m = jnp.where(core, level, jnp.where(upper, beyond[1], beyond[-1]))
        return jnp.where(low, 1.0, m)

    row8 = lax.broadcasted_iota(jnp.int32, (8, LANES), 0)
    one = jnp.ones((8, LANES), jnp.float32)
    for number, sx in enumerate((-1, 1)):
        m = {sy: crossing(x_way(sx), (0, sy), (sx, sy)) for sy in (-1, 0, 1)}
        mx[number, 0:8, :] = jnp.where(row8 < 4, m[-1], m[0])
        mx[number, 8:16, :] = jnp.where(row8 < 4, m[0], m[1])
    y_sign = {}
    for number, sx in enumerate((-1, 0, 1)):
        m = {sy: crossing(y_way(sy), (sx, 0), (sx, sy)) for sy in (-1, 1)}
        y_sign[sx] = m
        myp[number, 0:8, :] = jnp.where(row8 == 3, m[-1], one)
        myp[number, 8:16, :] = jnp.where(row8 == 3, m[1], one)
        mym[number, 0:8, :] = jnp.where(row8 == 4, m[-1], one)
        mym[number, 8:16, :] = jnp.where(row8 == 4, m[1], one)

    outer = {}
    for key, held in table.items():
        m = jnp.where(upper, sign(held, 4), sign(held, 5))
        outer[key] = jnp.where(low, 1.0, m)

    def spread(v, zu, zd, shift_u, shift_d, key):
        rows = v.shape[0]
        tall = lambda a: a if rows == 8 else jnp.concatenate([a] * (rows // 8), axis=0)
        if zu is None:
            return roll(v, 16), roll(v, -16)
        m, c, u = tall(outer[key]), tall(core), tall(upper)
        pot = jnp.where(u, roll(zu, 48 + shift_u), roll(zd, -16 + shift_d)) * m
        rho = jnp.where(u, roll(zu, 16 + shift_u), roll(zd, -48 + shift_d)) * m
        return jnp.where(c, roll(v, 16), pot), jnp.where(c, roll(v, -16), rho)

    def fill(i, c):
        x = i + c * THIRD
        at = pl.ds(pl.multiple_of(x * 8, 8), 8)
        to = pl.ds(pl.multiple_of(PAD + (x + DEPTH) * SPAN + 4, 4), 8)
        for j in range(QUADS):
            zat = pl.ds(pl.multiple_of((j * THIRD + i) * 8, 8), 8)
            pot, rho = spread(pd[j, at, :], zup[zat, :], zdn[zat, :], -DEPTH * c, DEPTH * c, (0, 0))
            ua[j, to, :] = pot
            dn[j, to, :] = rho

    def fill_three(i, carry):
        for c in range(3):
            fill(i, c)
        return carry

    lax.fori_loop(0, THIRD - 1, fill_three, 0)
    fill(THIRD - 1, 0)
    fill(THIRD - 1, 1)

    for number, (sx, sy) in enumerate(SIDES):
        ref, base = where[(-sx, -sy)]
        for l in range(DEPTH):
            v = ref[base + l * SIDE : base + (l + 1) * SIDE, :]
            zu = zd = None
            off = 0
            if l < 8:
                block, off = ZH_PLACE[number % 2, l]
                block += number // 2 * 3
                at = slice(block * SIDE, (block + 1) * SIDE)
                zu, zd = zhup[at, :], zhdn[at, :]
            pot, rho = spread(v, zu, zd, -off, off, (sx, sy))
            if sx:
                x = SIDE + l if sx > 0 else -1 - l
                start = PAD + (x + DEPTH) * SPAN + 4
                for j in range(QUADS):
                    ua[j, start : start + 8, :] = pot[j * 8 : j * 8 + 8]
                    dn[j, start : start + 8, :] = rho[j * 8 : j * 8 + 8]
            else:
                j = l % 4 if sy > 0 else 3 - l % 4
                row = 12 + l // 4 if sy > 0 else 3 - l // 4
                at = pl.ds(PAD + DEPTH * SPAN + row, SIDE, stride=SPAN)
                ua[j, at, :] = pot
                dn[j, at, :] = rho
    for number, (sx, sy) in enumerate(CORNERS):
        ref, base = where[(-sx, -sy)]
        for m in range(8):
            v = ref[base + m * 8 : base + m * 8 + 8, :]
            at = slice(ZH_EDGE + m * 8, ZH_EDGE + m * 8 + 8)
            pot, rho = spread(v, zhup[at, :], zhdn[at, :], -8 * number, 8 * number, (sx, sy))
            row = (12 if sy > 0 else 2) + m // 4
            x = SIDE if sx > 0 else -8
            to = pl.ds(PAD + (x + DEPTH) * SPAN + row, 8, stride=SPAN)
            ua[m % 4, to, :] = pot
            dn[m % 4, to, :] = rho

    scale = 1.0 / (6.0 + screening)

    def slab(src, dst, x, sx, before=None, after=None):
        r = pl.multiple_of(PAD + (x + DEPTH) * SPAN, 8)
        at = pl.ds(r, SPAN)
        c = [src[j, at, :] for j in range(QUADS)]
        for j in range(QUADS):
            left = src[j, pl.ds(r - SPAN, SPAN), :]
            right = src[j, pl.ds(r + SPAN, SPAN), :]
            if before is not None:
                left = left * mx[before]
            if after is not None:
                right = right * mx[after]
            north = c[j + 1] if j < 3 else src[0, pl.ds(r + 1, SPAN), :] * myp[sx + 1]
            south = c[j - 1] if j > 0 else src[3, pl.ds(r - 1, SPAN), :] * mym[sx + 1]
            total = (left + right) + (north + south) + (roll(c[j], 1) + roll(c[j], -1)) + dn[j, at, :]
            dst[j, at, :] = total * scale

    def sweep(src, dst, t):
        def middle(i, carry):
            for n in range(MIDDLE):
                slab(src, dst, 1 + i * MIDDLE + n, 0)
            return carry

        def fringe(i, carry):
            for n in range(2):
                slab(src, dst, -2 - 2 * i - n, -1)
                slab(src, dst, SIDE + 1 + 2 * i + n, 1)
            return carry

        lax.fori_loop(0, (SIDE - 2) // MIDDLE, middle, 0)
        slab(src, dst, -1, -1, after=0)
        slab(src, dst, 0, 0, before=0)
        slab(src, dst, SIDE - 1, 0, after=1)
        slab(src, dst, SIDE, 1, before=1)
        lax.fori_loop(0, (SWEEPS + 1 - t) // 2, fringe, 0)

    def two_sweeps(i, carry):
        sweep(ua, ub, 2 * i + 1)
        sweep(ub, ua, 2 * i + 2)
        return carry

    lax.fori_loop(0, SWEEPS // 2, two_sweeps, 0)

    lane16 = lane_of(SPAN)
    first = (lane16 & 32) == 0
    row16 = lax.broadcasted_iota(jnp.int32, (SPAN, LANES), 0)

    def slots(x, m, centre=False):
        r = pl.multiple_of(PAD + (x + DEPTH) * SPAN, 8)
        near = pl.ds(pl.multiple_of((x + 1) * SPAN, 8), SPAN)
        for j in range(QUADS):
            c = ua[j, pl.ds(r, SPAN), :] * m
            t = roll(c, 64)
            u = 0.5 * jnp.where(lane16 < 64, c + t, t - c)
            if centre:
                udv[j, pl.ds(pl.multiple_of(x * 8, 8), 8), :] = u[4:12]
            fdv[j, near, :] = jnp.where(first, roll(u, -16), roll(u, 16))

    tall = lambda a: jnp.concatenate([a, a], axis=0)
    beside = jnp.where(row16 >= 12, tall(y_sign[0][1]), jnp.where(row16 < 4, tall(y_sign[0][-1]), 1.0))
    slots(-1, mx[0])
    slots(SIDE, mx[1])
    def all_slots(i, carry):
        for n in range(4):
            slots(4 * i + n, beside, True)
        return carry

    lax.fori_loop(0, SIDE // 4, all_slots, 0)
    back = [pltpu.make_async_copy(udv, ud, out_sems.at[0]), pltpu.make_async_copy(fdv, fd, out_sems.at[1])]
    for c in back:
        c.start()
    for c in late:
        c.wait()
    halos = [(ref, start + Y_ION) for ref, start in (where[(1, 0)], where[(-1, 0)], where[(0, 1)], where[(0, -1)])]
    update_half(0, se_cube, we_cube, zw, own, *halos, zhup, zhdn, udv, fdv, *scalars, keep, send)
    for c in back:
        c.wait()


def ion_copies(half, sp, wd, se_cube, we_cube, sems):
    first, skip = (0, 1) if half == 0 else (half * HALF - 1, 0)
    at, to = pl.ds(first, HALF + 1), (pl.ds(skip, HALF + 1), pl.ds(4, YQ))
    copies = [pltpu.make_async_copy(sp.at[k, :, at], se_cube.at[(k, slice(None), *to)], sems.at[k]) for k in range(PAIRS)]
    copies.append(pltpu.make_async_copy(wd.at[:, at], we_cube.at[(slice(None), *to)], sems.at[PAIRS]))
    return copies


def update_kernel(half, starts, sp, wd, *refs):
    sources, scalars, outs = refs[:9], refs[9:13], refs[13:15]
    se_cube, we_cube, zw, sems = refs[15:19]
    held = refs[19:]
    copies = ion_copies(half, sp, wd, se_cube, we_cube, sems)
    copies += [pltpu.make_async_copy(src, dst, sems.at[FIELDS + n]) for n, (src, dst) in enumerate(zip(sources, held))]
    for c in copies:
        c.start()
    for c in copies:
        c.wait()
    own, *others = held
    halos = list(zip(others[:4], starts))
    update_half(half, se_cube, we_cube, zw, own, *halos, *others[4:], *scalars, *outs)


def update_half(
    half,
    se_cube,
    we_cube,
    zw,
    own,
    xdn,
    xup,
    ydn,
    yup,
    zup,
    zdn,
    ud,
    fd,
    diffusivity,
    rate_const,
    opened,
    give_slot,
    keep,
    send,
):
    x0 = half * HALF
    layers = HALF + 2
    se = se_cube.reshape(PAIRS, QUADS, layers * SPAN, LANES)
    we = we_cube.reshape(QUADS, layers * SPAN, LANES)

    lane = lane_of(8)
    lane32 = lane & 31
    low = lane < 64
    even = (lane & 32) == 0

    def turned(v, way):
        s = jnp.broadcast_to(own[way : way + 1, :], v.shape)
        return jnp.where(s > 0, v, roll(v, 64))

    def put(k, j, rows, v):
        if k < PAIRS:
            se[k, j, rows, :] = v
        else:
            we[j, rows, :] = v

    for k in range(FIELDS):
        (ref, start), way, layer = (xdn, 1, 0) if half == 0 else (xup, 0, layers - 1)
        v = turned(ref[start + k * SIDE : start + (k + 1) * SIDE, :], way)
        for j in range(QUADS):
            put(k, j, slice(layer * SPAN + 4, layer * SPAN + 12), v[j * 8 : j * 8 + 8])
        for j, row, way, (ref, start) in ((0, 12, 2, yup), (3, 3, 3, ydn)):
            rows = slice(start + k * SIDE + x0, start + k * SIDE + x0 + HALF)
            put(k, j, pl.ds(SPAN + row, HALF, stride=SPAN), turned(ref[rows, :], way))

    odd = (lane & 1) == 1
    for j in range(QUADS):
        for i in range(FIELDS):
            rows = slice(ZH_ION + j * SIDE + i * 8, ZH_ION + j * SIDE + i * 8 + 8)
            zu = turned(zup[rows, :], 4)
            zd = roll(turned(zdn[rows, :], 5), -31)
            both = (jnp.where(odd, zd, zu), jnp.where(odd, zu, zd))
            for c in range(BLOCKS // 2):
                spots = (c + half * (BLOCKS // 2)) * FIELDS
                x = c * FIELDS + i
                for k in range(FIELDS):
                    zw[k, j, x * 8 : x * 8 + 8, :] = roll(both[(spots + k) % 2], 31 - spots - k)

    def by_ion(values, k):
        return jnp.where(even, values[k], values[k + PAIRS])

    half_charge = [by_ion([0.5 * v for v in valences], k) for k in range(PAIRS)]
    rates = [by_ion([diffusivity[i] for i in range(2 * PAIRS)], k) for k in range(PAIRS)]
    signs = [by_ion(reaction_signs, k) for k in range(PAIRS)]
    reactivity = [rate_const[b] * opened[b].astype(jnp.float32) for b in range(2)]
    reactivity = jnp.where(low, reactivity[0], reactivity[1])
    given = give_slot[0]
    top, bottom = lane32 == 31, lane32 == 0
    add = lambda values: functools.reduce(lambda a, b: a + b, values)

    def update(i, carry):
        x = i + x0
        at = pl.ds(pl.multiple_of(i * 8, 8), 8)
        done = [[None] * QUADS for _ in range(PAIRS + 1)]
        for j in range(QUADS):

            def around(ref, lead, layer):
                q = pl.multiple_of(layer * SPAN, 8)
                here = pl.ds(q + 4, 8)
                return (
                    ref[lead + (j, here)],
                    ref[lead + (j, pl.ds(q + 4 + SPAN, 8))],
                    ref[lead + (j, pl.ds(q + 4 - SPAN, 8))],
                    ref[lead + (j + 1, here)] if j < 3 else ref[lead + (0, pl.ds(q + 5, 8))],
                    ref[lead + (j - 1, here)] if j > 0 else ref[lead + (3, pl.ds(q + 3, 8))],
                )

            def all_around(ref, lead, k):
                c, *near = around(ref, lead, i + 1)
                z = zw[k, j, at, :]
                return c, near + [jnp.where(top, z, roll(c, -1)), jnp.where(bottom, z, roll(c, 1))]

            w, near_w = all_around(we, (), PAIRS)
            u = ud[j, pl.ds(pl.multiple_of(x * 8, 8), 8), :]
            phi, *near_phi = around(fd, (), x + 1)
            near_phi += [jnp.where(even, roll(u, -17), roll(u, 15)), jnp.where(even, roll(u, -15), roll(u, 17))]
            drift = [near_w[d] * (phi - near_phi[d]) for d in range(6)]
            w_total, d_total = add(near_w), add(drift)
            conc = []
            for k in range(PAIRS):
                c, near_c = all_around(se, (k,), k)
                spread_w = add([near_w[d] * near_c[d] for d in range(6)])
                spread_d = add([drift[d] * near_c[d] for d in range(6)])
                outflow = w * ((c * w_total - spread_w) + half_charge[k] * (c * d_total + spread_d))
                conc.append(c)
                done[k][j] = c - rates[k] * outflow
            reaction = conc[2] - conc[0] * conc[1] / solubility
            reaction = jnp.where(w > 0, reactivity * reaction, 0.0)
            for k in range(PAIRS):
                done[k][j] = done[k][j] + signs[k] * reaction
            done[PAIRS][j] = phi
        for k in range(PAIRS + 1):
            native = swap_groups(done[k], lane)
            for f in range(2 if k < PAIRS else 1):
                ion = k + f * PAIRS if k < PAIRS else 2 * PAIRS
                send[ion, at, :] = jnp.where(given == 0, native[f], native[2 + f])
                keep[ion, at, :] = jnp.where(given == 0, native[2 + f], native[f])
        return carry

    lax.fori_loop(0, HALF, update, 0, unroll=2)


def place_kernel(give_slot, *refs):
    keep, received, (new_sp, new_pot) = refs[:2], refs[2:4], refs[4:]
    given = give_slot[0]
    ions = new_sp.shape[0]
    for half in range(2):
        rows = [pl.ds(half * PLANE + slot, PLANE // 2, stride=2) for slot in (given, 1 - given)]
        for i in range(ions):
            new_sp[i, rows[0], :] = received[half][i]
            new_sp[i, rows[1], :] = keep[half][i]
        new_pot[rows[0], :] = received[half][ions]
        new_pot[rows[1], :] = keep[half][ions]


VMEM = pl.BlockSpec(memory_space=pltpu.VMEM)
SMEM = pl.BlockSpec(memory_space=pltpu.SMEM)
ANY = pl.BlockSpec(memory_space=pl.ANY)
HBM = pl.BlockSpec(memory_space=pltpu.HBM)
MIB = 1024 * 1024


def grant(mib):
    return pltpu.CompilerParams(vmem_limit_bytes=mib * MIB)


def f32(*shape):
    return jax.ShapeDtypeStruct(shape, jnp.float32)


def rows_of(field):
    lead = field.shape[:-2]
    bricks, cells = field.shape[-2:]
    split = field.reshape(lead + (bricks, cells // LANES, LANES))
    return jnp.swapaxes(split, -3, -2).reshape(lead + (bricks * cells // LANES, LANES))


def cells_of(rows):
    lead = rows.shape[:-2]
    count, lanes = rows.shape[-2:]
    split = rows.reshape(lead + (count // 2, 2, lanes))
    return jnp.swapaxes(split, -3, -2).reshape(lead + (2, count // 2 * lanes))


def moved(block, axis, offset):
    n = lax.axis_size(axis)
    return lax.ppermute(block, axis, [(i, (i + offset) % n) for i in range(n)])


def local(
    species,
    potential,
    pore,
    openness,
    neighbours,
    diffusivity,
    rate_const,
    opened,
    partner,
    give_slot,
):
    ion_count, brick_count, cells = species.shape
    dev_count = lax.axis_size("dev")
    stride = dev_count // 4

    held = {}
    for sx, sy in SIDES + CORNERS:
        offset = (sx + sy * stride) % dev_count
        offset = offset if offset <= dev_count // 2 else offset - dev_count
        rows, pieces = held.get(offset, (0, ()))
        held[offset] = (rows + (Y_ROWS if 0 in (sx, sy) else EDGE_ROWS), pieces + (((sx, sy), rows),))
    offsets = sorted(held, key=lambda o: (-held[o][0], -abs(o), o))
    pieces = tuple(held[o][1] for o in offsets)

    with_face = [k for k, o in enumerate(offsets) if held[o][0] >= Y_ROWS]
    alone = [k for k in range(len(offsets)) if k not in with_face]
    rows = brick_count * PLANE
    species_rows, pore_rows, openness_rows = rows_of(species), rows_of(pore), rows_of(openness)
    field = pltpu.VMEM((rows, LANES), jnp.float32)
    field_int = pltpu.VMEM((rows, LANES), jnp.int32)
    fields = pltpu.VMEM((ion_count, rows, LANES), jnp.float32)
    pd, own, *blocks, down, up = pl.pallas_call(
        functools.partial(pack_kernel, pieces),
        out_shape=(
            f32(QUADS, PLANE, LANES),
            f32(8, LANES),
            *(f32(held[o][0], LANES) for o in offsets),
            f32(ZC_ROWS, LANES),
            f32(ZC_ROWS, LANES),
        ),
        in_specs=[HBM] * 4 + [SMEM],
        out_specs=tuple([VMEM] * (4 + len(offsets))),
        scratch_shapes=[fields, field, field_int, field, pltpu.SemaphoreType.DMA((PARTS, 3, 4))],
        compiler_params=grant(60),
        name="pack",
    )(species_rows, rows_of(potential), pore_rows, openness_rows, neighbours)
    faces = [k for k, o in enumerate(offsets) if held[o][0] >= Y_ROWS]
    lone = [k for k in range(len(offsets)) if k not in faces]
    rest = faces[-1:] + lone[1:]
    zup = moved(down, "group", -1)
    arrived = {k: moved(blocks[k], "dev", offsets[k]) for k in faces[:-1] + lone[:1]}

    sp, wd = pl.pallas_call(
        ions_kernel,
        out_shape=(f32(PAIRS, QUADS, PLANE, LANES), f32(QUADS, PLANE, LANES)),
        in_specs=[HBM] * 3,
        out_specs=(VMEM,) * 2,
        scratch_shapes=[fields, field_int, field, pltpu.SemaphoreType.DMA((2, 3))],
        compiler_params=grant(60),
        name="ions",
    )(species_rows, pore_rows, openness_rows)

    zup, up, sp, wd, *more = lax.optimization_barrier((zup, up, sp, wd, *(blocks[k] for k in rest)))
    arrived.update((k, moved(block, "dev", offsets[k])) for k, block in zip(rest, more))
    zdn = moved(up, "group", 1)

    zdown, zupper = pl.pallas_call(
        ion_z_kernel,
        out_shape=(f32(ION_ROWS, LANES),) * 2,
        in_specs=[VMEM] * 2,
        out_specs=(VMEM,) * 2,
        compiler_params=grant(8),
        name="ion_z_faces",
    )(sp, wd)

    arrived = [arrived[k] for k in range(len(offsets))]

    zl, zh = pl.pallas_call(
        functools.partial(relay_kernel, pieces),
        out_shape=(f32(ZH_ROWS, LANES),) * 2,
        in_specs=[VMEM] * len(offsets) + [ANY] + [VMEM] * 2,
        out_specs=(VMEM, VMEM),
        compiler_params=grant(6),
        name="relay",
    )(*arrived, zdn, zdown, zupper)
    zhup = moved(zl, "group", -1)
    zhdn = moved(zh, "group", 1)
    wide = pltpu.VMEM((QUADS, EXT * SPAN + 2 * PAD, LANES), jnp.float32)
    by_layer = lambda a: a.reshape(a.shape[:-2] + (SIDE, YQ, LANES))
    sp, wd = by_layer(sp), by_layer(wd)
    scalars = (diffusivity, rate_const, opened, give_slot)
    half_out = (f32(ion_count + 1, PLANE // 2, LANES),) * 2
    half_scratch = [
        pltpu.VMEM((PAIRS, QUADS, HALF + 2, SPAN, LANES), jnp.float32),
        pltpu.VMEM((QUADS, HALF + 2, SPAN, LANES), jnp.float32),
        pltpu.VMEM((FIELDS, QUADS, PLANE // 2, LANES), jnp.float32),
    ]
    sources = (own, pd, zup, zdn, zhup, zhdn, *arrived)
    ud, fd, *first_half = pl.pallas_call(
        functools.partial(sweep_kernel, pieces),
        out_shape=(f32(QUADS, PLANE, LANES), f32(QUADS, NEAR * SPAN, LANES), *half_out),
        in_specs=[HBM] * (len(sources) + 2) + [SMEM] * 4,
        out_specs=(HBM, HBM, VMEM, VMEM),
        scratch_shapes=[
            wide,
            wide,
            wide,
            pltpu.VMEM((2, SPAN, LANES), jnp.float32),
            pltpu.VMEM((3, SPAN, LANES), jnp.float32),
            pltpu.VMEM((3, SPAN, LANES), jnp.float32),
            *half_scratch,
            pltpu.VMEM((QUADS, PLANE, LANES), jnp.float32),
            pltpu.VMEM((QUADS, NEAR * SPAN, LANES), jnp.float32),
            pltpu.SemaphoreType.DMA((len(sources),)),
            pltpu.SemaphoreType.DMA((FIELDS,)),
            pltpu.SemaphoreType.DMA((2,)),
            *(pltpu.VMEM(a.shape, jnp.float32) for a in sources),
        ],
        compiler_params=grant(60),
        name="sweeps",
    )(*sources, sp, wd, *scalars)

    def second_half():
        halos, starts = [], []
        for way in ((1, 0), (-1, 0), (0, 1), (0, -1)):
            for k, parts in enumerate(pieces):
                for name, start in parts:
                    if name == way:
                        halos.append(arrived[k])
                        starts.append(start + Y_ION)
        sources = (own, *halos, zhup, zhdn, ud, fd)
        return pl.pallas_call(
            functools.partial(update_kernel, 1, starts),
            out_shape=half_out,
            in_specs=[HBM] * (len(sources) + 2) + [SMEM] * 4,
            out_specs=(VMEM, VMEM),
            scratch_shapes=[
                *half_scratch,
                pltpu.SemaphoreType.DMA((FIELDS + len(sources),)),
                *(pltpu.VMEM(a.shape, jnp.float32) for a in sources),
            ],
            compiler_params=grant(32),
            name="update",
        )(sp, wd, *sources, *scalars)

    def placed(kept, received):
        new_sp, new_pot = pl.pallas_call(
            place_kernel,
            out_shape=(f32(ion_count, rows, LANES), f32(rows, LANES)),
            in_specs=[SMEM] + [VMEM] * 4,
            out_specs=(VMEM, VMEM),
            compiler_params=grant(8),
            name="place",
        )(give_slot, *kept, *received)
        return cells_of(new_sp), cells_of(new_pot)

    def finished(route):
        across = lambda block: block if route is None else lax.ppermute(block, ("group", "dev"), route)
        keep, send = first_half
        keep_more, send_more = second_half()
        return placed((keep, keep_more), (across(send), across(send_more)))

    total = lax.axis_size("group") * dev_count
    own_index = lax.axis_index("group") * dev_count + lax.axis_index("dev")
    apart = jnp.bitwise_xor(own_index, partner[0])
    branch = jnp.int32(0)
    branches = [lambda: finished(None)]
    for bit in range(total.bit_length() - 1):
        route = [(i, i ^ (1 << bit)) for i in range(total)]
        branch = jnp.where(apart == (1 << bit), bit + 1, branch)
        branches.append(lambda route=route: finished(route))
    return lax.switch(branch, branches)


def solution(mesh):
    in_specs = (
        P(None, ("group", "dev"), None),
        P(("group", "dev"), None),
        P(("group", "dev"), None),
        P(("group", "dev"), None),
        P(("group", "dev"), None),
        P(),
        P(("group", "dev")),
        P(("group", "dev")),
        P(("group", "dev")),
        P(("group", "dev")),
    )
    out_specs = (P(None, ("group", "dev"), None), P(("group", "dev"), None))
    return jax.shard_map(local, mesh=mesh, in_specs=in_specs, out_specs=out_specs, check_vma=False)
```

```python
import functools

import jax
import jax.numpy as jnp
from jax import lax
from jax.experimental import pallas as pl
from jax.experimental.pallas import tpu as pltpu
from jax.sharding import PartitionSpec as P


SWEEPS = 8
DEPTH = SWEEPS + 1
LANES = 128

charge_scale = 0.5
screening = 0.5
solubility = 2.0
valences = (2.0, -1.0, 1.0, -1.0, 1.0, 2.0)
reaction_signs = (1.0, 1.0, -1.0, 0.0, 0.0, 0.0)

SIDE = 32
QUADS = 4
YQ = SIDE // QUADS
PAIRS = 3
PLANE = SIDE * YQ
HALF = SIDE // 2

FACE_TBL = DEPTH * SIDE
Y_ION = FACE_TBL + 8
EDGE_TBL = 64
EDGE_ROWS = EDGE_TBL + 8
THIRD = 11
ZC_TBL = QUADS * THIRD * YQ
ZC_ROWS = ZC_TBL + 8
ZH_EDGE = 2 * 3 * SIDE
ZH_TBL = ZH_EDGE + 64
ZH_ION = ZH_TBL + 32
FIELDS = PAIRS + 1
ION_ROWS = FIELDS * SIDE
Y_ROWS = Y_ION + ION_ROWS
BLOCKS = SIDE // FIELDS
ZH_ROWS = ZH_ION + ION_ROWS

ZH_PLACE = {
    (n, l): (n, off) if l < 5 else (2, 6 * n + off)
    for n in range(2)
    for l, off in enumerate((0, 8, 15, 21, 26, 0, 3, 5))
}

SIDES = ((-1, 0), (1, 0), (0, -1), (0, 1))
CORNERS = ((-1, -1), (-1, 1), (1, -1), (1, 1))
SPAN = 16
EXT = SIDE + 2 * DEPTH
MIDDLE = 15
PARTS = 3
PART = 4
NEAR = SIDE + 2
PAD = 24


def x_way(s):
    return 0 if s > 0 else 1


def y_way(s):
    return 2 if s > 0 else 3


def z_way(s):
    return 4 if s > 0 else 5


def roll(v, shift):
    shift = shift % LANES
    return v if shift == 0 else pltpu.roll(v, shift, 1)


def lane_of(rows):
    return lax.broadcasted_iota(jnp.int32, (rows, LANES), 1)


def swap_groups(v, lane):
    low = lane < 64
    a0 = jnp.where(low, v[0], roll(v[2], 64))
    a2 = jnp.where(low, roll(v[0], 64), v[2])
    a1 = jnp.where(low, v[1], roll(v[3], 64))
    a3 = jnp.where(low, roll(v[1], 64), v[3])
    even = (lane & 32) == 0
    return (
        jnp.where(even, a0, roll(a1, 32)),
        jnp.where(even, roll(a0, 96), a1),
        jnp.where(even, a2, roll(a3, 32)),
        jnp.where(even, roll(a2, 96), a3),
    )


def sign_rows(neighbours):
    row = lax.broadcasted_iota(jnp.int32, (8, LANES), 0)
    table = jnp.zeros((8, LANES), jnp.float32)
    for way in range(6):
        table = jnp.where(row == way, jnp.where(neighbours[0, way] == 0, 1.0, -1.0), table)
    return table


def pack_kernel(pieces, species_in, potential_in, pore_in, openness_in, neighbours, pd, own, *rest):
    n_out = len(pieces)
    outs, (zlo, zhi) = rest[:n_out], rest[n_out : n_out + 2]
    species, potential, pore, openness, sems = rest[n_out + 2 :]
    parts = []
    for part in range(PARTS):
        copies = []
        for c in range(3):
            x0 = c * THIRD + part * PART
            count = min(PART, (c + 1) * THIRD - x0, SIDE - x0)
            rows = pl.ds(x0 * 16, count * 16)
            for number, (src, dst) in enumerate(
                ((species_in, species), (potential_in, potential), (pore_in, pore), (openness_in, openness))
            ):
                at = (slice(None), rows) if number == 0 else (rows,)
                copies.append(pltpu.make_async_copy(src.at[at], dst.at[at], sems.at[part, c, number]))
                copies[-1].start()
        parts.append(copies)
    where = {name: (outs[k], base) for k, held in enumerate(pieces) for name, base in held}
    lane = lane_of(8)
    lane32 = lane & 31
    low = lane < 64
    table = sign_rows(neighbours)
    own[...] = table

    def planes_of(x):
        d, p = [], []
        for b in range(2):
            rows = pl.ds(x * 16 + b, 8, stride=2)
            total = valences[0] * species[0, rows, :]
            for i in range(1, 2 * PAIRS):
                total = total + valences[i] * species[i, rows, :]
            wet = pore[rows, :].astype(jnp.float32) * openness[rows, :]
            d.append(charge_scale * wet * total)
            p.append(potential[rows, :])
        mixed = []
        for v in swap_groups((p[0], d[0], p[1], d[1]), lane):
            r = roll(v, 64)
            mixed.append(jnp.where(low, v + r, r - v))
        at = pl.ds(pl.multiple_of(x * 8, 8), 8)
        for j in range(QUADS):
            pd[j, at, :] = mixed[j]
        return mixed

    def step(i, blocks=3):
        planes = [planes_of(i + c * THIRD) for c in range(blocks)]
        for j in range(QUADS):
            at = pl.ds(pl.multiple_of((j * THIRD + i) * 8, 8), 8)
            lo = hi = planes[0][j]
            for c in range(1, blocks):
                lo = jnp.where(lane32 >= DEPTH * c, roll(planes[c][j], DEPTH * c), lo)
                hi = jnp.where(lane32 < SIDE - DEPTH * c, roll(planes[c][j], -DEPTH * c), hi)
            zlo[at, :] = lo
            zhi[at, :] = hi

    for part in range(PARTS):
        for c in parts[part]:
            c.wait()
        end = min((part + 1) * PART, THIRD - 1)
        lax.fori_loop(part * PART, end, lambda i, carry: (step(i), carry)[1], 0, unroll=True)
    step(THIRD - 1, 2)

    zlo[ZC_TBL:, :] = table
    zhi[ZC_TBL:, :] = table

    def ion_planes(x, ref, start):
        for k, planes in enumerate(dense_ions(species, pore, openness, x, lane)):
            for j in range(QUADS):
                ref[start + k * SIDE + j * 8 : start + k * SIDE + j * 8 + 8, :] = planes[j]

    group = lane_of(SIDE) >> 5

    def ion_rows(y, ref, start):
        for k in range(FIELDS):
            v = jnp.zeros((SIDE, LANES), jnp.float32)
            for b in range(2):
                rows = pl.ds(y // 4 * 2 + b, SIDE, stride=16)
                if k == PAIRS:
                    wet = pore[rows, :].astype(jnp.float32) * openness[rows, :]
                for f in range(2):
                    native = species[k + f * PAIRS, rows, :] if k < PAIRS else wet
                    v = jnp.where(group == 2 * b + f, roll(native, (2 * b + f - y % 4) * SIDE), v)
            ref[start + k * SIDE : start + (k + 1) * SIDE, :] = v

    for sx, sy in SIDES:
        ref, base = where[(sx, sy)]
        for l in range(DEPTH):
            if sx:
                x = l if sx < 0 else SIDE - 1 - l
                for j in range(QUADS):
                    ref[base + l * SIDE + j * 8 : base + l * SIDE + j * 8 + 8, :] = pd[j, x * 8 : x * 8 + 8, :]
            else:
                y = l if sy < 0 else SIDE - 1 - l
                ref[base + l * SIDE : base + (l + 1) * SIDE, :] = pd[y % 4, pl.ds(y // 4, SIDE, stride=8), :]
        ref[base + FACE_TBL : base + Y_ION, :] = table
        if sx:
            ion_planes(0 if sx < 0 else SIDE - 1, ref, base + Y_ION)
        else:
            ion_rows(0 if sy < 0 else SIDE - 1, ref, base + Y_ION)
    for sx, sy in CORNERS:
        ref, base = where[(sx, sy)]
        x0 = 0 if sx < 0 else SIDE - 8
        for m in range(8):
            y = m if sy < 0 else SIDE - 8 + m
            ref[base + m * 8 : base + m * 8 + 8, :] = pd[y % 4, pl.ds(x0 * 8 + y // 4, 8, stride=8), :]
        ref[base + EDGE_TBL : base + EDGE_ROWS, :] = table


def dense_ions(species, pore, openness, x, lane):
    rows = [pl.ds(x * 16 + b, 8, stride=2) for b in range(2)]
    w = [pore[rows[b], :].astype(jnp.float32) * openness[rows[b], :] for b in range(2)]
    s = [[species[n, rows[b], :] for b in range(2)] for n in range(2 * PAIRS)]
    fields = [swap_groups((s[k][0], s[k + PAIRS][0], s[k][1], s[k + PAIRS][1]), lane) for k in range(PAIRS)]
    return fields + [swap_groups((w[0], w[0], w[1], w[1]), lane)]


def ions_kernel(species_in, pore_in, openness_in, sp, wd, species, pore, openness, sems):
    parts = []
    for part in range(2):
        rows = pl.ds(part * PLANE, PLANE)
        copies = [
            pltpu.make_async_copy(species_in.at[:, rows], species.at[:, rows], sems.at[part, 0]),
            pltpu.make_async_copy(pore_in.at[rows], pore.at[rows], sems.at[part, 1]),
            pltpu.make_async_copy(openness_in.at[rows], openness.at[rows], sems.at[part, 2]),
        ]
        for c in copies:
            c.start()
        parts.append(copies)
    lane = lane_of(8)

    def step(x, carry):
        at = pl.ds(pl.multiple_of(x * 8, 8), 8)
        for k, planes in enumerate(dense_ions(species, pore, openness, x, lane)):
            for j in range(QUADS):
                if k < PAIRS:
                    sp[k, j, at, :] = planes[j]
                else:
                    wd[j, at, :] = planes[j]
        return carry

    for part in range(2):
        for c in parts[part]:
            c.wait()
        lax.fori_loop(part * HALF, (part + 1) * HALF, step, 0, unroll=2)


def ion_z_kernel(sp, wd, zlo, zhi):
    lane32 = lane_of(8) & 31

    def step(i, carry):
        for j in range(QUADS):
            lo = hi = jnp.zeros((8, LANES), jnp.float32)
            for spot in range(SIDE):
                block, k = spot // FIELDS, spot % FIELDS
                at = pl.ds(pl.multiple_of((i + block * FIELDS) * 8, 8), 8)
                v = sp[k, j, at, :] if k < PAIRS else wd[j, at, :]
                lo = jnp.where(lane32 == spot, roll(v, spot), lo)
                hi = jnp.where(lane32 == spot, roll(v, spot - 31), hi)
            zat = pl.ds(pl.multiple_of(j * SIDE + i * 8, 8), 8)
            zlo[zat, :] = lo
            zhi[zat, :] = hi
        return carry

    lax.fori_loop(0, FIELDS, step, 0)


def relay_kernel(pieces, *refs):
    arrived, (ions_lo, ions_hi, zl, zh) = refs[:-5], refs[-4:]
    zl[ZH_ION:, :] = ions_lo[...]
    zh[ZH_ION:, :] = ions_hi[...]
    where = {name: (arrived[k], base) for k, held in enumerate(pieces) for name, base in held}
    lane32 = lane_of(SIDE) & 31
    for axis in range(2):
        lo = [jnp.zeros((SIDE, LANES), jnp.float32)] * 3
        hi = [jnp.zeros((SIDE, LANES), jnp.float32)] * 3
        for n in range(2):
            sx, sy = SIDES[2 * axis + n]
            ref, base = where[(-sx, -sy)]
            for l in range(8):
                block, off = ZH_PLACE[n, l]
                width = 8 - l
                v = ref[base + l * SIDE : base + (l + 1) * SIDE, :]
                lo[block] = jnp.where((lane32 >= off) & (lane32 < off + width), roll(v, off), lo[block])
                hi[block] = jnp.where((lane32 <= 31 - off) & (lane32 > 31 - off - width), roll(v, -off), hi[block])
            at = slice(ZH_TBL + (2 * axis + n) * 8, ZH_TBL + (2 * axis + n) * 8 + 8)
            zl[at, :] = ref[base + FACE_TBL : base + Y_ION, :]
            zh[at, :] = ref[base + FACE_TBL : base + Y_ION, :]
        for block in range(3):
            at = slice((axis * 3 + block) * SIDE, (axis * 3 + block + 1) * SIDE)
            zl[at, :] = lo[block]
            zh[at, :] = hi[block]
    group = lane_of(64) & 31
    lo = jnp.zeros((64, LANES), jnp.float32)
    hi = lo
    for number, (sx, sy) in enumerate(CORNERS):
        ref, base = where[(-sx, -sy)]
        v = ref[base : base + EDGE_TBL, :]
        lo = jnp.where((group >= 8 * number) & (group < 8 * number + 8), roll(v, 8 * number), lo)
        hi = jnp.where((group <= 31 - 8 * number) & (group > 23 - 8 * number), roll(v, -8 * number), hi)
    zl[ZH_EDGE : ZH_EDGE + 64, :] = lo
    zh[ZH_EDGE : ZH_EDGE + 64, :] = hi


def sweep_kernel(pieces, *refs):
    n_in = 6 + len(pieces)
    sources, (sp, wd), scalars = refs[:n_in], refs[n_in : n_in + 2], refs[n_in + 2 : n_in + 6]
    ud, fd, keep, send = refs[n_in + 6 : n_in + 10]
    ua, ub, dn, mx, myp, mym, se_cube, we_cube, zw, udv, fdv, sems, ion_sems, out_sems = refs[n_in + 10 : n_in + 24]
    held = refs[n_in + 24 :]
    copies = [pltpu.make_async_copy(src, dst, sems.at[i]) for i, (src, dst) in enumerate(zip(sources, held))]
    for c in copies:
        c.start()
    late = ion_copies(0, sp, wd, se_cube, we_cube, ion_sems)
    for c in late:
        c.start()
    own, pd, zup, zdn, zhup, zhdn = held[:6]
    arrived = held[6:]
    where = {name: (arrived[k], base) for k, held in enumerate(pieces) for name, base in held}

    lane = lane_of(8)
    lane64 = lane & 63
    low = lane < 64
    core = (lane64 >= 16) & (lane64 < 48)
    upper = lane64 >= 48

    for c in copies[:4]:
        c.wait()
    def sign(held, way):
        return jnp.broadcast_to(held[way : way + 1, :], (8, LANES))

    outer = {}

    def outward(key, held):
        m = jnp.where(upper, sign(held, 4), sign(held, 5))
        outer[key] = jnp.where(low, 1.0, m)

    outward((0, 0), own)

    def spread(v, zu, zd, shift_u, shift_d, key):
        rows = v.shape[0]
        tall = lambda a: a if rows == 8 else jnp.concatenate([a] * (rows // 8), axis=0)
        if zu is None:
            return roll(v, 16), roll(v, -16)
        m, c, u = tall(outer[key]), tall(core), tall(upper)
        pot = jnp.where(u, roll(zu, 48 + shift_u), roll(zd, -16 + shift_d)) * m
        rho = jnp.where(u, roll(zu, 16 + shift_u), roll(zd, -48 + shift_d)) * m
        return jnp.where(c, roll(v, 16), pot), jnp.where(c, roll(v, -16), rho)

    def fill(i, c):
        x = i + c * THIRD
        at = pl.ds(pl.multiple_of(x * 8, 8), 8)
        to = pl.ds(pl.multiple_of(PAD + (x + DEPTH) * SPAN + 4, 4), 8)
        for j in range(QUADS):
            zat = pl.ds(pl.multiple_of((j * THIRD + i) * 8, 8), 8)
            pot, rho = spread(pd[j, at, :], zup[zat, :], zdn[zat, :], -DEPTH * c, DEPTH * c, (0, 0))
            ua[j, to, :] = pot
            dn[j, to, :] = rho

    def fill_three(i, carry):
        for c in range(3):
            fill(i, c)
        return carry

    lax.fori_loop(0, THIRD - 1, fill_three, 0, unroll=2)
    fill(THIRD - 1, 0)
    fill(THIRD - 1, 1)

    for c in copies[4:]:
        c.wait()
    table = {(0, 0): own[...]}
    ztable = {1: {(0, 0): zup[ZC_TBL:, :]}, -1: {(0, 0): zdn[ZC_TBL:, :]}}
    for number, (sx, sy) in enumerate(SIDES):
        ref, base = where[(-sx, -sy)]
        table[(sx, sy)] = ref[base + FACE_TBL : base + Y_ION, :]
        for sz, held in ((1, zhup), (-1, zhdn)):
            ztable[sz][(sx, sy)] = held[ZH_TBL + number * 8 : ZH_TBL + number * 8 + 8, :]
    for sx, sy in CORNERS:
        ref, base = where[(-sx, -sy)]
        table[(sx, sy)] = ref[base + EDGE_TBL : base + EDGE_ROWS, :]

    def crossing(way, here, there):
        level = sign(table[here], way)
        beyond = {}
        for sz in (1, -1):
            z = z_way(sz)
            beyond[sz] = sign(ztable[sz][here], way) * sign(table[here], z) * sign(table[there], z)
        m = jnp.where(core, level, jnp.where(upper, beyond[1], beyond[-1]))
        return jnp.where(low, 1.0, m)

    for key, held_table in table.items():
        outward(key, held_table)

    row8 = lax.broadcasted_iota(jnp.int32, (8, LANES), 0)
    one = jnp.ones((8, LANES), jnp.float32)
    for number, sx in enumerate((-1, 1)):
        m = {sy: crossing(x_way(sx), (0, sy), (sx, sy)) for sy in (-1, 0, 1)}
        mx[number, 0:8, :] = jnp.where(row8 < 4, m[-1], m[0])
        mx[number, 8:16, :] = jnp.where(row8 < 4, m[0], m[1])
    y_sign = {}
    for number, sx in enumerate((-1, 0, 1)):
        m = {sy: crossing(y_way(sy), (sx, 0), (sx, sy)) for sy in (-1, 1)}
        y_sign[sx] = m
        myp[number, 0:8, :] = jnp.where(row8 == 3, m[-1], one)
        myp[number, 8:16, :] = jnp.where(row8 == 3, m[1], one)
        mym[number, 0:8, :] = jnp.where(row8 == 4, m[-1], one)
        mym[number, 8:16, :] = jnp.where(row8 == 4, m[1], one)

    for number, (sx, sy) in enumerate(SIDES):
        ref, base = where[(-sx, -sy)]
        for l in range(DEPTH):
            v = ref[base + l * SIDE : base + (l + 1) * SIDE, :]
            zu = zd = None
            off = 0
            if l < 8:
                block, off = ZH_PLACE[number % 2, l]
                block += number // 2 * 3
                at = slice(block * SIDE, (block + 1) * SIDE)
                zu, zd = zhup[at, :], zhdn[at, :]
            pot, rho = spread(v, zu, zd, -off, off, (sx, sy))
            if sx:
                x = SIDE + l if sx > 0 else -1 - l
                start = PAD + (x + DEPTH) * SPAN + 4
                for j in range(QUADS):
                    ua[j, start : start + 8, :] = pot[j * 8 : j * 8 + 8]
                    dn[j, start : start + 8, :] = rho[j * 8 : j * 8 + 8]
            else:
                j = l % 4 if sy > 0 else 3 - l % 4
                row = 12 + l // 4 if sy > 0 else 3 - l // 4
                at = pl.ds(PAD + DEPTH * SPAN + row, SIDE, stride=SPAN)
                ua[j, at, :] = pot
                dn[j, at, :] = rho
    for number, (sx, sy) in enumerate(CORNERS):
        ref, base = where[(-sx, -sy)]
        for m in range(8):
            v = ref[base + m * 8 : base + m * 8 + 8, :]
            at = slice(ZH_EDGE + m * 8, ZH_EDGE + m * 8 + 8)
            pot, rho = spread(v, zhup[at, :], zhdn[at, :], -8 * number, 8 * number, (sx, sy))
            row = (12 if sy > 0 else 2) + m // 4
            x = SIDE if sx > 0 else -8
            to = pl.ds(PAD + (x + DEPTH) * SPAN + row, 8, stride=SPAN)
            ua[m % 4, to, :] = pot
            dn[m % 4, to, :] = rho

    scale = 1.0 / (6.0 + screening)

    def slab(src, dst, x, sx, before=None, after=None):
        r = PAD + (x + DEPTH) * SPAN
        r = r if isinstance(x, int) else pl.multiple_of(r, 8)
        at = pl.ds(r, SPAN)
        c = [src[j, at, :] for j in range(QUADS)]
        for j in range(QUADS):
            left = src[j, pl.ds(r - SPAN, SPAN), :]
            right = src[j, pl.ds(r + SPAN, SPAN), :]
            if before is not None:
                left = left * mx[before]
            if after is not None:
                right = right * mx[after]
            north = c[j + 1] if j < 3 else src[0, pl.ds(r + 1, SPAN), :] * myp[sx + 1]
            south = c[j - 1] if j > 0 else src[3, pl.ds(r - 1, SPAN), :] * mym[sx + 1]
            total = (left + right) + (north + south) + (roll(c[j], 1) + roll(c[j], -1)) + dn[j, at, :]
            dst[j, at, :] = total * scale

    def sweep(src, dst, t):
        def middle(i, carry):
            for n in range(MIDDLE):
                slab(src, dst, 1 + i * MIDDLE + n, 0)
            return carry

        lax.fori_loop(0, (SIDE - 2) // MIDDLE, middle, 0)
        slab(src, dst, -1, -1, after=0)
        slab(src, dst, 0, 0, before=0)
        slab(src, dst, SIDE - 1, 0, after=1)
        slab(src, dst, SIDE, 1, before=1)
        for n in range(DEPTH - t - 1):
            slab(src, dst, -2 - n, -1)
            slab(src, dst, SIDE + 1 + n, 1)

    for t in range(1, SWEEPS + 1):
        sweep(*((ua, ub) if t % 2 else (ub, ua)), t)

    lane16 = lane_of(SPAN)
    first = (lane16 & 32) == 0
    row16 = lax.broadcasted_iota(jnp.int32, (SPAN, LANES), 0)

    def slots(v, m):
        wide_lane = lane_of(v.shape[0])
        c = v * m
        r = roll(c, 64)
        u = 0.5 * jnp.where(wide_lane < 64, c + r, r - c)
        return u, jnp.where((wide_lane & 32) == 0, roll(u, -16), roll(u, 16))

    def rows_at(x):
        return pl.ds(PAD + (x + DEPTH) * SPAN + 4, 8), pl.ds((x + 1) * SPAN + 4, 8)

    for x, number in ((-1, 0), (SIDE, 1)):
        at, near = rows_at(x)
        for j in range(QUADS):
            fdv[j, near, :] = slots(ua[j, at, :], mx[number, 4:12, :])[1]
    for j, row, sy in ((0, 12, 1), (3, 3, -1)):
        v = ua[j, pl.ds(PAD + DEPTH * SPAN + row, SIDE, stride=SPAN), :]
        m = jnp.concatenate([y_sign[0][sy]] * (SIDE // 8), axis=0)
        fdv[j, pl.ds(SPAN + row, SIDE, stride=SPAN), :] = slots(v, m)[1]

    def all_slots(i, carry):
        for n in range(4):
            x = 4 * i + n
            at, near = rows_at(x)
            for j in range(QUADS):
                u, dense = slots(ua[j, at, :], one)
                udv[j, pl.ds(pl.multiple_of(x * 8, 8), 8), :] = u
                fdv[j, near, :] = dense
        return carry

    lax.fori_loop(0, SIDE // 4, all_slots, 0)
    back = [pltpu.make_async_copy(udv, ud, out_sems.at[0]), pltpu.make_async_copy(fdv, fd, out_sems.at[1])]
    for c in back:
        c.start()
    for c in late:
        c.wait()
    halos = [(ref, start + Y_ION) for ref, start in (where[(1, 0)], where[(-1, 0)], where[(0, 1)], where[(0, -1)])]
    update_half(0, se_cube, we_cube, zw, own, *halos, zhup, zhdn, udv, fdv, *scalars, keep, send)
    for c in back:
        c.wait()


def ion_copies(half, sp, wd, se_cube, we_cube, sems):
    first, skip = (0, 1) if half == 0 else (half * HALF - 1, 0)
    at, to = pl.ds(first, HALF + 1), (pl.ds(skip, HALF + 1), pl.ds(4, YQ))
    copies = [pltpu.make_async_copy(sp.at[k, :, at], se_cube.at[(k, slice(None), *to)], sems.at[k]) for k in range(PAIRS)]
    copies.append(pltpu.make_async_copy(wd.at[:, at], we_cube.at[(slice(None), *to)], sems.at[PAIRS]))
    return copies


def update_kernel(half, starts, sp, wd, *refs):
    sources, scalars, outs = refs[:9], refs[9:13], refs[13:15]
    se_cube, we_cube, zw, sems = refs[15:19]
    held = refs[19:]
    copies = ion_copies(half, sp, wd, se_cube, we_cube, sems)
    copies += [pltpu.make_async_copy(src, dst, sems.at[FIELDS + n]) for n, (src, dst) in enumerate(zip(sources, held))]
    for c in copies:
        c.start()
    for c in copies:
        c.wait()
    own, *others = held
    halos = list(zip(others[:4], starts))
    update_half(half, se_cube, we_cube, zw, own, *halos, *others[4:], *scalars, *outs)


def update_half(
    half,
    se_cube,
    we_cube,
    zw,
    own,
    xdn,
    xup,
    ydn,
    yup,
    zup,
    zdn,
    ud,
    fd,
    diffusivity,
    rate_const,
    opened,
    give_slot,
    keep,
    send,
):
    x0 = half * HALF
    layers = HALF + 2
    se = se_cube.reshape(PAIRS, QUADS, layers * SPAN, LANES)
    we = we_cube.reshape(QUADS, layers * SPAN, LANES)

    lane = lane_of(8)
    lane32 = lane & 31
    low = lane < 64
    even = (lane & 32) == 0

    def turned(v, way):
        s = jnp.broadcast_to(own[way : way + 1, :], v.shape)
        return jnp.where(s > 0, v, roll(v, 64))

    def put(k, j, rows, v):
        if k < PAIRS:
            se[k, j, rows, :] = v
        else:
            we[j, rows, :] = v

    for k in range(FIELDS):
        (ref, start), way, layer = (xdn, 1, 0) if half == 0 else (xup, 0, layers - 1)
        v = turned(ref[start + k * SIDE : start + (k + 1) * SIDE, :], way)
        for j in range(QUADS):
            put(k, j, slice(layer * SPAN + 4, layer * SPAN + 12), v[j * 8 : j * 8 + 8])
        for j, row, way, (ref, start) in ((0, 12, 2, yup), (3, 3, 3, ydn)):
            rows = slice(start + k * SIDE + x0, start + k * SIDE + x0 + HALF)
            put(k, j, pl.ds(SPAN + row, HALF, stride=SPAN), turned(ref[rows, :], way))

    odd = (lane & 1) == 1
    for j in range(QUADS):
        for i in range(FIELDS):
            rows = slice(ZH_ION + j * SIDE + i * 8, ZH_ION + j * SIDE + i * 8 + 8)
            zu = turned(zup[rows, :], 4)
            zd = roll(turned(zdn[rows, :], 5), -31)
            both = (jnp.where(odd, zd, zu), jnp.where(odd, zu, zd))
            for c in range(BLOCKS // 2):
                spots = (c + half * (BLOCKS // 2)) * FIELDS
                x = c * FIELDS + i
                for k in range(FIELDS):
                    zw[k, j, x * 8 : x * 8 + 8, :] = roll(both[(spots + k) % 2], 31 - spots - k)

    def by_ion(values, k):
        return jnp.where(even, values[k], values[k + PAIRS])

    half_charge = [by_ion([0.5 * v for v in valences], k) for k in range(PAIRS)]
    rates = [by_ion([diffusivity[i] for i in range(2 * PAIRS)], k) for k in range(PAIRS)]
    signs = [by_ion(reaction_signs, k) for k in range(PAIRS)]
    reactivity = [rate_const[b] * opened[b].astype(jnp.float32) for b in range(2)]
    reactivity = jnp.where(low, reactivity[0], reactivity[1])
    given = give_slot[0]
    top, bottom = lane32 == 31, lane32 == 0
    add = lambda values: functools.reduce(lambda a, b: a + b, values)

    def update(i, carry):
        x = i + x0
        at = pl.ds(pl.multiple_of(i * 8, 8), 8)
        done = [[None] * QUADS for _ in range(PAIRS + 1)]
        for j in range(QUADS):

            def around(ref, lead, layer):
                q = pl.multiple_of(layer * SPAN, 8)
                here = pl.ds(q + 4, 8)
                return (
                    ref[lead + (j, here)],
                    ref[lead + (j, pl.ds(q + 4 + SPAN, 8))],
                    ref[lead + (j, pl.ds(q + 4 - SPAN, 8))],
                    ref[lead + (j + 1, here)] if j < 3 else ref[lead + (0, pl.ds(q + 5, 8))],
                    ref[lead + (j - 1, here)] if j > 0 else ref[lead + (3, pl.ds(q + 3, 8))],
                )

            def all_around(ref, lead, k):
                c, *near = around(ref, lead, i + 1)
                z = zw[k, j, at, :]
                return c, near + [jnp.where(top, z, roll(c, -1)), jnp.where(bottom, z, roll(c, 1))]

            w, near_w = all_around(we, (), PAIRS)
            u = ud[j, pl.ds(pl.multiple_of(x * 8, 8), 8), :]
            phi, *near_phi = around(fd, (), x + 1)
            near_phi += [jnp.where(even, roll(u, -17), roll(u, 15)), jnp.where(even, roll(u, -15), roll(u, 17))]
            drift = [near_w[d] * (phi - near_phi[d]) for d in range(6)]
            w_total, d_total = add(near_w), add(drift)
            conc = []
            for k in range(PAIRS):
                c, near_c = all_around(se, (k,), k)
                spread_w = add([near_w[d] * near_c[d] for d in range(6)])
                spread_d = add([drift[d] * near_c[d] for d in range(6)])
                outflow = w * ((c * w_total - spread_w) + half_charge[k] * (c * d_total + spread_d))
                conc.append(c)
                done[k][j] = c - rates[k] * outflow
            reaction = conc[2] - conc[0] * conc[1] / solubility
            reaction = jnp.where(w > 0, reactivity * reaction, 0.0)
            for k in range(PAIRS):
                done[k][j] = done[k][j] + signs[k] * reaction
            done[PAIRS][j] = phi
        for k in range(PAIRS + 1):
            native = swap_groups(done[k], lane)
            for f in range(2 if k < PAIRS else 1):
                ion = k + f * PAIRS if k < PAIRS else 2 * PAIRS
                send[ion, at, :] = jnp.where(given == 0, native[f], native[2 + f])
                keep[ion, at, :] = jnp.where(given == 0, native[2 + f], native[f])
        return carry

    lax.fori_loop(0, HALF, update, 0, unroll=2)


def place_kernel(give_slot, *refs):
    keep, received, (new_sp, new_pot) = refs[:2], refs[2:4], refs[4:]
    given = give_slot[0]
    ions = new_sp.shape[0]
    for half in range(2):
        rows = [pl.ds(half * PLANE + slot, PLANE // 2, stride=2) for slot in (given, 1 - given)]
        for i in range(ions):
            new_sp[i, rows[0], :] = received[half][i]
            new_sp[i, rows[1], :] = keep[half][i]
        new_pot[rows[0], :] = received[half][ions]
        new_pot[rows[1], :] = keep[half][ions]


VMEM = pl.BlockSpec(memory_space=pltpu.VMEM)
SMEM = pl.BlockSpec(memory_space=pltpu.SMEM)
ANY = pl.BlockSpec(memory_space=pl.ANY)
HBM = pl.BlockSpec(memory_space=pltpu.HBM)
MIB = 1024 * 1024


def grant(mib):
    return pltpu.CompilerParams(vmem_limit_bytes=mib * MIB)


def f32(*shape):
    return jax.ShapeDtypeStruct(shape, jnp.float32)


def rows_of(field):
    lead = field.shape[:-2]
    bricks, cells = field.shape[-2:]
    split = field.reshape(lead + (bricks, cells // LANES, LANES))
    return jnp.swapaxes(split, -3, -2).reshape(lead + (bricks * cells // LANES, LANES))


def cells_of(rows):
    lead = rows.shape[:-2]
    count, lanes = rows.shape[-2:]
    split = rows.reshape(lead + (count // 2, 2, lanes))
    return jnp.swapaxes(split, -3, -2).reshape(lead + (2, count // 2 * lanes))


def moved(block, axis, offset):
    n = lax.axis_size(axis)
    return lax.ppermute(block, axis, [(i, (i + offset) % n) for i in range(n)])


def local(
    species,
    potential,
    pore,
    openness,
    neighbours,
    diffusivity,
    rate_const,
    opened,
    partner,
    give_slot,
):
    ion_count, brick_count, cells = species.shape
    dev_count = lax.axis_size("dev")
    stride = dev_count // 4

    held = {}
    for sx, sy in SIDES + CORNERS:
        offset = (sx + sy * stride) % dev_count
        offset = offset if offset <= dev_count // 2 else offset - dev_count
        rows, pieces = held.get(offset, (0, ()))
        held[offset] = (rows + (Y_ROWS if 0 in (sx, sy) else EDGE_ROWS), pieces + (((sx, sy), rows),))
    offsets = sorted(held, key=lambda o: (-held[o][0], -abs(o), o))
    pieces = tuple(held[o][1] for o in offsets)

    with_face = [k for k, o in enumerate(offsets) if held[o][0] >= Y_ROWS]
    alone = [k for k in range(len(offsets)) if k not in with_face]
    rows = brick_count * PLANE
    species_rows, pore_rows, openness_rows = rows_of(species), rows_of(pore), rows_of(openness)
    field = pltpu.VMEM((rows, LANES), jnp.float32)
    field_int = pltpu.VMEM((rows, LANES), jnp.int32)
    fields = pltpu.VMEM((ion_count, rows, LANES), jnp.float32)
    pd, own, *blocks, down, up = pl.pallas_call(
        functools.partial(pack_kernel, pieces),
        out_shape=(
            f32(QUADS, PLANE, LANES),
            f32(8, LANES),
            *(f32(held[o][0], LANES) for o in offsets),
            f32(ZC_ROWS, LANES),
            f32(ZC_ROWS, LANES),
        ),
        in_specs=[HBM] * 4 + [SMEM],
        out_specs=tuple([VMEM] * (4 + len(offsets))),
        scratch_shapes=[fields, field, field_int, field, pltpu.SemaphoreType.DMA((PARTS, 3, 4))],
        compiler_params=grant(60),
        name="pack",
    )(species_rows, rows_of(potential), pore_rows, openness_rows, neighbours)
    faces = [k for k, o in enumerate(offsets) if held[o][0] >= Y_ROWS]
    lone = [k for k in range(len(offsets)) if k not in faces]
    rest = faces[-1:] + lone[1:]
    zup = moved(down, "group", -1)
    arrived = {k: moved(blocks[k], "dev", offsets[k]) for k in faces[:-1] + lone[:1]}

    sp, wd = pl.pallas_call(
        ions_kernel,
        out_shape=(f32(PAIRS, QUADS, PLANE, LANES), f32(QUADS, PLANE, LANES)),
        in_specs=[HBM] * 3,
        out_specs=(VMEM,) * 2,
        scratch_shapes=[fields, field_int, field, pltpu.SemaphoreType.DMA((2, 3))],
        compiler_params=grant(60),
        name="ions",
    )(species_rows, pore_rows, openness_rows)

    zup, up, sp, wd, *more = lax.optimization_barrier((zup, up, sp, wd, *(blocks[k] for k in rest)))
    arrived.update((k, moved(block, "dev", offsets[k])) for k, block in zip(rest, more))
    zdn = moved(up, "group", 1)

    zdown, zupper = pl.pallas_call(
        ion_z_kernel,
        out_shape=(f32(ION_ROWS, LANES),) * 2,
        in_specs=[VMEM] * 2,
        out_specs=(VMEM,) * 2,
        compiler_params=grant(8),
        name="ion_z_faces",
    )(sp, wd)

    arrived = [arrived[k] for k in range(len(offsets))]

    zl, zh = pl.pallas_call(
        functools.partial(relay_kernel, pieces),
        out_shape=(f32(ZH_ROWS, LANES),) * 2,
        in_specs=[VMEM] * len(offsets) + [ANY] + [VMEM] * 2,
        out_specs=(VMEM, VMEM),
        compiler_params=grant(6),
        name="relay",
    )(*arrived, zdn, zdown, zupper)
    zhup = moved(zl, "group", -1)
    zhdn = moved(zh, "group", 1)
    wide = pltpu.VMEM((QUADS, EXT * SPAN + 2 * PAD, LANES), jnp.float32)
    by_layer = lambda a: a.reshape(a.shape[:-2] + (SIDE, YQ, LANES))
    sp, wd = by_layer(sp), by_layer(wd)
    scalars = (diffusivity, rate_const, opened, give_slot)
    half_out = (f32(ion_count + 1, PLANE // 2, LANES),) * 2
    half_scratch = [
        pltpu.VMEM((PAIRS, QUADS, HALF + 2, SPAN, LANES), jnp.float32),
        pltpu.VMEM((QUADS, HALF + 2, SPAN, LANES), jnp.float32),
        pltpu.VMEM((FIELDS, QUADS, PLANE // 2, LANES), jnp.float32),
    ]
    sources = (own, pd, zup, zdn, zhup, zhdn, *arrived)
    ud, fd, *first_half = pl.pallas_call(
        functools.partial(sweep_kernel, pieces),
        out_shape=(f32(QUADS, PLANE, LANES), f32(QUADS, NEAR * SPAN, LANES), *half_out),
        in_specs=[HBM] * (len(sources) + 2) + [SMEM] * 4,
        out_specs=(HBM, HBM, VMEM, VMEM),
        scratch_shapes=[
            wide,
            wide,
            wide,
            pltpu.VMEM((2, SPAN, LANES), jnp.float32),
            pltpu.VMEM((3, SPAN, LANES), jnp.float32),
            pltpu.VMEM((3, SPAN, LANES), jnp.float32),
            *half_scratch,
            pltpu.VMEM((QUADS, PLANE, LANES), jnp.float32),
            pltpu.VMEM((QUADS, NEAR * SPAN, LANES), jnp.float32),
            pltpu.SemaphoreType.DMA((len(sources),)),
            pltpu.SemaphoreType.DMA((FIELDS,)),
            pltpu.SemaphoreType.DMA((2,)),
            *(pltpu.VMEM(a.shape, jnp.float32) for a in sources),
        ],
        compiler_params=grant(60),
        name="sweeps",
    )(*sources, sp, wd, *scalars)

    def second_half():
        halos, starts = [], []
        for way in ((1, 0), (-1, 0), (0, 1), (0, -1)):
            for k, parts in enumerate(pieces):
                for name, start in parts:
                    if name == way:
                        halos.append(arrived[k])
                        starts.append(start + Y_ION)
        sources = (own, *halos, zhup, zhdn, ud, fd)
        return pl.pallas_call(
            functools.partial(update_kernel, 1, starts),
            out_shape=half_out,
            in_specs=[HBM] * (len(sources) + 2) + [SMEM] * 4,
            out_specs=(VMEM, VMEM),
            scratch_shapes=[
                *half_scratch,
                pltpu.SemaphoreType.DMA((FIELDS + len(sources),)),
                *(pltpu.VMEM(a.shape, jnp.float32) for a in sources),
            ],
            compiler_params=grant(32),
            name="update",
        )(sp, wd, *sources, *scalars)

    def placed(kept, received):
        new_sp, new_pot = pl.pallas_call(
            place_kernel,
            out_shape=(f32(ion_count, rows, LANES), f32(rows, LANES)),
            in_specs=[SMEM] + [VMEM] * 4,
            out_specs=(VMEM, VMEM),
            compiler_params=grant(8),
            name="place",
        )(give_slot, *kept, *received)
        return cells_of(new_sp), cells_of(new_pot)

    def finished(route):
        across = lambda block: block if route is None else lax.ppermute(block, ("group", "dev"), route)
        keep, send = first_half
        keep_more, send_more = second_half()
        return placed((keep, keep_more), (across(send), across(send_more)))

    total = lax.axis_size("group") * dev_count
    own_index = lax.axis_index("group") * dev_count + lax.axis_index("dev")
    apart = jnp.bitwise_xor(own_index, partner[0])
    branch = jnp.int32(0)
    branches = [lambda: finished(None)]
    for bit in range(total.bit_length() - 1):
        route = [(i, i ^ (1 << bit)) for i in range(total)]
        branch = jnp.where(apart == (1 << bit), bit + 1, branch)
        branches.append(lambda route=route: finished(route))
    return lax.switch(branch, branches)


def solution(mesh):
    in_specs = (
        P(None, ("group", "dev"), None),
        P(("group", "dev"), None),
        P(("group", "dev"), None),
        P(("group", "dev"), None),
        P(("group", "dev"), None),
        P(),
        P(("group", "dev")),
        P(("group", "dev")),
        P(("group", "dev")),
        P(("group", "dev")),
    )
    out_specs = (P(None, ("group", "dev"), None), P(("group", "dev"), None))
    return jax.shard_map(local, mesh=mesh, in_specs=in_specs, out_specs=out_specs, check_vma=False)
```

```python
import functools

import jax
import jax.numpy as jnp
from jax import lax
from jax.experimental import pallas as pl
from jax.experimental.pallas import tpu as pltpu
from jax.sharding import PartitionSpec as P


SWEEPS = 8
DEPTH = SWEEPS + 1
LANES = 128

charge_scale = 0.5
screening = 0.5
solubility = 2.0
valences = (2.0, -1.0, 1.0, -1.0, 1.0, 2.0)
reaction_signs = (1.0, 1.0, -1.0, 0.0, 0.0, 0.0)

SIDE = 32
QUADS = 4
YQ = SIDE // QUADS
PAIRS = 3
PLANE = SIDE * YQ
HALF = SIDE // 2

FACE_TBL = DEPTH * SIDE
Y_ION = FACE_TBL + 8
EDGE_TBL = 64
EDGE_ROWS = EDGE_TBL + 8
THIRD = 11
ZC_TBL = QUADS * THIRD * YQ
ZC_ROWS = ZC_TBL + 8
ZH_EDGE = 2 * 3 * SIDE
ZH_TBL = ZH_EDGE + 64
ZH_ION = ZH_TBL + 32
FIELDS = PAIRS + 1
ION_ROWS = FIELDS * SIDE
Y_ROWS = Y_ION + ION_ROWS
BLOCKS = SIDE // FIELDS
ZH_ROWS = ZH_ION + ION_ROWS

ZH_PLACE = {
    (n, l): (n, off) if l < 5 else (2, 6 * n + off)
    for n in range(2)
    for l, off in enumerate((0, 8, 15, 21, 26, 0, 3, 5))
}

SIDES = ((-1, 0), (1, 0), (0, -1), (0, 1))
CORNERS = ((-1, -1), (-1, 1), (1, -1), (1, 1))
SPAN = 16
EXT = SIDE + 2 * DEPTH
MIDDLE = 30
PARTS = 3
PART = 4
NEAR = SIDE + 2
PAD = 24


def x_way(s):
    return 0 if s > 0 else 1


def y_way(s):
    return 2 if s > 0 else 3


def z_way(s):
    return 4 if s > 0 else 5


def roll(v, shift):
    shift = shift % LANES
    return v if shift == 0 else pltpu.roll(v, shift, 1)


def lane_of(rows):
    return lax.broadcasted_iota(jnp.int32, (rows, LANES), 1)


def swap_groups(v, lane):
    low = lane < 64
    a0 = jnp.where(low, v[0], roll(v[2], 64))
    a2 = jnp.where(low, roll(v[0], 64), v[2])
    a1 = jnp.where(low, v[1], roll(v[3], 64))
    a3 = jnp.where(low, roll(v[1], 64), v[3])
    even = (lane & 32) == 0
    return (
        jnp.where(even, a0, roll(a1, 32)),
        jnp.where(even, roll(a0, 96), a1),
        jnp.where(even, a2, roll(a3, 32)),
        jnp.where(even, roll(a2, 96), a3),
    )


def sign_rows(neighbours):
    row = lax.broadcasted_iota(jnp.int32, (8, LANES), 0)
    table = jnp.zeros((8, LANES), jnp.float32)
    for way in range(6):
        table = jnp.where(row == way, jnp.where(neighbours[0, way] == 0, 1.0, -1.0), table)
    return table


def pack_kernel(pieces, species_in, potential_in, pore_in, openness_in, neighbours, pd, own, *rest):
    n_out = len(pieces)
    outs, (zlo, zhi) = rest[:n_out], rest[n_out : n_out + 2]
    species, potential, pore, openness, sems = rest[n_out + 2 :]
    parts = []
    for part in range(PARTS):
        copies = []
        for c in range(3):
            x0 = c * THIRD + part * PART
            count = min(PART, (c + 1) * THIRD - x0, SIDE - x0)
            rows = pl.ds(x0 * 16, count * 16)
            for number, (src, dst) in enumerate(
                ((species_in, species), (potential_in, potential), (pore_in, pore), (openness_in, openness))
            ):
                at = (slice(None), rows) if number == 0 else (rows,)
                copies.append(pltpu.make_async_copy(src.at[at], dst.at[at], sems.at[part, c, number]))
                copies[-1].start()
        parts.append(copies)
    where = {name: (outs[k], base) for k, held in enumerate(pieces) for name, base in held}
    lane = lane_of(8)
    lane32 = lane & 31
    low = lane < 64
    table = sign_rows(neighbours)
    own[...] = table

    def planes_of(x):
        d, p = [], []
        for b in range(2):
            rows = pl.ds(x * 16 + b, 8, stride=2)
            total = valences[0] * species[0, rows, :]
            for i in range(1, 2 * PAIRS):
                total = total + valences[i] * species[i, rows, :]
            wet = pore[rows, :].astype(jnp.float32) * openness[rows, :]
            d.append(charge_scale * wet * total)
            p.append(potential[rows, :])
        mixed = []
        for v in swap_groups((p[0], d[0], p[1], d[1]), lane):
            r = roll(v, 64)
            mixed.append(jnp.where(low, v + r, r - v))
        at = pl.ds(pl.multiple_of(x * 8, 8), 8)
        for j in range(QUADS):
            pd[j, at, :] = mixed[j]
        return mixed

    def step(i, blocks=3):
        planes = [planes_of(i + c * THIRD) for c in range(blocks)]
        for j in range(QUADS):
            at = pl.ds(pl.multiple_of((j * THIRD + i) * 8, 8), 8)
            lo = hi = planes[0][j]
            for c in range(1, blocks):
                lo = jnp.where(lane32 >= DEPTH * c, roll(planes[c][j], DEPTH * c), lo)
                hi = jnp.where(lane32 < SIDE - DEPTH * c, roll(planes[c][j], -DEPTH * c), hi)
            zlo[at, :] = lo
            zhi[at, :] = hi

    for part in range(PARTS):
        for c in parts[part]:
            c.wait()
        end = min((part + 1) * PART, THIRD - 1)
        lax.fori_loop(part * PART, end, lambda i, carry: (step(i), carry)[1], 0, unroll=True)
    step(THIRD - 1, 2)

    zlo[ZC_TBL:, :] = table
    zhi[ZC_TBL:, :] = table

    def ion_planes(x, ref, start):
        for k, planes in enumerate(dense_ions(species, pore, openness, x, lane)):
            for j in range(QUADS):
                ref[start + k * SIDE + j * 8 : start + k * SIDE + j * 8 + 8, :] = planes[j]

    group = lane_of(SIDE) >> 5

    def ion_rows(y, ref, start):
        for k in range(FIELDS):
            v = jnp.zeros((SIDE, LANES), jnp.float32)
            for b in range(2):
                rows = pl.ds(y // 4 * 2 + b, SIDE, stride=16)
                if k == PAIRS:
                    wet = pore[rows, :].astype(jnp.float32) * openness[rows, :]
                for f in range(2):
                    native = species[k + f * PAIRS, rows, :] if k < PAIRS else wet
                    v = jnp.where(group == 2 * b + f, roll(native, (2 * b + f - y % 4) * SIDE), v)
            ref[start + k * SIDE : start + (k + 1) * SIDE, :] = v

    for sx, sy in SIDES:
        ref, base = where[(sx, sy)]
        for l in range(DEPTH):
            if sx:
                x = l if sx < 0 else SIDE - 1 - l
                for j in range(QUADS):
                    ref[base + l * SIDE + j * 8 : base + l * SIDE + j * 8 + 8, :] = pd[j, x * 8 : x * 8 + 8, :]
            else:
                y = l if sy < 0 else SIDE - 1 - l
                ref[base + l * SIDE : base + (l + 1) * SIDE, :] = pd[y % 4, pl.ds(y // 4, SIDE, stride=8), :]
        ref[base + FACE_TBL : base + Y_ION, :] = table
        if sx:
            ion_planes(0 if sx < 0 else SIDE - 1, ref, base + Y_ION)
        else:
            ion_rows(0 if sy < 0 else SIDE - 1, ref, base + Y_ION)
    for sx, sy in CORNERS:
        ref, base = where[(sx, sy)]
        x0 = 0 if sx < 0 else SIDE - 8
        for m in range(8):
            y = m if sy < 0 else SIDE - 8 + m
            ref[base + m * 8 : base + m * 8 + 8, :] = pd[y % 4, pl.ds(x0 * 8 + y // 4, 8, stride=8), :]
        ref[base + EDGE_TBL : base + EDGE_ROWS, :] = table


def dense_ions(species, pore, openness, x, lane):
    rows = [pl.ds(x * 16 + b, 8, stride=2) for b in range(2)]
    w = [pore[rows[b], :].astype(jnp.float32) * openness[rows[b], :] for b in range(2)]
    s = [[species[n, rows[b], :] for b in range(2)] for n in range(2 * PAIRS)]
    fields = [swap_groups((s[k][0], s[k + PAIRS][0], s[k][1], s[k + PAIRS][1]), lane) for k in range(PAIRS)]
    return fields + [swap_groups((w[0], w[0], w[1], w[1]), lane)]


def ions_kernel(species_in, pore_in, openness_in, sp, wd, species, pore, openness, sems):
    parts = []
    for part in range(2):
        rows = pl.ds(part * PLANE, PLANE)
        copies = [
            pltpu.make_async_copy(species_in.at[:, rows], species.at[:, rows], sems.at[part, 0]),
            pltpu.make_async_copy(pore_in.at[rows], pore.at[rows], sems.at[part, 1]),
            pltpu.make_async_copy(openness_in.at[rows], openness.at[rows], sems.at[part, 2]),
        ]
        for c in copies:
            c.start()
        parts.append(copies)
    lane = lane_of(8)

    def step(x, carry):
        at = pl.ds(pl.multiple_of(x * 8, 8), 8)
        for k, planes in enumerate(dense_ions(species, pore, openness, x, lane)):
            for j in range(QUADS):
                if k < PAIRS:
                    sp[k, j, at, :] = planes[j]
                else:
                    wd[j, at, :] = planes[j]
        return carry

    for part in range(2):
        for c in parts[part]:
            c.wait()
        lax.fori_loop(part * HALF, (part + 1) * HALF, step, 0, unroll=2)


def ion_z_kernel(sp, wd, zlo, zhi):
    lane32 = lane_of(8) & 31

    def step(i, carry):
        for j in range(QUADS):
            lo = hi = jnp.zeros((8, LANES), jnp.float32)
            for spot in range(SIDE):
                block, k = spot // FIELDS, spot % FIELDS
                at = pl.ds(pl.multiple_of((i + block * FIELDS) * 8, 8), 8)
                v = sp[k, j, at, :] if k < PAIRS else wd[j, at, :]
                lo = jnp.where(lane32 == spot, roll(v, spot), lo)
                hi = jnp.where(lane32 == spot, roll(v, spot - 31), hi)
            zat = pl.ds(pl.multiple_of(j * SIDE + i * 8, 8), 8)
            zlo[zat, :] = lo
            zhi[zat, :] = hi
        return carry

    lax.fori_loop(0, FIELDS, step, 0)


def relay_kernel(pieces, *refs):
    arrived, (ions_lo, ions_hi, zl, zh) = refs[:-5], refs[-4:]
    zl[ZH_ION:, :] = ions_lo[...]
    zh[ZH_ION:, :] = ions_hi[...]
    where = {name: (arrived[k], base) for k, held in enumerate(pieces) for name, base in held}
    lane32 = lane_of(SIDE) & 31
    for axis in range(2):
        lo = [jnp.zeros((SIDE, LANES), jnp.float32)] * 3
        hi = [jnp.zeros((SIDE, LANES), jnp.float32)] * 3
        for n in range(2):
            sx, sy = SIDES[2 * axis + n]
            ref, base = where[(-sx, -sy)]
            for l in range(8):
                block, off = ZH_PLACE[n, l]
                width = 8 - l
                v = ref[base + l * SIDE : base + (l + 1) * SIDE, :]
                lo[block] = jnp.where((lane32 >= off) & (lane32 < off + width), roll(v, off), lo[block])
                hi[block] = jnp.where((lane32 <= 31 - off) & (lane32 > 31 - off - width), roll(v, -off), hi[block])
            at = slice(ZH_TBL + (2 * axis + n) * 8, ZH_TBL + (2 * axis + n) * 8 + 8)
            zl[at, :] = ref[base + FACE_TBL : base + Y_ION, :]
            zh[at, :] = ref[base + FACE_TBL : base + Y_ION, :]
        for block in range(3):
            at = slice((axis * 3 + block) * SIDE, (axis * 3 + block + 1) * SIDE)
            zl[at, :] = lo[block]
            zh[at, :] = hi[block]
    group = lane_of(64) & 31
    lo = jnp.zeros((64, LANES), jnp.float32)
    hi = lo
    for number, (sx, sy) in enumerate(CORNERS):
        ref, base = where[(-sx, -sy)]
        v = ref[base : base + EDGE_TBL, :]
        lo = jnp.where((group >= 8 * number) & (group < 8 * number + 8), roll(v, 8 * number), lo)
        hi = jnp.where((group <= 31 - 8 * number) & (group > 23 - 8 * number), roll(v, -8 * number), hi)
    zl[ZH_EDGE : ZH_EDGE + 64, :] = lo
    zh[ZH_EDGE : ZH_EDGE + 64, :] = hi


def sweep_kernel(pieces, *refs):
    n_in = 6 + len(pieces)
    sources, (sp, wd), scalars = refs[:n_in], refs[n_in : n_in + 2], refs[n_in + 2 : n_in + 6]
    ud, fd, keep, send = refs[n_in + 6 : n_in + 10]
    ua, ub, dn, mx, myp, mym, se_cube, we_cube, zw, udv, fdv, sems, ion_sems, out_sems = refs[n_in + 10 : n_in + 24]
    held = refs[n_in + 24 :]
    copies = [pltpu.make_async_copy(src, dst, sems.at[i]) for i, (src, dst) in enumerate(zip(sources, held))]
    for c in copies:
        c.start()
    late = ion_copies(0, sp, wd, se_cube, we_cube, ion_sems)
    for c in late:
        c.start()
    own, pd, zup, zdn, zhup, zhdn = held[:6]
    arrived = held[6:]
    where = {name: (arrived[k], base) for k, held in enumerate(pieces) for name, base in held}

    lane = lane_of(8)
    lane64 = lane & 63
    low = lane < 64
    core = (lane64 >= 16) & (lane64 < 48)
    upper = lane64 >= 48

    for c in copies[:4]:
        c.wait()
    def sign(held, way):
        return jnp.broadcast_to(held[way : way + 1, :], (8, LANES))

    outer = {}

    def outward(key, held):
        m = jnp.where(upper, sign(held, 4), sign(held, 5))
        outer[key] = jnp.where(low, 1.0, m)

    outward((0, 0), own)

    def spread(v, zu, zd, shift_u, shift_d, key):
        rows = v.shape[0]
        tall = lambda a: a if rows == 8 else jnp.concatenate([a] * (rows // 8), axis=0)
        if zu is None:
            return roll(v, 16), roll(v, -16)
        m, c, u = tall(outer[key]), tall(core), tall(upper)
        pot = jnp.where(u, roll(zu, 48 + shift_u), roll(zd, -16 + shift_d)) * m
        rho = jnp.where(u, roll(zu, 16 + shift_u), roll(zd, -48 + shift_d)) * m
        return jnp.where(c, roll(v, 16), pot), jnp.where(c, roll(v, -16), rho)

    def fill(i, c):
        x = i + c * THIRD
        at = pl.ds(pl.multiple_of(x * 8, 8), 8)
        to = pl.ds(pl.multiple_of(PAD + (x + DEPTH) * SPAN + 4, 4), 8)
        for j in range(QUADS):
            zat = pl.ds(pl.multiple_of((j * THIRD + i) * 8, 8), 8)
            pot, rho = spread(pd[j, at, :], zup[zat, :], zdn[zat, :], -DEPTH * c, DEPTH * c, (0, 0))
            ua[j, to, :] = pot
            dn[j, to, :] = rho

    def fill_three(i, carry):
        for c in range(3):
            fill(i, c)
        return carry

    lax.fori_loop(0, THIRD - 1, fill_three, 0, unroll=5)
    fill(THIRD - 1, 0)
    fill(THIRD - 1, 1)

    for c in copies[4:]:
        c.wait()
    table = {(0, 0): own[...]}
    ztable = {1: {(0, 0): zup[ZC_TBL:, :]}, -1: {(0, 0): zdn[ZC_TBL:, :]}}
    for number, (sx, sy) in enumerate(SIDES):
        ref, base = where[(-sx, -sy)]
        table[(sx, sy)] = ref[base + FACE_TBL : base + Y_ION, :]
        for sz, held in ((1, zhup), (-1, zhdn)):
            ztable[sz][(sx, sy)] = held[ZH_TBL + number * 8 : ZH_TBL + number * 8 + 8, :]
    for sx, sy in CORNERS:
        ref, base = where[(-sx, -sy)]
        table[(sx, sy)] = ref[base + EDGE_TBL : base + EDGE_ROWS, :]

    def crossing(way, here, there):
        level = sign(table[here], way)
        beyond = {}
        for sz in (1, -1):
            z = z_way(sz)
            beyond[sz] = sign(ztable[sz][here], way) * sign(table[here], z) * sign(table[there], z)
        m = jnp.where(core, level, jnp.where(upper, beyond[1], beyond[-1]))
        return jnp.where(low, 1.0, m)

    for key, held_table in table.items():
        outward(key, held_table)

    row8 = lax.broadcasted_iota(jnp.int32, (8, LANES), 0)
    one = jnp.ones((8, LANES), jnp.float32)
    for number, sx in enumerate((-1, 1)):
        m = {sy: crossing(x_way(sx), (0, sy), (sx, sy)) for sy in (-1, 0, 1)}
        mx[number, 0:8, :] = jnp.where(row8 < 4, m[-1], m[0])
        mx[number, 8:16, :] = jnp.where(row8 < 4, m[0], m[1])
    y_sign = {}
    for number, sx in enumerate((-1, 0, 1)):
        m = {sy: crossing(y_way(sy), (sx, 0), (sx, sy)) for sy in (-1, 1)}
        y_sign[sx] = m
        myp[number, 0:8, :] = jnp.where(row8 == 3, m[-1], one)
        myp[number, 8:16, :] = jnp.where(row8 == 3, m[1], one)
        mym[number, 0:8, :] = jnp.where(row8 == 4, m[-1], one)
        mym[number, 8:16, :] = jnp.where(row8 == 4, m[1], one)

    for number, (sx, sy) in enumerate(SIDES):
        ref, base = where[(-sx, -sy)]
        for l in range(DEPTH):
            v = ref[base + l * SIDE : base + (l + 1) * SIDE, :]
            zu = zd = None
            off = 0
            if l < 8:
                block, off = ZH_PLACE[number % 2, l]
                block += number // 2 * 3
                at = slice(block * SIDE, (block + 1) * SIDE)
                zu, zd = zhup[at, :], zhdn[at, :]
            pot, rho = spread(v, zu, zd, -off, off, (sx, sy))
            if sx:
                x = SIDE + l if sx > 0 else -1 - l
                start = PAD + (x + DEPTH) * SPAN + 4
                for j in range(QUADS):
                    ua[j, start : start + 8, :] = pot[j * 8 : j * 8 + 8]
                    dn[j, start : start + 8, :] = rho[j * 8 : j * 8 + 8]
            else:
                j = l % 4 if sy > 0 else 3 - l % 4
                row = 12 + l // 4 if sy > 0 else 3 - l // 4
                at = pl.ds(PAD + DEPTH * SPAN + row, SIDE, stride=SPAN)
                ua[j, at, :] = pot
                dn[j, at, :] = rho
    for number, (sx, sy) in enumerate(CORNERS):
        ref, base = where[(-sx, -sy)]
        for m in range(8):
            v = ref[base + m * 8 : base + m * 8 + 8, :]
            at = slice(ZH_EDGE + m * 8, ZH_EDGE + m * 8 + 8)
            pot, rho = spread(v, zhup[at, :], zhdn[at, :], -8 * number, 8 * number, (sx, sy))
            row = (12 if sy > 0 else 2) + m // 4
            x = SIDE if sx > 0 else -8
            to = pl.ds(PAD + (x + DEPTH) * SPAN + row, 8, stride=SPAN)
            ua[m % 4, to, :] = pot
            dn[m % 4, to, :] = rho

    scale = 1.0 / (6.0 + screening)

    def slab(src, dst, x, sx, before=None, after=None):
        r = PAD + (x + DEPTH) * SPAN
        r = r if isinstance(x, int) else pl.multiple_of(r, 8)
        at = pl.ds(r, SPAN)
        c = [src[j, at, :] for j in range(QUADS)]
        for j in range(QUADS):
            left = src[j, pl.ds(r - SPAN, SPAN), :]
            right = src[j, pl.ds(r + SPAN, SPAN), :]
            if before is not None:
                left = left * mx[before]
            if after is not None:
                right = right * mx[after]
            north = c[j + 1] if j < 3 else src[0, pl.ds(r + 1, SPAN), :] * myp[sx + 1]
            south = c[j - 1] if j > 0 else src[3, pl.ds(r - 1, SPAN), :] * mym[sx + 1]
            total = (left + right) + (north + south) + (roll(c[j], 1) + roll(c[j], -1)) + dn[j, at, :]
            dst[j, at, :] = total * scale

    def sweep(src, dst, t):
        def middle(i, carry):
            for n in range(MIDDLE):
                slab(src, dst, 1 + i * MIDDLE + n, 0)
            return carry

        lax.fori_loop(0, (SIDE - 2) // MIDDLE, middle, 0)
        slab(src, dst, -1, -1, after=0)
        slab(src, dst, 0, 0, before=0)
        slab(src, dst, SIDE - 1, 0, after=1)
        slab(src, dst, SIDE, 1, before=1)
        for n in range(DEPTH - t - 1):
            slab(src, dst, -2 - n, -1)
            slab(src, dst, SIDE + 1 + n, 1)

    for t in range(1, SWEEPS + 1):
        sweep(*((ua, ub) if t % 2 else (ub, ua)), t)

    lane16 = lane_of(SPAN)
    first = (lane16 & 32) == 0
    row16 = lax.broadcasted_iota(jnp.int32, (SPAN, LANES), 0)

    def slots(v, m):
        wide_lane = lane_of(v.shape[0])
        c = v * m
        r = roll(c, 64)
        u = 0.5 * jnp.where(wide_lane < 64, c + r, r - c)
        return u, jnp.where((wide_lane & 32) == 0, roll(u, -16), roll(u, 16))

    def rows_at(x):
        return pl.ds(PAD + (x + DEPTH) * SPAN + 4, 8), pl.ds((x + 1) * SPAN + 4, 8)

    for x, number in ((-1, 0), (SIDE, 1)):
        at, near = rows_at(x)
        for j in range(QUADS):
            fdv[j, near, :] = slots(ua[j, at, :], mx[number, 4:12, :])[1]
    for j, row, sy in ((0, 12, 1), (3, 3, -1)):
        v = ua[j, pl.ds(PAD + DEPTH * SPAN + row, SIDE, stride=SPAN), :]
        m = jnp.concatenate([y_sign[0][sy]] * (SIDE // 8), axis=0)
        fdv[j, pl.ds(SPAN + row, SIDE, stride=SPAN), :] = slots(v, m)[1]

    def all_slots(i, carry):
        for n in range(8):
            x = 8 * i + n
            at, near = rows_at(x)
            for j in range(QUADS):
                u, dense = slots(ua[j, at, :], one)
                udv[j, pl.ds(pl.multiple_of(x * 8, 8), 8), :] = u
                fdv[j, near, :] = dense
        return carry

    lax.fori_loop(0, SIDE // 8, all_slots, 0)
    back = [pltpu.make_async_copy(udv, ud, out_sems.at[0]), pltpu.make_async_copy(fdv, fd, out_sems.at[1])]
    for c in back:
        c.start()
    for c in late:
        c.wait()
    halos = [(ref, start + Y_ION) for ref, start in (where[(1, 0)], where[(-1, 0)], where[(0, 1)], where[(0, -1)])]
    update_half(0, se_cube, we_cube, zw, own, *halos, zhup, zhdn, udv, fdv, *scalars, keep, send)
    for c in back:
        c.wait()


def ion_copies(half, sp, wd, se_cube, we_cube, sems):
    first, skip = (0, 1) if half == 0 else (half * HALF - 1, 0)
    at, to = pl.ds(first, HALF + 1), (pl.ds(skip, HALF + 1), pl.ds(4, YQ))
    copies = [pltpu.make_async_copy(sp.at[k, :, at], se_cube.at[(k, slice(None), *to)], sems.at[k]) for k in range(PAIRS)]
    copies.append(pltpu.make_async_copy(wd.at[:, at], we_cube.at[(slice(None), *to)], sems.at[PAIRS]))
    return copies


def update_kernel(half, starts, sp, wd, *refs):
    sources, scalars, outs = refs[:9], refs[9:13], refs[13:15]
    se_cube, we_cube, zw, sems = refs[15:19]
    held = refs[19:]
    copies = ion_copies(half, sp, wd, se_cube, we_cube, sems)
    copies += [pltpu.make_async_copy(src, dst, sems.at[FIELDS + n]) for n, (src, dst) in enumerate(zip(sources, held))]
    for c in copies:
        c.start()
    for c in copies:
        c.wait()
    own, *others = held
    halos = list(zip(others[:4], starts))
    update_half(half, se_cube, we_cube, zw, own, *halos, *others[4:], *scalars, *outs)


def update_half(
    half,
    se_cube,
    we_cube,
    zw,
    own,
    xdn,
    xup,
    ydn,
    yup,
    zup,
    zdn,
    ud,
    fd,
    diffusivity,
    rate_const,
    opened,
    give_slot,
    keep,
    send,
):
    x0 = half * HALF
    layers = HALF + 2
    se = se_cube.reshape(PAIRS, QUADS, layers * SPAN, LANES)
    we = we_cube.reshape(QUADS, layers * SPAN, LANES)

    lane = lane_of(8)
    lane32 = lane & 31
    low = lane < 64
    even = (lane & 32) == 0

    def turned(v, way):
        s = jnp.broadcast_to(own[way : way + 1, :], v.shape)
        return jnp.where(s > 0, v, roll(v, 64))

    def put(k, j, rows, v):
        if k < PAIRS:
            se[k, j, rows, :] = v
        else:
            we[j, rows, :] = v

    for k in range(FIELDS):
        (ref, start), way, layer = (xdn, 1, 0) if half == 0 else (xup, 0, layers - 1)
        v = turned(ref[start + k * SIDE : start + (k + 1) * SIDE, :], way)
        for j in range(QUADS):
            put(k, j, slice(layer * SPAN + 4, layer * SPAN + 12), v[j * 8 : j * 8 + 8])
        for j, row, way, (ref, start) in ((0, 12, 2, yup), (3, 3, 3, ydn)):
            rows = slice(start + k * SIDE + x0, start + k * SIDE + x0 + HALF)
            put(k, j, pl.ds(SPAN + row, HALF, stride=SPAN), turned(ref[rows, :], way))

    odd = (lane & 1) == 1
    for j in range(QUADS):
        for i in range(FIELDS):
            rows = slice(ZH_ION + j * SIDE + i * 8, ZH_ION + j * SIDE + i * 8 + 8)
            zu = turned(zup[rows, :], 4)
            zd = roll(turned(zdn[rows, :], 5), -31)
            both = (jnp.where(odd, zd, zu), jnp.where(odd, zu, zd))
            for c in range(BLOCKS // 2):
                spots = (c + half * (BLOCKS // 2)) * FIELDS
                x = c * FIELDS + i
                for k in range(FIELDS):
                    zw[k, j, x * 8 : x * 8 + 8, :] = roll(both[(spots + k) % 2], 31 - spots - k)

    def by_ion(values, k):
        return jnp.where(even, values[k], values[k + PAIRS])

    half_charge = [by_ion([0.5 * v for v in valences], k) for k in range(PAIRS)]
    rates = [by_ion([diffusivity[i] for i in range(2 * PAIRS)], k) for k in range(PAIRS)]
    signs = [by_ion(reaction_signs, k) for k in range(PAIRS)]
    reactivity = [rate_const[b] * opened[b].astype(jnp.float32) for b in range(2)]
    reactivity = jnp.where(low, reactivity[0], reactivity[1])
    given = give_slot[0]
    top, bottom = lane32 == 31, lane32 == 0
    add = lambda values: functools.reduce(lambda a, b: a + b, values)

    def update(i, carry):
        x = i + x0
        at = pl.ds(pl.multiple_of(i * 8, 8), 8)
        done = [[None] * QUADS for _ in range(PAIRS + 1)]
        for j in range(QUADS):

            def around(ref, lead, layer):
                q = pl.multiple_of(layer * SPAN, 8)
                here = pl.ds(q + 4, 8)
                return (
                    ref[lead + (j, here)],
                    ref[lead + (j, pl.ds(q + 4 + SPAN, 8))],
                    ref[lead + (j, pl.ds(q + 4 - SPAN, 8))],
                    ref[lead + (j + 1, here)] if j < 3 else ref[lead + (0, pl.ds(q + 5, 8))],
                    ref[lead + (j - 1, here)] if j > 0 else ref[lead + (3, pl.ds(q + 3, 8))],
                )

            def all_around(ref, lead, k):
                c, *near = around(ref, lead, i + 1)
                z = zw[k, j, at, :]
                return c, near + [jnp.where(top, z, roll(c, -1)), jnp.where(bottom, z, roll(c, 1))]

            w, near_w = all_around(we, (), PAIRS)
            u = ud[j, pl.ds(pl.multiple_of(x * 8, 8), 8), :]
            phi, *near_phi = around(fd, (), x + 1)
            near_phi += [jnp.where(even, roll(u, -17), roll(u, 15)), jnp.where(even, roll(u, -15), roll(u, 17))]
            drift = [near_w[d] * (phi - near_phi[d]) for d in range(6)]
            w_total, d_total = add(near_w), add(drift)
            conc = []
            for k in range(PAIRS):
                c, near_c = all_around(se, (k,), k)
                spread_w = add([near_w[d] * near_c[d] for d in range(6)])
                spread_d = add([drift[d] * near_c[d] for d in range(6)])
                outflow = w * ((c * w_total - spread_w) + half_charge[k] * (c * d_total + spread_d))
                conc.append(c)
                done[k][j] = c - rates[k] * outflow
            reaction = conc[2] - conc[0] * conc[1] / solubility
            reaction = jnp.where(w > 0, reactivity * reaction, 0.0)
            for k in range(PAIRS):
                done[k][j] = done[k][j] + signs[k] * reaction
            done[PAIRS][j] = phi
        for k in range(PAIRS + 1):
            native = swap_groups(done[k], lane)
            for f in range(2 if k < PAIRS else 1):
                ion = k + f * PAIRS if k < PAIRS else 2 * PAIRS
                send[ion, at, :] = jnp.where(given == 0, native[f], native[2 + f])
                keep[ion, at, :] = jnp.where(given == 0, native[2 + f], native[f])
        return carry

    lax.fori_loop(0, HALF, update, 0, unroll=2)


def place_kernel(give_slot, *refs):
    keep, received, (new_sp, new_pot) = refs[:2], refs[2:4], refs[4:]
    given = give_slot[0]
    ions = new_sp.shape[0]
    for half in range(2):
        rows = [pl.ds(half * PLANE + slot, PLANE // 2, stride=2) for slot in (given, 1 - given)]
        for i in range(ions):
            new_sp[i, rows[0], :] = received[half][i]
            new_sp[i, rows[1], :] = keep[half][i]
        new_pot[rows[0], :] = received[half][ions]
        new_pot[rows[1], :] = keep[half][ions]


VMEM = pl.BlockSpec(memory_space=pltpu.VMEM)
SMEM = pl.BlockSpec(memory_space=pltpu.SMEM)
ANY = pl.BlockSpec(memory_space=pl.ANY)
HBM = pl.BlockSpec(memory_space=pltpu.HBM)
MIB = 1024 * 1024


def grant(mib):
    return pltpu.CompilerParams(vmem_limit_bytes=mib * MIB)


def f32(*shape):
    return jax.ShapeDtypeStruct(shape, jnp.float32)


def rows_of(field):
    lead = field.shape[:-2]
    bricks, cells = field.shape[-2:]
    split = field.reshape(lead + (bricks, cells // LANES, LANES))
    return jnp.swapaxes(split, -3, -2).reshape(lead + (bricks * cells // LANES, LANES))


def cells_of(rows):
    lead = rows.shape[:-2]
    count, lanes = rows.shape[-2:]
    split = rows.reshape(lead + (count // 2, 2, lanes))
    return jnp.swapaxes(split, -3, -2).reshape(lead + (2, count // 2 * lanes))


def moved(block, axis, offset):
    n = lax.axis_size(axis)
    return lax.ppermute(block, axis, [(i, (i + offset) % n) for i in range(n)])


def local(
    species,
    potential,
    pore,
    openness,
    neighbours,
    diffusivity,
    rate_const,
    opened,
    partner,
    give_slot,
):
    ion_count, brick_count, cells = species.shape
    dev_count = lax.axis_size("dev")
    stride = dev_count // 4

    held = {}
    for sx, sy in SIDES + CORNERS:
        offset = (sx + sy * stride) % dev_count
        offset = offset if offset <= dev_count // 2 else offset - dev_count
        rows, pieces = held.get(offset, (0, ()))
        held[offset] = (rows + (Y_ROWS if 0 in (sx, sy) else EDGE_ROWS), pieces + (((sx, sy), rows),))
    offsets = sorted(held, key=lambda o: (-held[o][0], -abs(o), o))
    pieces = tuple(held[o][1] for o in offsets)

    with_face = [k for k, o in enumerate(offsets) if held[o][0] >= Y_ROWS]
    alone = [k for k in range(len(offsets)) if k not in with_face]
    rows = brick_count * PLANE
    species_rows, pore_rows, openness_rows = rows_of(species), rows_of(pore), rows_of(openness)
    field = pltpu.VMEM((rows, LANES), jnp.float32)
    field_int = pltpu.VMEM((rows, LANES), jnp.int32)
    fields = pltpu.VMEM((ion_count, rows, LANES), jnp.float32)
    pd, own, *blocks, down, up = pl.pallas_call(
        functools.partial(pack_kernel, pieces),
        out_shape=(
            f32(QUADS, PLANE, LANES),
            f32(8, LANES),
            *(f32(held[o][0], LANES) for o in offsets),
            f32(ZC_ROWS, LANES),
            f32(ZC_ROWS, LANES),
        ),
        in_specs=[HBM] * 4 + [SMEM],
        out_specs=tuple([VMEM] * (4 + len(offsets))),
        scratch_shapes=[fields, field, field_int, field, pltpu.SemaphoreType.DMA((PARTS, 3, 4))],
        compiler_params=grant(60),
        name="pack",
    )(species_rows, rows_of(potential), pore_rows, openness_rows, neighbours)
    faces = [k for k, o in enumerate(offsets) if held[o][0] >= Y_ROWS]
    lone = [k for k in range(len(offsets)) if k not in faces]
    rest = lone[1:] + faces[-1:]
    zup = moved(down, "group", -1)
    arrived = {k: moved(blocks[k], "dev", offsets[k]) for k in faces[:-1] + lone[:1]}

    sp, wd = pl.pallas_call(
        ions_kernel,
        out_shape=(f32(PAIRS, QUADS, PLANE, LANES), f32(QUADS, PLANE, LANES)),
        in_specs=[HBM] * 3,
        out_specs=(VMEM,) * 2,
        scratch_shapes=[fields, field_int, field, pltpu.SemaphoreType.DMA((2, 3))],
        compiler_params=grant(60),
        name="ions",
    )(species_rows, pore_rows, openness_rows)

    zup, up, sp, wd, *more = lax.optimization_barrier((zup, up, sp, wd, *(blocks[k] for k in rest)))
    arrived.update((k, moved(block, "dev", offsets[k])) for k, block in zip(rest, more))
    zdn = moved(up, "group", 1)

    zdown, zupper = pl.pallas_call(
        ion_z_kernel,
        out_shape=(f32(ION_ROWS, LANES),) * 2,
        in_specs=[VMEM] * 2,
        out_specs=(VMEM,) * 2,
        compiler_params=grant(8),
        name="ion_z_faces",
    )(sp, wd)

    arrived = [arrived[k] for k in range(len(offsets))]

    zl, zh = pl.pallas_call(
        functools.partial(relay_kernel, pieces),
        out_shape=(f32(ZH_ROWS, LANES),) * 2,
        in_specs=[VMEM] * len(offsets) + [ANY] + [VMEM] * 2,
        out_specs=(VMEM, VMEM),
        compiler_params=grant(6),
        name="relay",
    )(*arrived, zdn, zdown, zupper)
    zhup = moved(zl, "group", -1)
    zhdn = moved(zh, "group", 1)
    wide = pltpu.VMEM((QUADS, EXT * SPAN + 2 * PAD, LANES), jnp.float32)
    by_layer = lambda a: a.reshape(a.shape[:-2] + (SIDE, YQ, LANES))
    sp, wd = by_layer(sp), by_layer(wd)
    scalars = (diffusivity, rate_const, opened, give_slot)
    half_out = (f32(ion_count + 1, PLANE // 2, LANES),) * 2
    half_scratch = [
        pltpu.VMEM((PAIRS, QUADS, HALF + 2, SPAN, LANES), jnp.float32),
        pltpu.VMEM((QUADS, HALF + 2, SPAN, LANES), jnp.float32),
        pltpu.VMEM((FIELDS, QUADS, PLANE // 2, LANES), jnp.float32),
    ]
    sources = (own, pd, zup, zdn, zhup, zhdn, *arrived)
    ud, fd, *first_half = pl.pallas_call(
        functools.partial(sweep_kernel, pieces),
        out_shape=(f32(QUADS, PLANE, LANES), f32(QUADS, NEAR * SPAN, LANES), *half_out),
        in_specs=[HBM] * (len(sources) + 2) + [SMEM] * 4,
        out_specs=(HBM, HBM, VMEM, VMEM),
        scratch_shapes=[
            wide,
            wide,
            wide,
            pltpu.VMEM((2, SPAN, LANES), jnp.float32),
            pltpu.VMEM((3, SPAN, LANES), jnp.float32),
            pltpu.VMEM((3, SPAN, LANES), jnp.float32),
            *half_scratch,
            pltpu.VMEM((QUADS, PLANE, LANES), jnp.float32),
            pltpu.VMEM((QUADS, NEAR * SPAN, LANES), jnp.float32),
            pltpu.SemaphoreType.DMA((len(sources),)),
            pltpu.SemaphoreType.DMA((FIELDS,)),
            pltpu.SemaphoreType.DMA((2,)),
            *(pltpu.VMEM(a.shape, jnp.float32) for a in sources),
        ],
        compiler_params=grant(60),
        name="sweeps",
    )(*sources, sp, wd, *scalars)

    def second_half():
        halos, starts = [], []
        for way in ((1, 0), (-1, 0), (0, 1), (0, -1)):
            for k, parts in enumerate(pieces):
                for name, start in parts:
                    if name == way:
                        halos.append(arrived[k])
                        starts.append(start + Y_ION)
        sources = (own, *halos, zhup, zhdn, ud, fd)
        return pl.pallas_call(
            functools.partial(update_kernel, 1, starts),
            out_shape=half_out,
            in_specs=[HBM] * (len(sources) + 2) + [SMEM] * 4,
            out_specs=(VMEM, VMEM),
            scratch_shapes=[
                *half_scratch,
                pltpu.SemaphoreType.DMA((FIELDS + len(sources),)),
                *(pltpu.VMEM(a.shape, jnp.float32) for a in sources),
            ],
            compiler_params=grant(32),
            name="update",
        )(sp, wd, *sources, *scalars)

    def placed(kept, received):
        new_sp, new_pot = pl.pallas_call(
            place_kernel,
            out_shape=(f32(ion_count, rows, LANES), f32(rows, LANES)),
            in_specs=[SMEM] + [VMEM] * 4,
            out_specs=(VMEM, VMEM),
            compiler_params=grant(8),
            name="place",
        )(give_slot, *kept, *received)
        return cells_of(new_sp), cells_of(new_pot)

    def finished(route):
        across = lambda block: block if route is None else lax.ppermute(block, ("group", "dev"), route)
        keep, send = first_half
        keep_more, send_more = second_half()
        return placed((keep, keep_more), (across(send), across(send_more)))

    total = lax.axis_size("group") * dev_count
    own_index = lax.axis_index("group") * dev_count + lax.axis_index("dev")
    apart = jnp.bitwise_xor(own_index, partner[0])
    branch = jnp.int32(0)
    branches = [lambda: finished(None)]
    for bit in range(total.bit_length() - 1):
        route = [(i, i ^ (1 << bit)) for i in range(total)]
        branch = jnp.where(apart == (1 << bit), bit + 1, branch)
        branches.append(lambda route=route: finished(route))
    return lax.switch(branch, branches)


def solution(mesh):
    in_specs = (
        P(None, ("group", "dev"), None),
        P(("group", "dev"), None),
        P(("group", "dev"), None),
        P(("group", "dev"), None),
        P(("group", "dev"), None),
        P(),
        P(("group", "dev")),
        P(("group", "dev")),
        P(("group", "dev")),
        P(("group", "dev")),
    )
    out_specs = (P(None, ("group", "dev"), None), P(("group", "dev"), None))
    return jax.shard_map(local, mesh=mesh, in_specs=in_specs, out_specs=out_specs, check_vma=False)
```
